32 devices in a mesh: wide: 16 (over z, x, core), narrow: 2 (over y).
Axes of the slice: x: 2, y: 2, z: 4, core: 2. Of those that a mesh axis runs over, the one named last changes fastest.
Arguments:
- inputs: bfloat16 [64, 512, 512], P('wide', 'narrow'), may hold values from -12 to 12
- cotangent: bfloat16 [64, 512, 512], P('wide', 'narrow'), may hold values from -6 to 6
- ln1_gain: bfloat16 [512], replicated, may hold values from 0.5 to 1.5
- w_qkv: bfloat16 [512, 1536], replicated, may hold values from -0.25 to 0.25
- w_attn_out: bfloat16 [512, 512], replicated, may hold values from -3.5 to 3.5
- ln2_gain: bfloat16 [512], replicated, may hold values from 0.5 to 1.5
- w_router: bfloat16 [512, 16], replicated, may hold values from -0.1875 to 0.1875
- expert_in: bfloat16 [16, 512, 2048], P('wide'), may hold values from -0.25 to 0.25
- expert_in_bias: bfloat16 [16, 2048], P('wide'), may hold values from -0.59765625 to 0.59765625
- expert_out: bfloat16 [16, 2048, 512], P('wide'), may hold values from -1.75 to 1.75
- expert_out_bias: bfloat16 [16, 512], P('wide'), may hold values from -4.78125 to 4.78125
- route_ids: int32 [64, 512, 2], P('wide', 'narrow'), may hold values from 0 to 15, as said below
- route_slots: int32 [64, 512, 2], P('wide', 'narrow'), may hold values from 0 to 133, as said below
- route_dropped: int32 [64, 512, 2], P('wide', 'narrow'), may hold values from 0 to 1, as said below
Outputs:
- block_out: bfloat16 [64, 512, 512], P('wide', 'narrow')
- input_grad: float32 [64, 512, 512], P('wide', 'narrow')
- grad_ln1_gain: float32 [512], replicated
- grad_qkv: float32 [512, 1536], replicated
- grad_attn_out: float32 [512, 512], replicated
- grad_ln2_gain: float32 [512], replicated
- grad_router: float32 [512, 16], replicated
- grad_expert_in: float32 [16, 512, 2048], P('wide')
- grad_expert_in_bias: float32 [16, 2048], P('wide')
- grad_expert_out: float32 [16, 2048, 512], P('wide')
- grad_expert_out_bias: float32 [16, 512], P('wide')
- stats: float32 [3], replicated
The draws below stay inside these ranges and needn't reach their ends.
Inputs may be any that keep to these rules, and one draw needn't show every extreme that they name: `route_ids`: each token names two different experts. `route_slots`: among the tokens of one device, the kept pairs of one expert take distinct slots, given in priority order with all first choices before all second choices; a dropped pair carries slot 0. In every group of devices along wide with the same index of narrow, one expert has all 134 slots taken from every device. `route_dropped`: 1 exactly for the pairs that come after the 134 kept pairs of their expert among the tokens of one device.
All inputs are finite; a program needn't handle non-finite values.
Results may differ from the reference program's by a relative error of at most 0.014.
Values may be sent and summed in bfloat16 or wider, within the bound.
No kernel may reach another device: no remote copies, remote signals or barrier semaphores. Data moves between devices by JAX's collectives and lax.ppermute only.
A program may use at most 384 MiB of HBM per device.

```python
import math
import jax
import jax.numpy as jnp
from jax import lax

D = 512
HEADS = 8
FF = 2048
TOP = 2
IMG_DEV = 4
ROWS = 256
EXPERTS = 16
SEQ = 512
IMAGES = 64
CAP = 134
N_WIDE = 16
N_NARROW = 2


def routing(key):
    blocks_wide = IMAGES // IMG_DEV
    blocks_narrow = SEQ // ROWS
    per_device = IMG_DEV * ROWS
    key_first, key_skew, key_hot, key_order, key_second, key_label = jax.random.split(key, 6)
    shape = (blocks_wide, blocks_narrow, per_device)
    raw = jax.random.randint(key_first, shape, 0, EXPERTS) * jax.random.randint(key_skew, shape, 1, EXPERTS + 1) // EXPERTS
    labels = jax.random.permutation(key_label, EXPERTS).astype(jnp.int32)
    first = labels[raw]
    order_keys = jax.random.split(key_order, blocks_wide * blocks_narrow)

    def shuffle(device_key):
        return jax.random.permutation(device_key, per_device).astype(jnp.int32)
    orders = jax.vmap(shuffle)(order_keys).reshape(shape)
    ranks = jnp.argsort(orders, axis=-1).astype(jnp.int32)
    hottest = jax.random.randint(key_hot, (blocks_narrow,), 0, EXPERTS)
    first = jnp.where(ranks < CAP + 4, hottest[None, :, None], first).astype(jnp.int32)
    second = ((first + 1 + jax.random.randint(key_second, shape, 0, EXPERTS - 1)) % EXPERTS).astype(jnp.int32)
    in_order = jnp.concatenate([jnp.take_along_axis(first, orders, -1), jnp.take_along_axis(second, orders, -1)], -1)
    selector = (in_order[..., None] == jnp.arange(EXPERTS, dtype=jnp.int32)).astype(jnp.int32)
    before = jnp.cumsum(selector, axis=2) - selector
    placed = jnp.sum(before * selector, -1)
    slot_first = jnp.take_along_axis(placed[..., :per_device], ranks, -1)
    slot_second = jnp.take_along_axis(placed[..., per_device:], ranks, -1)
    choice_ids = jnp.stack([first, second], -1)
    slot_table = jnp.stack([slot_first, slot_second], -1)
    dropped = (slot_table >= CAP).astype(jnp.int32)
    slot_table = jnp.where(dropped == 1, 0, slot_table).astype(jnp.int32)

    def arrange(table):
        table = table.reshape(blocks_wide, blocks_narrow, IMG_DEV, ROWS, TOP)
        return table.transpose(0, 2, 1, 3, 4).reshape(IMAGES, SEQ, TOP)
    return (arrange(choice_ids), arrange(slot_table), arrange(dropped))


def draw_route_ids(key, part):
    return routing(key)[0]


def draw_route_slots(key, part):
    return routing(key)[1]


def draw_route_dropped(key, part):
    return routing(key)[2]


def draw_inputs(key, part):
    key = jax.random.fold_in(key, 7)
    place_image = jnp.arange(IMAGES, dtype=jnp.float32)[:, None, None] / IMAGES
    place_patch = jnp.arange(SEQ, dtype=jnp.float32)[None, :, None] / SEQ
    base = jnp.clip(jax.random.normal(key, (IMAGES, SEQ, D), jnp.float32), -3.5, 3.5)
    scaled = base * 0.35 * 3.0 ** (place_image + place_patch)
    return scaled.astype(jnp.bfloat16)


def block_scale(key, shape, cuts, low, largest):
    def one(dim, parts):
        draws = jax.random.uniform(jax.random.fold_in(jax.random.fold_in(key, 6), dim), (parts,), jnp.float32, low / len(cuts), largest / len(cuts))
        return jnp.repeat(jnp.exp(draws), shape[dim] // parts).reshape((-1,) + (1,) * (len(shape) - dim - 1))

    factor_of = one(*cuts[0])
    for cut in cuts[1:]:
        factor_of = factor_of * one(*cut)
    return factor_of


def normal_values(stream_key, extent, spread, reach, shards=(), kind=jnp.bfloat16):
    level = block_scale(stream_key, extent, shards, -0.22, 0.18) if shards else 1.0
    values = jax.random.normal(stream_key, extent, jnp.float32) * spread * level
    return jnp.minimum(jnp.maximum(values, -reach), reach).astype(kind)


def setup_inputs(seed: int = 0) -> dict:
    arg_keys = jax.random.split(jax.random.key(seed), 15)
    return {
        "inputs": draw_inputs(jax.random.fold_in(arg_keys[14], 71), 0),
        "cotangent": normal_values(arg_keys[1], (IMAGES, SEQ, D), 1.0, 6.0, ((0, 16), (1, 2))),
        "ln1_gain": jnp.clip(1.0 + 0.1 * jax.random.normal(arg_keys[2], (D,), jnp.float32), 0.5, 1.5).astype(jnp.bfloat16),
        "w_qkv": normal_values(arg_keys[3], (D, 3 * D), D ** -0.5, 0.25),
        "w_attn_out": normal_values(arg_keys[4], (D, D), (max(1, 3 * D // SEQ)) ** -0.5, 3.5),
        "ln2_gain": jnp.clip(1.0 + 0.1 * jax.random.normal(arg_keys[5], (D,), jnp.float32), 0.5, 1.5).astype(jnp.bfloat16),
        "w_router": normal_values(arg_keys[6], (D, EXPERTS), (2 * D) ** -0.5, 0.1875),
        "expert_in": normal_values(arg_keys[7], (EXPERTS, D, FF), D ** -0.5, 0.25, ((0, 16),)),
        "expert_in_bias": normal_values(arg_keys[8], (EXPERTS, FF), 0.1, 0.59765625, ((0, 16),)),
        "expert_out": normal_values(arg_keys[9], (EXPERTS, FF, D), (max(1, 3 * FF // (2 * EXPERTS * EXPERTS))) ** -0.5, 1.75, ((0, 16),)),
        "expert_out_bias": normal_values(arg_keys[10], (EXPERTS, D), (0.05 * EXPERTS), 4.78125, ((0, 16),)),
        "route_ids": draw_route_ids(jax.random.fold_in(arg_keys[14], 71), 0),
        "route_slots": draw_route_slots(jax.random.fold_in(arg_keys[14], 71), 0),
        "route_dropped": draw_route_dropped(jax.random.fold_in(arg_keys[14], 71), 0),
    }


EPS = 1e-06

@jax.custom_vjp
def low(v):
    return lax.optimization_barrier(v.astype(jnp.bfloat16)).astype(jnp.float32)

@jax.custom_vjp
def low_back(v):
    return v

def low_keep(v):
    return (low(v), None)

def low_pass(kept, grad):
    return (grad,)

def back_keep(v):
    return (v, None)

def back_low(kept, grad):
    return (low(grad),)
low.defvjp(low_keep, low_pass)
low_back.defvjp(back_keep, back_low)

def matmul(left, right):
    return jnp.dot(left, right, precision=lax.Precision.HIGHEST, preferred_element_type=jnp.float32)

def layer_norm(values, gain):
    centre = lax.optimization_barrier(jnp.mean(values, -1, keepdims=True))
    shifted = values - centre
    return shifted * lax.rsqrt(lax.optimization_barrier(jnp.mean(shifted * shifted, -1, keepdims=True)) + EPS) * gain

def softmax_rows(scores):
    top = lax.optimization_barrier(jnp.max(scores, -1, keepdims=True))
    exponent = jnp.exp(scores - top)
    return exponent / lax.optimization_barrier(jnp.sum(exponent, -1, keepdims=True))

def attend(block):
    head_dim = D // HEADS
    queries = block[:, :, 0]
    keys = block[:, :, 1]
    values = block[:, :, 2]
    scores = jnp.einsum('gqhd,gkhd->ghqk', queries, keys, precision=lax.Precision.HIGHEST) * head_dim ** (-0.5)
    probs = softmax_rows(low_back(scores))
    mixed = jnp.einsum('ghqk,gkhd->gqhd', low(probs), values, precision=lax.Precision.HIGHEST)
    return low(low_back(mixed))

def expert_mlp(operands):
    rows_in, in_weight, in_bias, out_weight, out_bias = operands
    hidden_pre = low_back(matmul(rows_in, in_weight) + in_bias)
    activated = low(jax.nn.gelu(hidden_pre))
    return low(low_back(matmul(activated, out_weight) + out_bias))

def reference(inputs, cotangent, ln1_gain, w_qkv, w_attn_out, ln2_gain, w_router, expert_in, expert_in_bias, expert_out, expert_out_bias, route_ids, route_slots, route_dropped):
    tokens = IMAGES * SEQ
    sources = N_WIDE * N_NARROW
    all_slots = EXPERTS * sources * CAP
    head_dim = D // HEADS
    choice_ids = route_ids.reshape(tokens, TOP)
    dropped = route_dropped.reshape(tokens, TOP)
    kept = (1 - dropped).astype(jnp.float32)
    position = jnp.arange(tokens, dtype=jnp.int32)
    source = position // SEQ // IMG_DEV * N_NARROW + position % SEQ // ROWS
    placed = (choice_ids * sources + source[:, None]) * CAP + route_slots.reshape(tokens, TOP)
    target = jnp.where(dropped == 0, placed, all_slots).reshape(-1)
    fetch = jnp.minimum(target, all_slots - 1)
    selector = (choice_ids[:, :, None] == jnp.arange(EXPERTS, dtype=jnp.int32)).astype(jnp.float32)
    group = math.gcd(IMAGES, max(1, 4096 // SEQ))

    def forward(x_float, gain_one, qkv_weight, attn_weight, gain_two, router_weight, in_weight, in_bias, out_weight, out_bias):
        input_one = low(layer_norm(x_float, gain_one))
        projected = low(low_back(matmul(input_one, qkv_weight)))
        heads_in = projected.reshape(IMAGES // group, group, SEQ, 3, HEADS, head_dim)
        heads_out = lax.map(jax.checkpoint(attend), heads_in).reshape(tokens, D)
        attn_out = low_back(matmul(heads_out, attn_weight))
        residual = x_float + attn_out
        input_two = low(layer_norm(residual, gain_two))
        gate_probs = softmax_rows(low_back(matmul(input_two, router_weight)))
        combine = lax.optimization_barrier(jnp.sum(selector * gate_probs[:, None, :], -1)) * kept
        pair_rows = jnp.broadcast_to(input_two[:, None, :], (tokens, TOP, D)).reshape(tokens * TOP, D)
        dispatch = jnp.zeros((all_slots, D), jnp.float32).at[target].set(pair_rows, mode='drop')
        dispatch = low_back(dispatch).reshape(EXPERTS, sources * CAP, D)
        produced = lax.map(jax.checkpoint(expert_mlp), (dispatch, in_weight, in_bias, out_weight, out_bias))
        picked = produced.reshape(all_slots, D)[fetch].reshape(tokens, TOP, D)
        moe_out = lax.optimization_barrier(jnp.sum(combine[:, :, None] * picked, 1))
        return (residual + moe_out, (residual, attn_out, moe_out))
    primals = (inputs.astype(jnp.float32).reshape(tokens, D), ln1_gain.astype(jnp.float32), w_qkv.astype(jnp.float32), w_attn_out.astype(jnp.float32), ln2_gain.astype(jnp.float32), w_router.astype(jnp.float32), expert_in.astype(jnp.float32), expert_in_bias.astype(jnp.float32), expert_out.astype(jnp.float32), expert_out_bias.astype(jnp.float32))
    result, pull, extras = jax.vjp(forward, *primals, has_aux=True)
    grads = pull(cotangent.astype(jnp.float32).reshape(tokens, D))
    stats = jnp.stack([jnp.sqrt(jnp.mean(member * member) + EPS) for member in extras])
    return (result.astype(jnp.bfloat16).reshape(IMAGES, SEQ, D), grads[0].reshape(IMAGES, SEQ, D), grads[1], grads[2], grads[3], grads[4], grads[5], grads[6], grads[7], grads[8], grads[9], stats)
```

```python
import functools
import math

import jax
import jax.numpy as jnp
from jax import lax
from jax.experimental import pallas as pl
from jax.experimental.pallas import tpu as pltpu
from jax.sharding import PartitionSpec as P

HEADS = 8
TOP = 2


EPS = 1e-06
BF16 = jnp.bfloat16
F32 = jnp.float32
MIB = 1 << 20


def normalize(values):
    centre = jnp.mean(values, -1, keepdims=True)
    shifted = values - centre
    inverse = lax.rsqrt(jnp.mean(shifted * shifted, -1, keepdims=True) + EPS)
    return (shifted * inverse, inverse)


def norm_back(d_normed, normed, inverse):
    return inverse * (
        d_normed
        - jnp.mean(d_normed, -1, keepdims=True)
        - normed * jnp.mean(d_normed * normed, -1, keepdims=True)
    )


def dot(left, right, left_dim=1, right_dim=0):
    return lax.dot_general(
        left, right, (((left_dim,), (right_dim,)), ((), ())), preferred_element_type=F32
    )


def params(mib):
    return pltpu.CompilerParams(vmem_limit_bytes=mib * MIB)


def cost(flops, bytes_accessed, transcendentals=0):
    return pl.CostEstimate(
        flops=int(flops), bytes_accessed=int(bytes_accessed), transcendentals=int(transcendentals)
    )


def whole(shape):
    return pl.BlockSpec(shape, lambda *unused: (0,) * len(shape))


def hits(slots, places):
    first, second = slots
    return jnp.where((places == first) | (places == second), 1.0, 0.0).astype(BF16)


def put_rows(slots_ref, rows_ref, out_ref):
    step = out_ref.shape[0]
    places = lax.broadcasted_iota(jnp.int32, (step, rows_ref.shape[0]), 0) + pl.program_id(0) * step
    out_ref[...] = dot(hits((slots_ref[0:1, :], slots_ref[1:2, :]), places), rows_ref[...]).astype(
        BF16
    )


def dispatch_rows(slot_rows, rows, total, steps=8):
    tokens, width = rows.shape
    step = total // steps
    return pl.pallas_call(
        put_rows,
        grid=(steps,),
        in_specs=[whole(slot_rows.shape), whole(rows.shape)],
        out_specs=pl.BlockSpec((step, width), lambda i: (i, 0)),
        out_shape=jax.ShapeDtypeStruct((total, width), BF16),
        compiler_params=params(32),
        cost_estimate=cost(2 * total * tokens * width, 4 * total * width),
        name="dispatch_rows",
    )(slot_rows, rows)


def attend_kernel(
    flag_ref, own_ref, far_ref, gain_ref, wt_ref, own_out, far_out, proj_ref, total_ref, mixed
):
    del flag_ref
    rows, width = own_ref.shape[1], own_ref.shape[2]
    head_dim = width // HEADS
    scale = head_dim ** (-0.5)
    x_float = jnp.concatenate([own_ref[0], far_ref[0]], 0).astype(F32)
    normed, unused = normalize(x_float)
    normed = (normed * gain_ref[...]).astype(BF16)
    proj_ref[0] = dot(wt_ref[...], normed, 1, 1).astype(BF16)

    def head(h, carry):
        at = pl.multiple_of(h * head_dim, head_dim)
        query = proj_ref[0, pl.ds(at, head_dim), :]
        key = proj_ref[0, pl.ds(at + width, head_dim), :]
        value = proj_ref[0, pl.ds(at + 2 * width, head_dim), :]
        scores = dot(key, query, 0, 0) * scale
        top = jnp.max(scores, 0, keepdims=True)
        exponent = jnp.exp(scores - top)
        total = jnp.sum(exponent, 0, keepdims=True)
        out = dot(value, exponent.astype(BF16)) * (1.0 / total)
        mixed[pl.ds(at, head_dim), :] = out
        total_ref[0, pl.ds(h, 1), :] = top + jnp.log(total)
        return carry

    lax.fori_loop(0, HEADS, head, 0)
    heads_out = mixed[...].T.astype(BF16)
    own_out[0] = heads_out[:rows]
    far_out[0] = heads_out[rows:]


def attend(flag, inputs, far, gain, w_qkv_t):
    part, rows, width = far.shape
    seq_len = 2 * rows
    block = lambda *shape: pl.BlockSpec((1,) + shape, lambda i, flag_ref: (i,) + (0,) * len(shape))
    return pl.pallas_call(
        attend_kernel,
        grid_spec=pltpu.PrefetchScalarGridSpec(
            num_scalar_prefetch=1,
            grid=(part,),
            in_specs=[
                pl.BlockSpec((1, rows, width), lambda i, flag_ref: (i + flag_ref[0] * part, 0, 0)),
                block(rows, width),
                whole(gain.shape),
                whole(w_qkv_t.shape),
            ],
            out_specs=[
                block(rows, width),
                block(rows, width),
                block(3 * width, seq_len),
                block(HEADS, seq_len),
            ],
            scratch_shapes=[pltpu.VMEM((width, seq_len), F32)],
        ),
        out_shape=[
            jax.ShapeDtypeStruct((part, rows, width), BF16),
            jax.ShapeDtypeStruct((part, rows, width), BF16),
            jax.ShapeDtypeStruct((part, 3 * width, seq_len), BF16),
            jax.ShapeDtypeStruct((part, HEADS, seq_len), F32),
        ],
        compiler_params=params(40),
        cost_estimate=cost(part * 8e9, 8 * MIB, part * HEADS * seq_len**2),
        name="attend",
    )(flag, inputs, far, gain, w_qkv_t)


def attend_back_kernel(
    flag_ref,
    own_ref,
    far_ref,
    gain_ref,
    wt_ref,
    proj_ref,
    total_ref,
    d_own_ref,
    d_far_ref,
    own_out,
    far_out,
    weight_out,
    gain_out,
    d_proj,
    d_mixed,
    weight_sum,
):
    del flag_ref
    image, last = pl.program_id(0), pl.num_programs(0) - 1
    rows, width = own_ref.shape[1], own_ref.shape[2]
    head_dim = width // HEADS
    scale = head_dim ** (-0.5)
    d_mixed[...] = jnp.concatenate([d_own_ref[0], d_far_ref[0]], 0).astype(F32).T.astype(BF16)

    def head(h, carry):
        at = pl.multiple_of(h * head_dim, head_dim)
        query = proj_ref[0, pl.ds(at, head_dim), :]
        key = proj_ref[0, pl.ds(at + width, head_dim), :]
        value = proj_ref[0, pl.ds(at + 2 * width, head_dim), :]
        d_out = d_mixed[pl.ds(at, head_dim), :]
        weights = jnp.exp(dot(key, query, 0, 0) * scale - total_ref[0, pl.ds(h, 1), :])
        product = weights * dot(value, d_out, 0, 0)
        spread = jnp.sum(product, 0, keepdims=True)
        d_scores = (product - weights * spread).astype(BF16)
        d_proj[pl.ds(at, head_dim), :] = (dot(key, d_scores) * scale).astype(BF16)
        d_proj[pl.ds(at + width, head_dim), :] = (dot(query, d_scores, 1, 1) * scale).astype(BF16)
        d_proj[pl.ds(at + 2 * width, head_dim), :] = dot(d_out, weights.astype(BF16), 1, 1).astype(
            BF16
        )
        return carry

    lax.fori_loop(0, HEADS, head, 0)
    x_float = jnp.concatenate([own_ref[0], far_ref[0]], 0).astype(F32)
    normed, inverse = normalize(x_float)
    d_input = dot(d_proj[...], wt_ref[...], 0, 0)
    weight_term = dot(d_proj[...], (normed * gain_ref[...]).astype(BF16))
    gain_term = jnp.sum(d_input * normed, 0, keepdims=True)
    d_x = norm_back(d_input * gain_ref[...], normed, inverse).astype(BF16)
    own_out[0] = d_x[:rows]
    far_out[0] = d_x[rows:]

    @pl.when(image == 0)
    def start():
        weight_sum[...] = weight_term
        gain_out[...] = gain_term

    @pl.when(image != 0)
    def add():
        weight_sum[...] += weight_term
        gain_out[...] += gain_term

    @pl.when(image == last)
    def finish():
        weight_out[...] = weight_sum[...].T


def attend_back(flag, inputs, far, gain, w_qkv_t, proj, total, d_heads, d_far):
    part, rows, width = far.shape
    seq_len = 2 * rows
    block = lambda *shape: pl.BlockSpec((1,) + shape, lambda i, flag_ref: (i,) + (0,) * len(shape))
    return pl.pallas_call(
        attend_back_kernel,
        grid_spec=pltpu.PrefetchScalarGridSpec(
            num_scalar_prefetch=1,
            grid=(part,),
            in_specs=[
                pl.BlockSpec((1, rows, width), lambda i, flag_ref: (i + flag_ref[0] * part, 0, 0)),
                block(rows, width),
                whole(gain.shape),
                whole(w_qkv_t.shape),
                block(3 * width, seq_len),
                block(HEADS, seq_len),
                block(rows, width),
                block(rows, width),
            ],
            out_specs=[
                block(rows, width),
                block(rows, width),
                whole((width, 3 * width)),
                whole((1, width)),
            ],
            scratch_shapes=[
                pltpu.VMEM((3 * width, seq_len), BF16),
                pltpu.VMEM((width, seq_len), BF16),
                pltpu.VMEM((3 * width, width), F32),
            ],
        ),
        out_shape=[
            jax.ShapeDtypeStruct((part, rows, width), BF16),
            jax.ShapeDtypeStruct((part, rows, width), BF16),
            jax.ShapeDtypeStruct((width, 3 * width), F32),
            jax.ShapeDtypeStruct((1, width), F32),
        ],
        compiler_params=params(48),
        cost_estimate=cost(part * 16e9, 12 * MIB, part * HEADS * seq_len**2),
        name="attend_back",
    )(flag, inputs, far, gain, w_qkv_t, proj, total, d_heads, d_far)


def residual_kernel(
    flag_ref,
    own_ref,
    far_ref,
    x_ref,
    w_out_ref,
    gain_ref,
    slots_ref,
    heads_out,
    resid_out,
    normed_out,
    rows_out,
    moments_out,
):
    images, rows, width = x_ref.shape
    part = own_ref.shape[0]

    @pl.when(pl.program_id(0) == 0)
    def tokens():
        moments = [jnp.zeros((1, width), F32), jnp.zeros((1, width), F32)]
        for i in range(images):
            mine = (flag_ref[0] == 0) == (i < part)
            heads = jnp.where(mine, own_ref[i % part], far_ref[i % part])
            attn = dot(heads, w_out_ref[...])
            resid = x_ref[i].astype(F32) + attn
            normed, unused = normalize(resid)
            at = pl.ds(i * rows, rows)
            heads_out[at, :] = heads
            resid_out[at, :] = resid
            normed_out[at, :] = (normed * gain_ref[...]).astype(BF16)
            moments[0] += jnp.sum(resid * resid, 0, keepdims=True)
            moments[1] += jnp.sum(attn * attn, 0, keepdims=True)
        moments_out[...] = jnp.concatenate(moments, 0)

    put_rows(slots_ref, normed_out, rows_out)


def residual_rows(flag, own, far, inputs, w_attn_out, gain, slot_rows, total, steps=8):
    images, rows, width = inputs.shape
    tokens = images * rows
    step = total // steps
    return pl.pallas_call(
        residual_kernel,
        grid_spec=pltpu.PrefetchScalarGridSpec(
            num_scalar_prefetch=1,
            grid=(steps,),
            in_specs=[
                whole(own.shape),
                whole(far.shape),
                whole(inputs.shape),
                whole(w_attn_out.shape),
                whole(gain.shape),
                whole(slot_rows.shape),
            ],
            out_specs=[
                whole((tokens, width)),
                whole((tokens, width)),
                whole((tokens, width)),
                pl.BlockSpec((step, width), lambda i, flag_ref: (i, 0)),
                whole((2, width)),
            ],
        ),
        out_shape=[
            jax.ShapeDtypeStruct((tokens, width), BF16),
            jax.ShapeDtypeStruct((tokens, width), F32),
            jax.ShapeDtypeStruct((tokens, width), BF16),
            jax.ShapeDtypeStruct((total, width), BF16),
            jax.ShapeDtypeStruct((2, width), F32),
        ],
        compiler_params=params(40),
        cost_estimate=cost(2 * (total + width) * tokens * width, 10 * MIB),
        name="residual_rows",
    )(flag, own, far, inputs, w_attn_out, gain, slot_rows)


def expert_kernel(
    capacity,
    slots,
    rows_ref,
    up_ref,
    own_ref,
    router_ref,
    w_in_ref,
    b_in_ref,
    w_out_ref,
    b_out_ref,
    y_out,
    back_out,
    act_out,
    d_hidden_out,
    d_y_out,
    b_in_sum,
    b_out_sum,
):
    step, width = rows_ref.shape
    hidden_width = w_in_ref.shape[1]
    chunk = 512
    rows, up = rows_ref[...], up_ref[...]
    logits = dot(rows, router_ref[...])
    gate = jnp.exp(logits - jnp.max(logits, -1, keepdims=True))
    gate = jnp.sum(gate * own_ref[...], -1, keepdims=True) / jnp.sum(gate, -1, keepdims=True)
    up_float = up.astype(F32)
    d_y = (gate * up_float).astype(BF16)
    d_y_out[...] = d_y
    y = jnp.zeros((step, width), F32)
    back = jnp.zeros((step, width), F32)
    first = pl.program_id(0) == 0

    def accumulate(ref, at, value):
        ref[:, at] = jnp.where(first, 0.0, ref[:, at]) + jnp.sum(
            value.astype(F32), 0, keepdims=True
        )

    for c in range(hidden_width // chunk):
        at = slice(c * chunk, (c + 1) * chunk)
        hidden = dot(rows, w_in_ref[:, at]) + b_in_ref[:, at]
        square = hidden * hidden
        root = math.sqrt(2.0 / math.pi)
        slope = jnp.tanh(hidden * (root + (root * 0.044715) * square))
        half = 0.5 * (1.0 + slope)
        act = (hidden * half).astype(BF16)
        d_gelu = half + (0.5 * hidden) * (1.0 - slope * slope) * (
            root + (3.0 * root * 0.044715) * square
        )
        d_hidden = (dot(d_y, w_out_ref[at, :], 1, 1) * d_gelu).astype(BF16)
        act_out[:, at] = act
        d_hidden_out[:, at] = d_hidden
        y += dot(act, w_out_ref[at, :])
        back += dot(d_hidden, w_in_ref[:, at], 1, 1)
        accumulate(b_in_sum, at, d_hidden)
    accumulate(b_out_sum, slice(0, width), d_y)
    y = (y + b_out_ref[...]).astype(BF16).astype(F32)
    d_weight = jnp.sum(y * up_float, -1, keepdims=True)
    y_out[...] = (y * gate).astype(BF16)
    row = lax.broadcasted_iota(jnp.int32, (step, width), 0)
    lane = lax.broadcasted_iota(jnp.int32, (step, width), 1)
    for s in range(step // slots):
        line = jnp.sum(jnp.where(row - s * slots == lane, d_weight, 0.0), 0, keepdims=True)
        line = jnp.where(lane[:1] < capacity, line, 0.0)
        high = line.astype(BF16).astype(F32)
        back = jnp.where(row == s * slots + capacity, high, back)
        back = jnp.where(row == s * slots + capacity + 1, line - high, back)
    back_out[...] = back.astype(BF16)


def expert_rows(
    rows, up, own, w_router, w_in, b_in, w_out, b_out, capacity, slots, steps=8
):
    total, width = rows.shape
    hidden_width = w_in.shape[1]
    step = total // steps
    block = lambda size: pl.BlockSpec((step, size), lambda i: (i, 0))
    return pl.pallas_call(
        functools.partial(expert_kernel, capacity, slots),
        grid=(steps,),
        in_specs=[
            block(width),
            block(width),
            whole(own.shape),
            whole(w_router.shape),
            whole(w_in.shape),
            whole(b_in.shape),
            whole(w_out.shape),
            whole(b_out.shape),
        ],
        out_specs=[
            block(width),
            block(width),
            block(hidden_width),
            block(hidden_width),
            block(width),
            whole((1, hidden_width)),
            whole((1, width)),
        ],
        out_shape=[
            jax.ShapeDtypeStruct((total, width), BF16),
            jax.ShapeDtypeStruct((total, width), BF16),
            jax.ShapeDtypeStruct((total, hidden_width), BF16),
            jax.ShapeDtypeStruct((total, hidden_width), BF16),
            jax.ShapeDtypeStruct((total, width), BF16),
            jax.ShapeDtypeStruct((1, hidden_width), F32),
            jax.ShapeDtypeStruct((1, width), F32),
        ],
        compiler_params=params(48),
        cost_estimate=cost(8 * total * width * hidden_width, 32 * MIB, total * hidden_width),
        name="expert_rows",
    )(rows, up, own, w_router, w_in, b_in, w_out, b_out)


def weight_kernel(left_ref, right_ref, out_ref, turned):
    @pl.when(pl.program_id(0) == 0)
    def turn():
        turned[...] = left_ref[...].T

    out_ref[...] = dot(turned[...], right_ref[...]).astype(BF16)


def weight_grad(left, right, block=512):
    total, width = left.shape
    hidden_width = right.shape[1]
    return pl.pallas_call(
        weight_kernel,
        grid=(hidden_width // block,),
        in_specs=[whole(left.shape), pl.BlockSpec((total, block), lambda i: (0, i))],
        out_specs=pl.BlockSpec((width, block), lambda i: (0, i)),
        out_shape=jax.ShapeDtypeStruct((width, hidden_width), BF16),
        scratch_shapes=[pltpu.VMEM((width, total), BF16)],
        compiler_params=params(40),
        cost_estimate=cost(2 * total * width * hidden_width, 14 * MIB),
        name="weight_grad",
    )(left, right)


def turned_sum_kernel(own_ref, far_ref, out_ref):
    out_ref[...] = (own_ref[...].astype(F32) + far_ref[...].astype(F32)).T


def turned_sum(own, far, block=512):
    width, hidden_width = own.shape
    return pl.pallas_call(
        turned_sum_kernel,
        grid=(hidden_width // block,),
        in_specs=[pl.BlockSpec((width, block), lambda i: (0, i))] * 2,
        out_specs=pl.BlockSpec((block, width), lambda i: (i, 0)),
        out_shape=jax.ShapeDtypeStruct((hidden_width, width), F32),
        compiler_params=params(32),
        cost_estimate=cost(width * hidden_width, 8 * width * hidden_width),
        name="turned_sum",
    )(own, far)


def combine_kernel(slots_ref, y_ref, resid_ref, out_ref, moment_ref):
    step, total = out_ref.shape[0], y_ref.shape[0]
    places = lax.broadcasted_iota(jnp.int32, (step, total), 1)
    moe = dot(hits((slots_ref[:, 0:1], slots_ref[:, 1:2]), places), y_ref[...])
    out_ref[...] = (resid_ref[...] + moe).astype(BF16)
    moment = jnp.sum(moe * moe, 0, keepdims=True)
    moment_ref[...] = jnp.where(pl.program_id(0) == 0, 0.0, moment_ref[...]) + moment


def combine_rows(slot_columns, y, resid, step):
    tokens, width = resid.shape
    total = y.shape[0]
    block = lambda size: pl.BlockSpec((step, size), lambda i: (i, 0))
    return pl.pallas_call(
        combine_kernel,
        grid=(tokens // step,),
        in_specs=[block(TOP), whole(y.shape), block(width)],
        out_specs=[block(width), whole((1, width))],
        out_shape=[
            jax.ShapeDtypeStruct((tokens, width), BF16),
            jax.ShapeDtypeStruct((1, width), F32),
        ],
        compiler_params=params(40),
        cost_estimate=cost(2 * total * tokens * width, 8 * MIB),
        name="combine_rows",
    )(slot_columns, y, resid)


def token_back_kernel(
    capacity,
    slots,
    flag_ref,
    columns_ref,
    lines_ref,
    back_ref,
    resid_ref,
    normed_ref,
    heads_ref,
    up_ref,
    w_out_ref,
    router_ref,
    gain_ref,
    d_resid_out,
    d_heads_out,
    attn_sum,
    router_sum,
    gain_sum,
    d_weights,
):
    del flag_ref
    step, width = resid_ref.shape
    total = back_ref.shape[0]
    experts = router_ref.shape[0]
    first = pl.program_id(0) == 0

    @pl.when(first)
    def columns():
        row = lax.broadcasted_iota(jnp.int32, (slots, 256), 0)
        lane = lax.broadcasted_iota(jnp.int32, (slots, 256), 1)
        for e in range(experts):
            block = back_ref[e * slots : (e + 1) * slots, 0:256].astype(F32)
            line = jnp.sum(jnp.where(row >= capacity, block, 0.0), 0, keepdims=True)
            column = jnp.sum(jnp.where(row == lane, line, 0.0), -1, keepdims=True)
            d_weights[e * slots : (e + 1) * slots, :] = jnp.broadcast_to(column, (slots, step))

    def accumulate(ref, value):
        ref[...] = jnp.where(first, 0.0, ref[...]) + value

    line_slots = (lines_ref[0:1, :], lines_ref[1:2, :])
    d_gates = []
    for e in range(experts):
        places = lax.broadcasted_iota(jnp.int32, (slots, step), 0) + e * slots
        hit = (places == line_slots[0]) | (places == line_slots[1])
        d_gates.append(
            jnp.sum(
                jnp.where(hit, d_weights[e * slots : (e + 1) * slots, :], 0.0), 0, keepdims=True
            )
        )
    d_gates = jnp.concatenate(d_gates, 0)
    logits = dot(router_ref[...], normed_ref[...], 1, 1)
    gates = jnp.exp(logits - jnp.max(logits, 0, keepdims=True))
    gates = gates / jnp.sum(gates, 0, keepdims=True)
    d_logits = (gates * (d_gates - jnp.sum(gates * d_gates, 0, keepdims=True))).astype(BF16)
    places = lax.broadcasted_iota(jnp.int32, (step, total), 1)
    d_normed = dot(hits((columns_ref[:, 0:1], columns_ref[:, 1:2]), places), back_ref[...])
    d_normed += dot(d_logits, router_ref[...], 0, 0)
    normed, inverse = normalize(resid_ref[...])
    d_resid = up_ref[...].astype(F32) + norm_back(d_normed * gain_ref[...], normed, inverse)
    d_attn = d_resid.astype(BF16)
    d_resid_out[...] = d_resid
    d_heads_out[...] = dot(d_attn, w_out_ref[...], 1, 1).astype(BF16)
    accumulate(attn_sum, dot(heads_ref[...], d_attn, 0, 0))
    accumulate(router_sum, dot(d_logits, normed_ref[...]))
    accumulate(gain_sum, jnp.sum(d_normed * normed, 0, keepdims=True))


def token_back(
    flag,
    slot_columns,
    slot_rows,
    back,
    resid,
    normed,
    heads,
    up,
    w_attn_out,
    w_router_t,
    gain,
    capacity,
    slots,
    step,
    part,
):
    tokens, width = resid.shape
    total = back.shape[0]
    experts = w_router_t.shape[0]
    images = tokens // step
    block = lambda size: pl.BlockSpec((step, size), lambda i, flag_ref: (i, 0))
    return pl.pallas_call(
        functools.partial(token_back_kernel, capacity, slots),
        grid_spec=pltpu.PrefetchScalarGridSpec(
            num_scalar_prefetch=1,
            grid=(images,),
            in_specs=[
                block(TOP),
                pl.BlockSpec((TOP, step), lambda i, flag_ref: (0, i)),
                whole(back.shape),
                block(width),
                block(width),
                block(width),
                block(width),
                whole(w_attn_out.shape),
                whole(w_router_t.shape),
                whole(gain.shape),
            ],
            out_specs=[
                block(width),
                pl.BlockSpec(
                    (step, width),
                    lambda i, flag_ref: (lax.rem(i + flag_ref[0] * part, images), 0),
                ),
                whole((width, width)),
                whole((experts, width)),
                whole((1, width)),
            ],
            scratch_shapes=[pltpu.VMEM((total, step), F32)],
        ),
        out_shape=[
            jax.ShapeDtypeStruct((tokens, width), F32),
            jax.ShapeDtypeStruct((tokens, width), BF16),
            jax.ShapeDtypeStruct((width, width), F32),
            jax.ShapeDtypeStruct((experts, width), F32),
            jax.ShapeDtypeStruct((1, width), F32),
        ],
        compiler_params=params(48),
        cost_estimate=cost(2 * (total + 2 * width) * tokens * width, 14 * MIB),
        name="token_back",
    )(
        flag,
        slot_columns,
        slot_rows,
        back,
        resid,
        normed,
        heads,
        up,
        w_attn_out,
        w_router_t,
        gain,
    )


def grad_sum_kernel(flag_ref, resid_ref, own_ref, far_ref, out_ref):
    mine = (flag_ref[0] == 0) == (pl.program_id(0) < pl.num_programs(0) // 2)
    out_ref[...] = resid_ref[...] + jnp.where(mine, own_ref[0], far_ref[0]).astype(F32)


def grad_sum(flag, d_resid, own, far):
    part, rows, width = own.shape
    tokens = d_resid.shape[0]
    pick = pl.BlockSpec((1, rows, width), lambda i, flag_ref: (lax.rem(i, part), 0, 0))
    return pl.pallas_call(
        grad_sum_kernel,
        grid_spec=pltpu.PrefetchScalarGridSpec(
            num_scalar_prefetch=1,
            grid=(tokens // rows,),
            in_specs=[pl.BlockSpec((rows, width), lambda i, flag_ref: (i, 0)), pick, pick],
            out_specs=pl.BlockSpec((rows, width), lambda i, flag_ref: (i, 0)),
        ),
        out_shape=jax.ShapeDtypeStruct((tokens, width), F32),
        compiler_params=params(16),
        cost_estimate=cost(tokens * width, 6 * MIB),
        name="grad_sum",
    )(flag, d_resid, own, far)


def sum_steps():
    steps = []
    for axis in ("wide", "narrow"):
        bit = 1
        while bit < lax.axis_size(axis):
            steps.append((axis, bit))
            bit *= 2
    return steps


def swap(value, axis, bit):
    return lax.ppermute(value, axis, [(i, i ^ bit) for i in range(lax.axis_size(axis))])


def sum_all(value):
    steps = sum_steps()
    for axis, bit in steps:
        half = value.shape[0] // 2
        side = (lax.axis_index(axis) // bit) % 2
        keep = lax.dynamic_slice_in_dim(value, side * half, half, 0)
        send = lax.dynamic_slice_in_dim(value, (1 - side) * half, half, 0).astype(BF16)
        value = keep + swap(send, axis, bit).astype(F32)
    value = value.astype(BF16)
    for axis, bit in reversed(steps):
        side = (lax.axis_index(axis) // bit) % 2
        far = swap(value, axis, bit)
        value = jnp.where(
            side == 0, jnp.concatenate([value, far], 0), jnp.concatenate([far, value], 0)
        )
    return value.astype(F32)


def sum_small(value):
    for axis, bit in sum_steps():
        value = value + swap(value, axis, bit)
    return value


def gathered_attention(inputs, gain_one, w_qkv):
    images, rows_dev, width = inputs.shape
    tokens = images * rows_dev
    head_dim = width // HEADS
    scale = head_dim ** (-0.5)
    seq_len = rows_dev * lax.axis_size("narrow")
    group = math.gcd(images, max(1, 512 // rows_dev))
    blocks = images // group
    normed_one, inverse_one = normalize(inputs.astype(F32).reshape(tokens, width))
    input_one = (normed_one * gain_one).astype(BF16)
    projected = jnp.dot(input_one, w_qkv, preferred_element_type=F32).astype(BF16)
    queries = projected[:, :width].reshape(images, rows_dev, width)
    keys_own = projected[:, width : 2 * width].reshape(images, rows_dev, width)
    values_own = projected[:, 2 * width :].reshape(images, rows_dev, width)
    keys_all = lax.all_gather(keys_own, "narrow", axis=1, tiled=True)
    values_all = lax.all_gather(values_own, "narrow", axis=1, tiled=True)
    query_blocks = queries.reshape(blocks, group, rows_dev, HEADS, head_dim)
    key_blocks = keys_all.reshape(blocks, group, seq_len, HEADS, head_dim)
    value_blocks = values_all.reshape(blocks, group, seq_len, HEADS, head_dim)

    def attend_block(operands):
        query_b, key_b, value_b = operands
        scores = jnp.einsum("gqhd,gkhd->ghqk", query_b, key_b, preferred_element_type=F32) * scale
        top_score = jnp.max(scores, -1, keepdims=True)
        exponent = jnp.exp(scores - top_score)
        total = jnp.sum(exponent, -1, keepdims=True)
        weights = (exponent / total).astype(BF16)
        mixed = jnp.einsum("ghqk,gkhd->gqhd", weights, value_b, preferred_element_type=F32)
        return (mixed.astype(BF16), (top_score + jnp.log(total))[..., 0])

    heads_out, log_total = lax.map(attend_block, (query_blocks, key_blocks, value_blocks))

    def back_block(operands):
        query_b, key_b, value_b, total_b, d_head_b = operands
        scores = jnp.einsum("gqhd,gkhd->ghqk", query_b, key_b, preferred_element_type=F32) * scale
        weights = jnp.exp(scores - total_b[..., None])
        d_weights = jnp.einsum("gqhd,gkhd->ghqk", d_head_b, value_b, preferred_element_type=F32)
        spread = jnp.sum(weights * d_weights, -1, keepdims=True)
        d_scores = (weights * (d_weights - spread)).astype(BF16)
        d_query = jnp.einsum("ghqk,gkhd->gqhd", d_scores, key_b, preferred_element_type=F32) * scale
        d_key = jnp.einsum("ghqk,gqhd->gkhd", d_scores, query_b, preferred_element_type=F32) * scale
        d_value = jnp.einsum(
            "ghqk,gqhd->gkhd", weights.astype(BF16), d_head_b, preferred_element_type=F32
        )
        return (d_query.astype(BF16), d_key, d_value)

    def back(d_heads, d_resid):
        d_head_blocks = d_heads.reshape(blocks, group, rows_dev, HEADS, head_dim)
        d_queries, key_terms, value_terms = lax.map(
            back_block, (query_blocks, key_blocks, value_blocks, log_total, d_head_blocks)
        )
        d_keys, d_values = (
            lax.psum_scatter(
                terms.reshape(images, seq_len, width), "narrow", scatter_dimension=1, tiled=True
            )
            .astype(BF16)
            .reshape(tokens, width)
            for terms in (key_terms, value_terms)
        )
        d_projected = jnp.concatenate([d_queries.reshape(tokens, width), d_keys, d_values], 1)
        d_weight = jnp.dot(input_one.T, d_projected, preferred_element_type=F32)
        d_input = jnp.dot(d_projected, w_qkv.T, preferred_element_type=F32)
        d_gain = jnp.sum(d_input * normed_one, 0, keepdims=True)
        return (
            d_resid + norm_back(d_input * gain_one, normed_one, inverse_one),
            d_weight,
            d_gain,
        )

    return heads_out.reshape(images, rows_dev, width), back


def shards(
    inputs,
    cotangent,
    ln1_gain,
    w_qkv,
    w_attn_out,
    ln2_gain,
    w_router,
    expert_in,
    expert_in_bias,
    expert_out,
    expert_out_bias,
    route_ids,
    route_slots,
    route_dropped,
):
    images, rows_dev, width = inputs.shape
    tokens = images * rows_dev
    experts = w_router.shape[1]
    n_wide = lax.axis_size("wide")
    n_narrow = lax.axis_size("narrow")
    capacity = max(2, 42 * tokens // (20 * experts))
    slots = -(-(capacity + 2) // 8) * 8
    total = experts * slots
    gain_one = ln1_gain.astype(F32).reshape(1, width)
    gain_two = ln2_gain.astype(F32).reshape(1, width)
    paired = n_narrow == 2 and images % 2 == 0
    part = images // 2
    place = lax.axis_index("narrow") if paired else jnp.int32(0)
    flag = place.reshape(1)

    if paired:
        far_inputs = swap(
            lax.dynamic_slice_in_dim(inputs, (1 - place) * part, part, 0), "narrow", 1
        )

    slot_columns = jnp.where(
        route_dropped == 0, route_ids * slots + route_slots, -1
    ).reshape(tokens, TOP)
    slot_rows = slot_columns.T
    up = cotangent.reshape(tokens, width)

    def exchange(rows):
        return lax.all_to_all(
            rows.reshape(experts, slots, width), "wide", split_axis=0, concat_axis=0, tiled=True
        ).reshape(total, width)

    up_here = exchange(dispatch_rows(slot_rows, up, total))

    if paired:
        w_qkv_t = w_qkv.T
        heads_own, heads_far, proj, log_total = attend(
            flag, inputs, far_inputs, gain_one, w_qkv_t
        )
        heads_far = swap(heads_far, "narrow", 1)
    else:
        heads_own, attention_back = gathered_attention(inputs, gain_one, w_qkv)
        heads_own, heads_far = heads_own[:part], heads_own[part:]

    heads, resid, normed_two, rows, moments = residual_rows(
        flag, heads_own, heads_far, inputs, w_attn_out, gain_two, slot_rows, total
    )
    rows_here = exchange(rows)
    own = (jnp.arange(experts) == lax.axis_index("wide")).astype(F32).reshape(1, experts)
    w_in, w_out = expert_in[0], expert_out[0]
    y, back, act, d_hidden, d_y, b_in_sum, b_out_sum = expert_rows(
        rows_here,
        up_here,
        own,
        w_router,
        w_in,
        expert_in_bias.astype(F32),
        w_out,
        expert_out_bias.astype(F32),
        capacity,
        slots,
    )
    back = exchange(back)
    y = exchange(y)
    grad_out_t = weight_grad(d_y, act)
    grad_in = weight_grad(rows_here, d_hidden)
    biases = jnp.concatenate([b_in_sum, b_out_sum], 1)
    if n_narrow == 2:
        grad_expert_out = turned_sum(grad_out_t, swap(grad_out_t, "narrow", 1))
        grad_expert_in = grad_in.astype(F32) + swap(grad_in, "narrow", 1).astype(F32)
        biases = biases + swap(biases, "narrow", 1)
    else:
        grad_out_t, grad_in = lax.psum((grad_out_t, grad_in), "narrow")
        grad_expert_out = grad_out_t.astype(F32).T
        grad_expert_in = grad_in.astype(F32)
        biases = lax.psum(biases, "narrow")

    d_resid, d_heads, attn_term, router_term, gain_two_term = token_back(
        flag,
        slot_columns,
        slot_rows,
        back,
        resid,
        normed_two,
        heads,
        up,
        w_attn_out,
        w_router.T,
        gain_two,
        capacity,
        slots,
        rows_dev,
        part,
    )
    d_heads = d_heads.reshape(images, rows_dev, width)
    if paired:
        d_far = swap(d_heads[part:], "narrow", 1)
        d_own, d_far, qkv_term, gain_one_term = attend_back(
            flag, inputs, far_inputs, gain_one, w_qkv_t, proj, log_total, d_heads, d_far
        )
        input_grad = grad_sum(flag, d_resid, d_own, swap(d_far, "narrow", 1))
    else:
        input_grad, qkv_term, gain_one_term = attention_back(d_heads, d_resid)

    block_out, moe_moment = combine_rows(slot_columns, y, resid, rows_dev)
    small = jnp.concatenate([router_term, gain_one_term, gain_two_term, moments, moe_moment], 0)
    small = sum_small(small)
    grad_attn_out = sum_all(attn_term)
    grad_qkv = sum_all(qkv_term)
    moment_count = tokens * width * n_wide * n_narrow
    stats = jnp.sqrt(jnp.sum(small[experts + 2 : experts + 5], 1) / moment_count + EPS)
    return (
        block_out.reshape(images, rows_dev, width),
        input_grad.reshape(images, rows_dev, width),
        small[experts],
        grad_qkv,
        grad_attn_out,
        small[experts + 1],
        small[:experts].T,
        grad_expert_in[None],
        biases[:, : w_in.shape[1]],
        grad_expert_out[None],
        biases[:, w_in.shape[1] :],
        stats,
    )


def solution(mesh):
    return jax.shard_map(
        shards,
        mesh=mesh,
        in_specs=(
            P("wide", "narrow", None),
            P("wide", "narrow", None),
            P(),
            P(),
            P(),
            P(),
            P(),
            P("wide", None, None),
            P("wide", None),
            P("wide", None, None),
            P("wide", None),
            P("wide", "narrow", None),
            P("wide", "narrow", None),
            P("wide", "narrow", None),
        ),
        out_specs=(
            P("wide", "narrow", None),
            P("wide", "narrow", None),
            P(),
            P(),
            P(),
            P(),
            P(),
            P("wide", None, None),
            P("wide", None),
            P("wide", None, None),
            P("wide", None),
            P(),
        ),
        check_vma=False,
    )
```

```python
import functools
import math

import jax
import jax.numpy as jnp
from jax import lax
from jax.experimental import pallas as pl
from jax.experimental.pallas import tpu as pltpu
from jax.sharding import PartitionSpec as P

HEADS = 8
TOP = 2


EPS = 1e-06
BF16 = jnp.bfloat16
F32 = jnp.float32
MIB = 1 << 20
SMALL = 128


def normalize(values):
    centre = jnp.mean(values, -1, keepdims=True)
    shifted = values - centre
    inverse = lax.rsqrt(jnp.mean(shifted * shifted, -1, keepdims=True) + EPS)
    return (shifted * inverse, inverse)


def norm_back(d_normed, normed, inverse):
    return inverse * (
        d_normed
        - jnp.mean(d_normed, -1, keepdims=True)
        - normed * jnp.mean(d_normed * normed, -1, keepdims=True)
    )


def dot(left, right, left_dim=1, right_dim=0):
    return lax.dot_general(
        left, right, (((left_dim,), (right_dim,)), ((), ())), preferred_element_type=F32
    )


def params(mib):
    return pltpu.CompilerParams(vmem_limit_bytes=mib * MIB)


def cost(flops, bytes_accessed, transcendentals=0):
    return pl.CostEstimate(
        flops=int(flops), bytes_accessed=int(bytes_accessed), transcendentals=int(transcendentals)
    )


def whole(shape):
    return pl.BlockSpec(shape, lambda *unused: (0,) * len(shape))


def hits(slots, places):
    first, second = slots
    return jnp.where((places == first) | (places == second), 1.0, 0.0).astype(BF16)


def put_rows(slots_ref, rows_ref, out_ref):
    step = out_ref.shape[0]
    places = lax.broadcasted_iota(jnp.int32, (step, rows_ref.shape[0]), 0) + pl.program_id(0) * step
    out_ref[...] = dot(hits((slots_ref[0:1, :], slots_ref[1:2, :]), places), rows_ref[...]).astype(
        BF16
    )


def dispatch_rows(slot_rows, rows, total, steps=8):
    tokens, width = rows.shape
    step = total // steps
    return pl.pallas_call(
        put_rows,
        grid=(steps,),
        in_specs=[whole(slot_rows.shape), whole(rows.shape)],
        out_specs=pl.BlockSpec((step, width), lambda i: (i, 0)),
        out_shape=jax.ShapeDtypeStruct((total, width), BF16),
        compiler_params=params(32),
        cost_estimate=cost(2 * total * tokens * width, 4 * total * width),
        name="dispatch_rows",
    )(slot_rows, rows)


def attend_kernel(
    flag_ref, own_ref, far_ref, gain_ref, wt_ref, own_out, far_out, proj_ref, total_ref, mixed
):
    del flag_ref
    rows, width = own_ref.shape[1], own_ref.shape[2]
    head_dim = width // HEADS
    scale = head_dim ** (-0.5)
    x_float = jnp.concatenate([own_ref[0], far_ref[0]], 0).astype(F32)
    normed, unused = normalize(x_float)
    normed = (normed * gain_ref[...]).astype(BF16)
    proj_ref[0] = dot(wt_ref[...], normed, 1, 1).astype(BF16)

    def head(h, carry):
        at = pl.multiple_of(h * head_dim, head_dim)
        query = proj_ref[0, pl.ds(at, head_dim), :]
        key = proj_ref[0, pl.ds(at + width, head_dim), :]
        value = proj_ref[0, pl.ds(at + 2 * width, head_dim), :]
        scores = dot(key, query, 0, 0) * scale
        top = jnp.max(scores, 0, keepdims=True)
        exponent = jnp.exp(scores - top)
        total = jnp.sum(exponent, 0, keepdims=True)
        out = dot(value, exponent.astype(BF16)) * (1.0 / total)
        mixed[pl.ds(at, head_dim), :] = out
        total_ref[0, pl.ds(h, 1), :] = top + jnp.log(total)
        return carry

    lax.fori_loop(0, HEADS, head, 0)
    heads_out = mixed[...].T.astype(BF16)
    own_out[0] = heads_out[:rows]
    far_out[0] = heads_out[rows:]


def attend(flag, inputs, far, gain, w_qkv_t):
    part, rows, width = far.shape
    seq_len = 2 * rows
    block = lambda *shape: pl.BlockSpec((1,) + shape, lambda i, flag_ref: (i,) + (0,) * len(shape))
    return pl.pallas_call(
        attend_kernel,
        grid_spec=pltpu.PrefetchScalarGridSpec(
            num_scalar_prefetch=1,
            grid=(part,),
            in_specs=[
                pl.BlockSpec((1, rows, width), lambda i, flag_ref: (i + flag_ref[0] * part, 0, 0)),
                block(rows, width),
                whole(gain.shape),
                whole(w_qkv_t.shape),
            ],
            out_specs=[
                block(rows, width),
                block(rows, width),
                block(3 * width, seq_len),
                block(HEADS, seq_len),
            ],
            scratch_shapes=[pltpu.VMEM((width, seq_len), F32)],
        ),
        out_shape=[
            jax.ShapeDtypeStruct((part, rows, width), BF16),
            jax.ShapeDtypeStruct((part, rows, width), BF16),
            jax.ShapeDtypeStruct((part, 3 * width, seq_len), BF16),
            jax.ShapeDtypeStruct((part, HEADS, seq_len), F32),
        ],
        compiler_params=params(40),
        cost_estimate=cost(part * 8e9, 8 * MIB, part * HEADS * seq_len**2),
        name="attend",
    )(flag, inputs, far, gain, w_qkv_t)


def small_columns(small, gain):
    rest = jnp.zeros((SMALL - small.shape[0] - 1, small.shape[1]), F32)
    return jnp.concatenate([small, gain, rest], 0).T


def attend_back_kernel(
    flag_ref,
    own_ref,
    far_ref,
    gain_ref,
    wt_ref,
    proj_ref,
    total_ref,
    d_own_ref,
    d_far_ref,
    attn_ref,
    small_ref,
    own_out,
    far_out,
    keep_out,
    send_out,
    d_proj,
    d_mixed,
    weight_sum,
    gain_out,
):
    image, last = pl.program_id(0), pl.num_programs(0) - 1
    rows, width = own_ref.shape[1], own_ref.shape[2]
    head_dim = width // HEADS
    scale = head_dim ** (-0.5)
    d_mixed[...] = jnp.concatenate([d_own_ref[0], d_far_ref[0]], 0).astype(F32).T.astype(BF16)

    def head(h, carry):
        at = pl.multiple_of(h * head_dim, head_dim)
        query = proj_ref[0, pl.ds(at, head_dim), :]
        key = proj_ref[0, pl.ds(at + width, head_dim), :]
        value = proj_ref[0, pl.ds(at + 2 * width, head_dim), :]
        d_out = d_mixed[pl.ds(at, head_dim), :]
        weights = jnp.exp(dot(key, query, 0, 0) * scale - total_ref[0, pl.ds(h, 1), :])
        product = weights * dot(value, d_out, 0, 0)
        spread = jnp.sum(product, 0, keepdims=True)
        d_scores = (product - weights * spread).astype(BF16)
        d_proj[pl.ds(at, head_dim), :] = (dot(key, d_scores) * scale).astype(BF16)
        d_proj[pl.ds(at + width, head_dim), :] = (dot(query, d_scores, 1, 1) * scale).astype(BF16)
        d_proj[pl.ds(at + 2 * width, head_dim), :] = dot(d_out, weights.astype(BF16), 1, 1).astype(
            BF16
        )
        return carry

    lax.fori_loop(0, HEADS, head, 0)
    x_float = jnp.concatenate([own_ref[0], far_ref[0]], 0).astype(F32)
    normed, inverse = normalize(x_float)
    d_input = dot(d_proj[...], wt_ref[...], 0, 0)
    weight_term = dot(d_proj[...], (normed * gain_ref[...]).astype(BF16))
    gain_term = jnp.sum(d_input * normed, 0, keepdims=True)
    d_x = norm_back(d_input * gain_ref[...], normed, inverse).astype(BF16)
    own_out[0] = d_x[:rows]
    far_out[0] = d_x[rows:]

    @pl.when(image == 0)
    def start():
        weight_sum[...] = weight_term
        gain_out[...] = gain_term

    @pl.when(image != 0)
    def add():
        weight_sum[...] += weight_term
        gain_out[...] += gain_term

    @pl.when(image == last)
    def finish():
        half = width // 2
        parts = ((weight_sum[...].T, 0), (attn_ref[...], 3 * width))
        parts += ((small_columns(small_ref[...], gain_out[...]), 4 * width),)
        upper = flag_ref[1] == 1
        for value, at in parts:
            at = slice(at, at + value.shape[1])
            keep_out[:, at] = jnp.where(upper, value[half:], value[:half])
            send_out[:, at] = jnp.where(upper, value[:half], value[half:]).astype(BF16)


def attend_back(flag, inputs, far, gain, w_qkv_t, proj, total, d_heads, d_far, attn_term, small):
    part, rows, width = far.shape
    seq_len = 2 * rows
    block = lambda *shape: pl.BlockSpec((1,) + shape, lambda i, flag_ref: (i,) + (0,) * len(shape))
    return pl.pallas_call(
        attend_back_kernel,
        grid_spec=pltpu.PrefetchScalarGridSpec(
            num_scalar_prefetch=1,
            grid=(part,),
            in_specs=[
                pl.BlockSpec((1, rows, width), lambda i, flag_ref: (i + flag_ref[0] * part, 0, 0)),
                block(rows, width),
                whole(gain.shape),
                whole(w_qkv_t.shape),
                block(3 * width, seq_len),
                block(HEADS, seq_len),
                block(rows, width),
                block(rows, width),
                whole(attn_term.shape),
                whole(small.shape),
            ],
            out_specs=[
                block(rows, width),
                block(rows, width),
                whole((width // 2, 4 * width + SMALL)),
                whole((width // 2, 4 * width + SMALL)),
            ],
            scratch_shapes=[
                pltpu.VMEM((3 * width, seq_len), BF16),
                pltpu.VMEM((width, seq_len), BF16),
                pltpu.VMEM((3 * width, width), F32),
                pltpu.VMEM((1, width), F32),
            ],
        ),
        out_shape=[
            jax.ShapeDtypeStruct((part, rows, width), BF16),
            jax.ShapeDtypeStruct((part, rows, width), BF16),
            jax.ShapeDtypeStruct((width // 2, 4 * width + SMALL), F32),
            jax.ShapeDtypeStruct((width // 2, 4 * width + SMALL), BF16),
        ],
        compiler_params=params(60),
        cost_estimate=cost(part * 16e9, 12 * MIB, part * HEADS * seq_len**2),
        name="attend_back",
    )(flag, inputs, far, gain, w_qkv_t, proj, total, d_heads, d_far, attn_term, small)


def residual_kernel(
    flag_ref,
    own_ref,
    far_ref,
    x_ref,
    w_out_ref,
    gain_ref,
    slots_ref,
    heads_out,
    resid_out,
    normed_out,
    rows_out,
    moments_out,
):
    images, rows, width = x_ref.shape
    part = own_ref.shape[0]

    @pl.when(pl.program_id(0) == 0)
    def tokens():
        moments = [jnp.zeros((1, width), F32), jnp.zeros((1, width), F32)]
        for i in range(images):
            mine = (flag_ref[0] == 0) == (i < part)
            heads = jnp.where(mine, own_ref[i % part], far_ref[i % part])
            attn = dot(heads, w_out_ref[...])
            resid = x_ref[i].astype(F32) + attn
            normed, unused = normalize(resid)
            at = pl.ds(i * rows, rows)
            heads_out[at, :] = heads
            resid_out[at, :] = resid
            normed_out[at, :] = (normed * gain_ref[...]).astype(BF16)
            moments[0] += jnp.sum(resid * resid, 0, keepdims=True)
            moments[1] += jnp.sum(attn * attn, 0, keepdims=True)
        moments_out[...] = jnp.concatenate(moments, 0)

    put_rows(slots_ref, normed_out, rows_out)


def residual_rows(flag, own, far, inputs, w_attn_out, gain, slot_rows, total, steps=8):
    images, rows, width = inputs.shape
    tokens = images * rows
    step = total // steps
    return pl.pallas_call(
        residual_kernel,
        grid_spec=pltpu.PrefetchScalarGridSpec(
            num_scalar_prefetch=1,
            grid=(steps,),
            in_specs=[
                whole(own.shape),
                whole(far.shape),
                whole(inputs.shape),
                whole(w_attn_out.shape),
                whole(gain.shape),
                whole(slot_rows.shape),
            ],
            out_specs=[
                whole((tokens, width)),
                whole((tokens, width)),
                whole((tokens, width)),
                pl.BlockSpec((step, width), lambda i, flag_ref: (i, 0)),
                whole((2, width)),
            ],
        ),
        out_shape=[
            jax.ShapeDtypeStruct((tokens, width), BF16),
            jax.ShapeDtypeStruct((tokens, width), F32),
            jax.ShapeDtypeStruct((tokens, width), BF16),
            jax.ShapeDtypeStruct((total, width), BF16),
            jax.ShapeDtypeStruct((2, width), F32),
        ],
        compiler_params=params(40),
        cost_estimate=cost(2 * (total + width) * tokens * width, 10 * MIB),
        name="residual_rows",
    )(flag, own, far, inputs, w_attn_out, gain, slot_rows)


def expert_kernel(
    capacity,
    slots,
    rows_ref,
    up_ref,
    own_ref,
    router_ref,
    w_in_ref,
    b_in_ref,
    w_out_ref,
    b_out_ref,
    y_out,
    back_out,
    act_out,
    d_hidden_out,
    d_y_out,
    b_in_sum,
    b_out_sum,
):
    step, width = rows_ref.shape
    hidden_width = w_in_ref.shape[1]
    chunk = 512
    rows, up = rows_ref[...], up_ref[...]
    logits = dot(rows, router_ref[...])
    gate = jnp.exp(logits - jnp.max(logits, -1, keepdims=True))
    gate = jnp.sum(gate * own_ref[...], -1, keepdims=True) / jnp.sum(gate, -1, keepdims=True)
    up_float = up.astype(F32)
    d_y = (gate * up_float).astype(BF16)
    d_y_out[...] = d_y
    y = jnp.zeros((step, width), F32)
    back = jnp.zeros((step, width), F32)
    first = pl.program_id(0) == 0

    def accumulate(ref, at, value):
        ref[:, at] = jnp.where(first, 0.0, ref[:, at]) + jnp.sum(
            value.astype(F32), 0, keepdims=True
        )

    for c in range(hidden_width // chunk):
        at = slice(c * chunk, (c + 1) * chunk)
        hidden = dot(rows, w_in_ref[:, at]) + b_in_ref[:, at]
        square = hidden * hidden
        root = math.sqrt(2.0 / math.pi)
        slope = jnp.tanh(hidden * (root + (root * 0.044715) * square))
        half = 0.5 * (1.0 + slope)
        act = (hidden * half).astype(BF16)
        d_gelu = half + (0.5 * hidden) * (1.0 - slope * slope) * (
            root + (3.0 * root * 0.044715) * square
        )
        d_hidden = (dot(d_y, w_out_ref[at, :], 1, 1) * d_gelu).astype(BF16)
        act_out[:, at] = act
        d_hidden_out[:, at] = d_hidden
        y += dot(act, w_out_ref[at, :])
        back += dot(d_hidden, w_in_ref[:, at], 1, 1)
        accumulate(b_in_sum, at, d_hidden)
    accumulate(b_out_sum, slice(0, width), d_y)
    y = (y + b_out_ref[...]).astype(BF16).astype(F32)
    d_weight = jnp.sum(y * up_float, -1, keepdims=True)
    y_out[...] = (y * gate).astype(BF16)
    row = lax.broadcasted_iota(jnp.int32, (step, width), 0)
    lane = lax.broadcasted_iota(jnp.int32, (step, width), 1)
    for s in range(step // slots):
        line = jnp.sum(jnp.where(row - s * slots == lane, d_weight, 0.0), 0, keepdims=True)
        line = jnp.where(lane[:1] < capacity, line, 0.0)
        high = line.astype(BF16).astype(F32)
        back = jnp.where(row == s * slots + capacity, high, back)
        back = jnp.where(row == s * slots + capacity + 1, line - high, back)
    back_out[...] = back.astype(BF16)


def expert_rows(
    rows, up, own, w_router, w_in, b_in, w_out, b_out, capacity, slots, steps=8
):
    total, width = rows.shape
    hidden_width = w_in.shape[1]
    step = total // steps
    block = lambda size: pl.BlockSpec((step, size), lambda i: (i, 0))
    return pl.pallas_call(
        functools.partial(expert_kernel, capacity, slots),
        grid=(steps,),
        in_specs=[
            block(width),
            block(width),
            whole(own.shape),
            whole(w_router.shape),
            whole(w_in.shape),
            whole(b_in.shape),
            whole(w_out.shape),
            whole(b_out.shape),
        ],
        out_specs=[
            block(width),
            block(width),
            block(hidden_width),
            block(hidden_width),
            block(width),
            whole((1, hidden_width)),
            whole((1, width)),
        ],
        out_shape=[
            jax.ShapeDtypeStruct((total, width), BF16),
            jax.ShapeDtypeStruct((total, width), BF16),
            jax.ShapeDtypeStruct((total, hidden_width), BF16),
            jax.ShapeDtypeStruct((total, hidden_width), BF16),
            jax.ShapeDtypeStruct((total, width), BF16),
            jax.ShapeDtypeStruct((1, hidden_width), F32),
            jax.ShapeDtypeStruct((1, width), F32),
        ],
        compiler_params=params(48),
        cost_estimate=cost(8 * total * width * hidden_width, 32 * MIB, total * hidden_width),
        name="expert_rows",
    )(rows, up, own, w_router, w_in, b_in, w_out, b_out)


def weight_kernel(left_ref, right_ref, out_ref, turned):
    @pl.when(pl.program_id(0) == 0)
    def turn():
        turned[...] = left_ref[...].T

    out_ref[...] = dot(turned[...], right_ref[...]).astype(BF16)


def weight_grad(left, right, block=512):
    total, width = left.shape
    hidden_width = right.shape[1]
    return pl.pallas_call(
        weight_kernel,
        grid=(hidden_width // block,),
        in_specs=[whole(left.shape), pl.BlockSpec((total, block), lambda i: (0, i))],
        out_specs=pl.BlockSpec((width, block), lambda i: (0, i)),
        out_shape=jax.ShapeDtypeStruct((width, hidden_width), BF16),
        scratch_shapes=[pltpu.VMEM((width, total), BF16)],
        compiler_params=params(60),
        cost_estimate=cost(2 * total * width * hidden_width, 14 * MIB),
        name="weight_grad",
    )(left, right)


def turned_sum_kernel(own_ref, far_ref, out_ref):
    out_ref[...] = (own_ref[...].astype(F32) + far_ref[...].astype(F32)).T


def turned_sum(own, far, block=512):
    width, hidden_width = own.shape
    return pl.pallas_call(
        turned_sum_kernel,
        grid=(hidden_width // block,),
        in_specs=[pl.BlockSpec((width, block), lambda i: (0, i))] * 2,
        out_specs=pl.BlockSpec((block, width), lambda i: (i, 0)),
        out_shape=jax.ShapeDtypeStruct((hidden_width, width), F32),
        compiler_params=params(32),
        cost_estimate=cost(width * hidden_width, 8 * width * hidden_width),
        name="turned_sum",
    )(own, far)


def combine_kernel(slots_ref, y_ref, resid_ref, out_ref, moment_ref):
    step, total = out_ref.shape[0], y_ref.shape[0]
    places = lax.broadcasted_iota(jnp.int32, (step, total), 1)
    moe = dot(hits((slots_ref[:, 0:1], slots_ref[:, 1:2]), places), y_ref[...])
    out_ref[...] = (resid_ref[...] + moe).astype(BF16)
    moment = jnp.sum(moe * moe, 0, keepdims=True)
    moment_ref[...] = jnp.where(pl.program_id(0) == 0, 0.0, moment_ref[...]) + moment


def combine_rows(slot_columns, y, resid, step):
    tokens, width = resid.shape
    total = y.shape[0]
    block = lambda size: pl.BlockSpec((step, size), lambda i: (i, 0))
    return pl.pallas_call(
        combine_kernel,
        grid=(tokens // step,),
        in_specs=[block(TOP), whole(y.shape), block(width)],
        out_specs=[block(width), whole((1, width))],
        out_shape=[
            jax.ShapeDtypeStruct((tokens, width), BF16),
            jax.ShapeDtypeStruct((1, width), F32),
        ],
        compiler_params=params(40),
        cost_estimate=cost(2 * total * tokens * width, 8 * MIB),
        name="combine_rows",
    )(slot_columns, y, resid)


def token_back_kernel(
    capacity,
    slots,
    flag_ref,
    columns_ref,
    lines_ref,
    back_ref,
    resid_ref,
    normed_ref,
    heads_ref,
    up_ref,
    w_out_ref,
    router_ref,
    gain_ref,
    d_resid_out,
    d_heads_out,
    attn_sum,
    router_sum,
    gain_sum,
    d_weights,
):
    del flag_ref
    step, width = resid_ref.shape
    total = back_ref.shape[0]
    experts = router_ref.shape[0]
    first = pl.program_id(0) == 0

    @pl.when(first)
    def columns():
        row = lax.broadcasted_iota(jnp.int32, (slots, 256), 0)
        lane = lax.broadcasted_iota(jnp.int32, (slots, 256), 1)
        for e in range(experts):
            block = back_ref[e * slots : (e + 1) * slots, 0:256].astype(F32)
            line = jnp.sum(jnp.where(row >= capacity, block, 0.0), 0, keepdims=True)
            column = jnp.sum(jnp.where(row == lane, line, 0.0), -1, keepdims=True)
            d_weights[e * slots : (e + 1) * slots, :] = jnp.broadcast_to(column, (slots, step))

    def accumulate(ref, value):
        ref[...] = jnp.where(first, 0.0, ref[...]) + value

    line_slots = (lines_ref[0:1, :], lines_ref[1:2, :])
    d_gates = []
    for e in range(experts):
        places = lax.broadcasted_iota(jnp.int32, (slots, step), 0) + e * slots
        hit = (places == line_slots[0]) | (places == line_slots[1])
        d_gates.append(
            jnp.sum(
                jnp.where(hit, d_weights[e * slots : (e + 1) * slots, :], 0.0), 0, keepdims=True
            )
        )
    d_gates = jnp.concatenate(d_gates, 0)
    logits = dot(router_ref[...], normed_ref[...], 1, 1)
    gates = jnp.exp(logits - jnp.max(logits, 0, keepdims=True))
    gates = gates / jnp.sum(gates, 0, keepdims=True)
    d_logits = (gates * (d_gates - jnp.sum(gates * d_gates, 0, keepdims=True))).astype(BF16)
    places = lax.broadcasted_iota(jnp.int32, (step, total), 1)
    d_normed = dot(hits((columns_ref[:, 0:1], columns_ref[:, 1:2]), places), back_ref[...])
    d_normed += dot(d_logits, router_ref[...], 0, 0)
    normed, inverse = normalize(resid_ref[...])
    d_resid = up_ref[...].astype(F32) + norm_back(d_normed * gain_ref[...], normed, inverse)
    d_attn = d_resid.astype(BF16)
    d_resid_out[...] = d_resid
    d_heads_out[...] = dot(d_attn, w_out_ref[...], 1, 1).astype(BF16)
    accumulate(attn_sum, dot(heads_ref[...], d_attn, 0, 0))
    accumulate(router_sum, dot(d_logits, normed_ref[...]))
    accumulate(gain_sum, jnp.sum(d_normed * normed, 0, keepdims=True))


def token_back(
    flag,
    slot_columns,
    slot_rows,
    back,
    resid,
    normed,
    heads,
    up,
    w_attn_out,
    w_router_t,
    gain,
    capacity,
    slots,
    step,
    part,
):
    tokens, width = resid.shape
    total = back.shape[0]
    experts = w_router_t.shape[0]
    images = tokens // step
    block = lambda size: pl.BlockSpec((step, size), lambda i, flag_ref: (i, 0))
    return pl.pallas_call(
        functools.partial(token_back_kernel, capacity, slots),
        grid_spec=pltpu.PrefetchScalarGridSpec(
            num_scalar_prefetch=1,
            grid=(images,),
            in_specs=[
                block(TOP),
                pl.BlockSpec((TOP, step), lambda i, flag_ref: (0, i)),
                whole(back.shape),
                block(width),
                block(width),
                block(width),
                block(width),
                whole(w_attn_out.shape),
                whole(w_router_t.shape),
                whole(gain.shape),
            ],
            out_specs=[
                block(width),
                pl.BlockSpec(
                    (step, width),
                    lambda i, flag_ref: (lax.rem(i + flag_ref[0] * part, images), 0),
                ),
                whole((width, width)),
                whole((experts, width)),
                whole((1, width)),
            ],
            scratch_shapes=[pltpu.VMEM((total, step), F32)],
        ),
        out_shape=[
            jax.ShapeDtypeStruct((tokens, width), F32),
            jax.ShapeDtypeStruct((tokens, width), BF16),
            jax.ShapeDtypeStruct((width, width), F32),
            jax.ShapeDtypeStruct((experts, width), F32),
            jax.ShapeDtypeStruct((1, width), F32),
        ],
        compiler_params=params(48),
        cost_estimate=cost(2 * (total + 2 * width) * tokens * width, 14 * MIB),
        name="token_back",
    )(
        flag,
        slot_columns,
        slot_rows,
        back,
        resid,
        normed,
        heads,
        up,
        w_attn_out,
        w_router_t,
        gain,
    )


def grad_sum_kernel(flag_ref, resid_ref, own_ref, far_ref, out_ref):
    mine = (flag_ref[0] == 0) == (pl.program_id(0) < pl.num_programs(0) // 2)
    out_ref[...] = resid_ref[...] + jnp.where(mine, own_ref[0], far_ref[0]).astype(F32)


def grad_sum(flag, d_resid, own, far):
    part, rows, width = own.shape
    tokens = d_resid.shape[0]
    pick = pl.BlockSpec((1, rows, width), lambda i, flag_ref: (lax.rem(i, part), 0, 0))
    return pl.pallas_call(
        grad_sum_kernel,
        grid_spec=pltpu.PrefetchScalarGridSpec(
            num_scalar_prefetch=1,
            grid=(tokens // rows,),
            in_specs=[pl.BlockSpec((rows, width), lambda i, flag_ref: (i, 0)), pick, pick],
            out_specs=pl.BlockSpec((rows, width), lambda i, flag_ref: (i, 0)),
        ),
        out_shape=jax.ShapeDtypeStruct((tokens, width), F32),
        compiler_params=params(16),
        cost_estimate=cost(tokens * width, 6 * MIB),
        name="grad_sum",
    )(flag, d_resid, own, far)


AXES = ("wide", "narrow")


def device_bits():
    n_narrow = lax.axis_size("narrow")
    masks = [1 << b for b in range((n_narrow * lax.axis_size("wide")).bit_length() - 1)]
    masks.remove(n_narrow)
    return [n_narrow] + masks


def sum_steps():
    first, *rest = device_bits()
    return [(first,)] + [tuple(rest[i : i + 2]) for i in range(0, len(rest), 2)]


def swap(value, mask, axes=AXES):
    size = math.prod(lax.axis_size(axis) for axis in axes)
    return lax.ppermute(value, axes, [(i, i ^ mask) for i in range(size)])


def partners(bits):
    me = lax.axis_index(AXES)
    place = sum(((me // bit) % 2) << b for b, bit in enumerate(bits))
    masks = [
        sum(bit for b, bit in enumerate(bits) if (j >> b) & 1) for j in range(1 << len(bits))
    ]
    return masks, place


def fold_kernel(given, members, place_ref, keep_ref, *refs):
    del place_ref
    step = pl.program_id(0)
    total = keep_ref[...]
    for far_ref in refs[:given]:
        total += far_ref[...].astype(F32)
    own_out, *send_outs = refs[given:]

    @pl.when(step == 0)
    def keep():
        own_out[...] = total

    for j, send_out in enumerate(send_outs):

        @pl.when(step == j + 1)
        def send():
            send_out[...] = total.astype(BF16)


def fold(keep, far, bits):
    masks, place = partners(bits)
    members = len(masks)
    rows, size = keep.shape
    part = rows // members
    pick = pl.BlockSpec((part, size), lambda j, place_ref: (place_ref[0] ^ j, 0))
    own, *send = pl.pallas_call(
        functools.partial(fold_kernel, len(far), members),
        grid_spec=pltpu.PrefetchScalarGridSpec(
            num_scalar_prefetch=1,
            grid=(members,),
            in_specs=[pick] * (1 + len(far)),
            out_specs=[whole((part, size))] * members,
        ),
        out_shape=[jax.ShapeDtypeStruct((part, size), F32)]
        + [jax.ShapeDtypeStruct((part, size), BF16)] * (members - 1),
        compiler_params=params(32),
        cost_estimate=cost(0, 8 * rows * size),
        name="fold",
    )(place.reshape(1).astype(jnp.int32), keep, *far)
    return own, [swap(value, mask) for value, mask in zip(send, masks[1:])]


def sum_parts(value, bits):
    masks, place = partners(bits)
    part = value.shape[0] // len(masks)
    pick = lambda j: lax.dynamic_slice_in_dim(value, (place ^ j) * part, part, 0)
    far = [swap(pick(j).astype(BF16), masks[j]) for j in range(1, len(masks))]
    total = pick(0)
    for term in far:
        total = total + term.astype(F32)
    return total


def spread_parts(value, bits):
    masks, place = partners(bits)
    parts = [value] + [swap(value, mask) for mask in masks[1:]]
    for b in range(len(bits)):
        side = (place >> b) % 2 == 0
        parts = [
            jnp.where(
                side,
                jnp.concatenate([parts[i], parts[i + 1]], 0),
                jnp.concatenate([parts[i + 1], parts[i]], 0),
            )
            for i in range(0, len(parts), 2)
        ]
    return parts[0]


def sums_kernel(flag_ref, own_ref, far_ref, qkv_out, attn_out, small_out):
    half, width = own_ref.shape[0], attn_out.shape[1]
    upper = flag_ref[1] == 1
    own, far = own_ref[...].astype(F32), far_ref[...].astype(F32)
    for rows, value in ((0, jnp.where(upper, far, own)), (half, jnp.where(upper, own, far))):
        rows = slice(rows, rows + half)
        qkv_out[rows, :] = value[:, : 3 * width]
        attn_out[rows, :] = value[:, 3 * width : 4 * width]
        small_out[rows, :] = value[:, 4 * width :]


def sums_apart(flag, own, far):
    width = 2 * own.shape[0]
    shapes = [(width, 3 * width), (width, width), (width, SMALL)]
    return pl.pallas_call(
        sums_kernel,
        grid_spec=pltpu.PrefetchScalarGridSpec(
            num_scalar_prefetch=1,
            grid=(1,),
            in_specs=[whole(own.shape), whole(far.shape)],
            out_specs=[whole(shape) for shape in shapes],
        ),
        out_shape=[jax.ShapeDtypeStruct(shape, F32) for shape in shapes],
        compiler_params=params(32),
        cost_estimate=cost(0, 8 * MIB),
        name="sums_apart",
    )(flag, own, far)


def gathered_attention(inputs, gain_one, w_qkv):
    images, rows_dev, width = inputs.shape
    tokens = images * rows_dev
    head_dim = width // HEADS
    scale = head_dim ** (-0.5)
    seq_len = rows_dev * lax.axis_size("narrow")
    group = math.gcd(images, max(1, 512 // rows_dev))
    blocks = images // group
    normed_one, inverse_one = normalize(inputs.astype(F32).reshape(tokens, width))
    input_one = (normed_one * gain_one).astype(BF16)
    projected = jnp.dot(input_one, w_qkv, preferred_element_type=F32).astype(BF16)
    queries = projected[:, :width].reshape(images, rows_dev, width)
    keys_own = projected[:, width : 2 * width].reshape(images, rows_dev, width)
    values_own = projected[:, 2 * width :].reshape(images, rows_dev, width)
    keys_all = lax.all_gather(keys_own, "narrow", axis=1, tiled=True)
    values_all = lax.all_gather(values_own, "narrow", axis=1, tiled=True)
    query_blocks = queries.reshape(blocks, group, rows_dev, HEADS, head_dim)
    key_blocks = keys_all.reshape(blocks, group, seq_len, HEADS, head_dim)
    value_blocks = values_all.reshape(blocks, group, seq_len, HEADS, head_dim)

    def attend_block(operands):
        query_b, key_b, value_b = operands
        scores = jnp.einsum("gqhd,gkhd->ghqk", query_b, key_b, preferred_element_type=F32) * scale
        top_score = jnp.max(scores, -1, keepdims=True)
        exponent = jnp.exp(scores - top_score)
        total = jnp.sum(exponent, -1, keepdims=True)
        weights = (exponent / total).astype(BF16)
        mixed = jnp.einsum("ghqk,gkhd->gqhd", weights, value_b, preferred_element_type=F32)
        return (mixed.astype(BF16), (top_score + jnp.log(total))[..., 0])

    heads_out, log_total = lax.map(attend_block, (query_blocks, key_blocks, value_blocks))

    def back_block(operands):
        query_b, key_b, value_b, total_b, d_head_b = operands
        scores = jnp.einsum("gqhd,gkhd->ghqk", query_b, key_b, preferred_element_type=F32) * scale
        weights = jnp.exp(scores - total_b[..., None])
        d_weights = jnp.einsum("gqhd,gkhd->ghqk", d_head_b, value_b, preferred_element_type=F32)
        spread = jnp.sum(weights * d_weights, -1, keepdims=True)
        d_scores = (weights * (d_weights - spread)).astype(BF16)
        d_query = jnp.einsum("ghqk,gkhd->gqhd", d_scores, key_b, preferred_element_type=F32) * scale
        d_key = jnp.einsum("ghqk,gqhd->gkhd", d_scores, query_b, preferred_element_type=F32) * scale
        d_value = jnp.einsum(
            "ghqk,gqhd->gkhd", weights.astype(BF16), d_head_b, preferred_element_type=F32
        )
        return (d_query.astype(BF16), d_key, d_value)

    def back(d_heads, d_resid):
        d_head_blocks = d_heads.reshape(blocks, group, rows_dev, HEADS, head_dim)
        d_queries, key_terms, value_terms = lax.map(
            back_block, (query_blocks, key_blocks, value_blocks, log_total, d_head_blocks)
        )
        d_keys, d_values = (
            lax.psum_scatter(
                terms.reshape(images, seq_len, width), "narrow", scatter_dimension=1, tiled=True
            )
            .astype(BF16)
            .reshape(tokens, width)
            for terms in (key_terms, value_terms)
        )
        d_projected = jnp.concatenate([d_queries.reshape(tokens, width), d_keys, d_values], 1)
        d_weight = jnp.dot(input_one.T, d_projected, preferred_element_type=F32)
        d_input = jnp.dot(d_projected, w_qkv.T, preferred_element_type=F32)
        d_gain = jnp.sum(d_input * normed_one, 0, keepdims=True)
        return (
            d_resid + norm_back(d_input * gain_one, normed_one, inverse_one),
            d_weight,
            d_gain,
        )

    return heads_out.reshape(images, rows_dev, width), back


def shards(
    inputs,
    cotangent,
    ln1_gain,
    w_qkv,
    w_attn_out,
    ln2_gain,
    w_router,
    expert_in,
    expert_in_bias,
    expert_out,
    expert_out_bias,
    route_ids,
    route_slots,
    route_dropped,
):
    images, rows_dev, width = inputs.shape
    tokens = images * rows_dev
    experts = w_router.shape[1]
    n_wide = lax.axis_size("wide")
    n_narrow = lax.axis_size("narrow")
    capacity = max(2, 42 * tokens // (20 * experts))
    slots = -(-(capacity + 2) // 8) * 8
    total = experts * slots
    gain_one = ln1_gain.astype(F32).reshape(1, width)
    gain_two = ln2_gain.astype(F32).reshape(1, width)
    paired = n_narrow == 2 and images % 2 == 0
    part = images // 2
    place = lax.axis_index("narrow") if paired else jnp.int32(0)
    flag = jnp.stack([place, lax.axis_index("wide") % 2])

    slot_columns = jnp.where(
        route_dropped == 0, route_ids * slots + route_slots, -1
    ).reshape(tokens, TOP)
    slot_rows = slot_columns.T
    up = cotangent.reshape(tokens, width)

    def exchange(rows):
        return lax.all_to_all(
            rows.reshape(experts, slots, width), "wide", split_axis=0, concat_axis=0, tiled=True
        ).reshape(total, width)

    if paired:
        sent = lax.dynamic_slice_in_dim(inputs, (1 - place) * part, part, 0)
        far_inputs = swap(sent, 1)
        w_qkv_t = w_qkv.T
    up_rows = dispatch_rows(slot_rows, up, total)
    if paired:
        far_inputs, up_rows, w_qkv_t = lax.optimization_barrier((far_inputs, up_rows, w_qkv_t))
    up_here = exchange(up_rows)

    if paired:
        heads_own, heads_far, proj, log_total = attend(
            flag, inputs, far_inputs, gain_one, w_qkv_t
        )
        heads_far = swap(heads_far, 1)
    else:
        heads_own, attention_back = gathered_attention(inputs, gain_one, w_qkv)
        heads_own, heads_far = heads_own[:part], heads_own[part:]

    heads, resid, normed_two, rows, moments = residual_rows(
        flag, heads_own, heads_far, inputs, w_attn_out, gain_two, slot_rows, total
    )
    rows_here = exchange(rows)
    own = (jnp.arange(experts) == lax.axis_index("wide")).astype(F32).reshape(1, experts)
    w_in, w_out = expert_in[0], expert_out[0]
    y, back, act, d_hidden, d_y, b_in_sum, b_out_sum = expert_rows(
        rows_here,
        up_here,
        own,
        w_router,
        w_in,
        expert_in_bias.astype(F32),
        w_out,
        expert_out_bias.astype(F32),
        capacity,
        slots,
    )
    back = exchange(back)
    grad_out_t = weight_grad(d_y, act)
    grad_in = weight_grad(rows_here, d_hidden)
    back, *unused = lax.optimization_barrier((back, grad_out_t, grad_in))
    if n_narrow == 2:
        far_out_t = swap(grad_out_t, 1)

    d_resid, d_heads, attn_term, router_term, gain_two_term = token_back(
        flag,
        slot_columns,
        slot_rows,
        back,
        resid,
        normed_two,
        heads,
        up,
        w_attn_out,
        w_router.T,
        gain_two,
        capacity,
        slots,
        rows_dev,
        part,
    )
    d_heads = d_heads.reshape(images, rows_dev, width)
    sent, y, grad_in = lax.optimization_barrier((d_heads[part:], y, grad_in))
    biases = jnp.concatenate([b_in_sum, b_out_sum], 1)
    small = jnp.concatenate([router_term, gain_two_term, moments], 0)
    steps = sum_steps()
    if paired:
        d_far = swap(sent, 1)
        far_in = swap(grad_in, 1)
        far_biases = swap(biases, 1)
        y = exchange(y)
        d_far, far_out_t = lax.optimization_barrier((d_far, far_out_t))
        d_own, d_far, keep, send = attend_back(
            flag,
            inputs,
            far_inputs,
            gain_one,
            w_qkv_t,
            proj,
            log_total,
            d_heads,
            d_far,
            attn_term,
            small,
        )
        keep, send, d_far, far_out_t = lax.optimization_barrier((keep, send, d_far, far_out_t))
        grad_expert_out = turned_sum(grad_out_t, far_out_t)
        keep, send, d_far, far_in, grad_expert_out = lax.optimization_barrier(
            (keep, send, d_far, far_in, grad_expert_out)
        )
        sums, far = fold(keep, [swap(send, steps[0][0])], steps[1])
        grad_expert_in = grad_in.astype(F32) + far_in.astype(F32)
        sums, far, y, d_far, grad_expert_in, far_biases = lax.optimization_barrier(
            (sums, far, y, d_far, grad_expert_in, far_biases)
        )
        d_far = swap(d_far, 1)
        biases = biases + far_biases
        for bits in steps[2:]:
            sums, far = fold(sums, far, bits)
        for term in far:
            sums = sums + term.astype(F32)
    else:
        y = exchange(y)
        grad_out_t, grad_in = lax.psum((grad_out_t, grad_in), "narrow")
        grad_expert_out = grad_out_t.astype(F32).T
        grad_expert_in = grad_in.astype(F32)
        biases = lax.psum(biases, "narrow")
        input_grad, qkv_term, gain_one_term = attention_back(d_heads, d_resid)
        small = small_columns(small, gain_one_term)
        sums = jnp.concatenate([qkv_term, attn_term, small], 1)
        for bits in steps:
            sums = sum_parts(sums, bits)
    block_out, moe_moment = combine_rows(slot_columns, y, resid, rows_dev)
    moe_moment = jnp.sum(moe_moment)
    high = moe_moment.astype(BF16).astype(F32)
    row = lax.broadcasted_iota(jnp.int32, sums.shape, 0)
    lane = lax.broadcasted_iota(jnp.int32, sums.shape, 1) - 4 * width - (experts + 4)
    extra = jnp.where(lane == 0, high, jnp.where(lane == 1, moe_moment - high, 0.0))
    sums = jnp.where((row == 0) & (lane >= 0), extra, sums).astype(BF16)
    for bits in reversed(steps[2:]):
        sums = spread_parts(sums, bits)
    if paired:
        sums, d_far, block_out = lax.optimization_barrier((sums, d_far, block_out))
        input_grad = grad_sum(flag, d_resid, d_own, d_far)
    sums = spread_parts(sums, steps[1])
    if paired:
        sums, input_grad = lax.optimization_barrier((sums, input_grad))
    grad_qkv, grad_attn_out, small = sums_apart(flag, sums, swap(sums, steps[0][0]))
    moment_count = tokens * width * n_wide * n_narrow
    moments = jnp.sum(small[:, experts + 1 : experts + 6], 0)
    moments = jnp.stack([moments[0], moments[1], moments[3] + moments[4]])
    stats = jnp.sqrt(moments / moment_count + EPS)
    return (
        block_out.reshape(images, rows_dev, width),
        input_grad.reshape(images, rows_dev, width),
        small[:, experts + 3],
        grad_qkv,
        grad_attn_out,
        small[:, experts],
        small[:, :experts],
        grad_expert_in[None],
        biases[:, : w_in.shape[1]],
        grad_expert_out[None],
        biases[:, w_in.shape[1] :],
        stats,
    )


def solution(mesh):
    return jax.shard_map(
        shards,
        mesh=mesh,
        in_specs=(
            P("wide", "narrow", None),
            P("wide", "narrow", None),
            P(),
            P(),
            P(),
            P(),
            P(),
            P("wide", None, None),
            P("wide", None),
            P("wide", None, None),
            P("wide", None),
            P("wide", "narrow", None),
            P("wide", "narrow", None),
            P("wide", "narrow", None),
        ),
        out_specs=(
            P("wide", "narrow", None),
            P("wide", "narrow", None),
            P(),
            P(),
            P(),
            P(),
            P(),
            P("wide", None, None),
            P("wide", None),
            P("wide", None, None),
            P("wide", None),
            P(),
        ),
        check_vma=False,
    )
```

```python
import functools
import math

import jax
import jax.numpy as jnp
from jax import lax
from jax.experimental import pallas as pl
from jax.experimental.pallas import tpu as pltpu
from jax.sharding import PartitionSpec as P

HEADS = 8
TOP = 2


EPS = 1e-06
BF16 = jnp.bfloat16
F32 = jnp.float32
MIB = 1 << 20
SMALL = 128
EARLY = 5


def normalize(values):
    centre = jnp.mean(values, -1, keepdims=True)
    shifted = values - centre
    inverse = lax.rsqrt(jnp.mean(shifted * shifted, -1, keepdims=True) + EPS)
    return (shifted * inverse, inverse)


def norm_back(d_normed, normed, inverse):
    return inverse * (
        d_normed
        - jnp.mean(d_normed, -1, keepdims=True)
        - normed * jnp.mean(d_normed * normed, -1, keepdims=True)
    )


def dot(left, right, left_dim=1, right_dim=0):
    return lax.dot_general(
        left, right, (((left_dim,), (right_dim,)), ((), ())), preferred_element_type=F32
    )


def params(mib):
    return pltpu.CompilerParams(vmem_limit_bytes=mib * MIB)


def in_hbm(value):
    return pltpu.with_memory_space_constraint(value, pltpu.HBM)


def in_vmem(value):
    return pltpu.with_memory_space_constraint(value, pltpu.VMEM)


def cost(flops, bytes_accessed, transcendentals=0):
    return pl.CostEstimate(
        flops=int(flops), bytes_accessed=int(bytes_accessed), transcendentals=int(transcendentals)
    )


def whole(shape):
    return pl.BlockSpec(shape, lambda *unused: (0,) * len(shape))


def hits(slots, places):
    first, second = slots
    return jnp.where((places == first) | (places == second), 1.0, 0.0).astype(BF16)


def put_rows(slots_ref, rows_ref, out_ref):
    step = out_ref.shape[0]
    places = lax.broadcasted_iota(jnp.int32, (step, rows_ref.shape[0]), 0) + pl.program_id(0) * step
    out_ref[...] = dot(hits((slots_ref[0:1, :], slots_ref[1:2, :]), places), rows_ref[...]).astype(
        BF16
    )


def dispatch_rows(slot_rows, rows, total, steps=8):
    tokens, width = rows.shape
    step = total // steps
    return pl.pallas_call(
        put_rows,
        grid=(steps,),
        in_specs=[whole(slot_rows.shape), whole(rows.shape)],
        out_specs=pl.BlockSpec((step, width), lambda i: (i, 0)),
        out_shape=jax.ShapeDtypeStruct((total, width), BF16),
        compiler_params=params(20),
        cost_estimate=cost(2 * total * tokens * width, 4 * total * width),
        name="dispatch_rows",
    )(slot_rows, rows)


def attend_kernel(flag_ref, own_ref, far_ref, gain_ref, wt_ref, *refs):
    del flag_ref
    own_out, far_out, proj_ref, total_ref, mixed = refs[-5:]
    rows, width = own_ref.shape[1], own_ref.shape[2]
    head_dim = width // HEADS
    scale = head_dim ** (-0.5)
    x_float = jnp.concatenate([own_ref[0], far_ref[0]], 0).astype(F32)
    normed, unused = normalize(x_float)
    normed = (normed * gain_ref[...]).astype(BF16)
    proj_ref[0] = dot(wt_ref[...], normed, 1, 1).astype(BF16)

    def head(h, carry):
        at = pl.multiple_of(h * head_dim, head_dim)
        query = proj_ref[0, pl.ds(at, head_dim), :]
        key = proj_ref[0, pl.ds(at + width, head_dim), :]
        value = proj_ref[0, pl.ds(at + 2 * width, head_dim), :]
        scores = dot(key, query * scale, 0, 0)
        top = jnp.max(scores, 0, keepdims=True)
        exponent = jnp.exp(scores - top)
        total = jnp.sum(exponent, 0, keepdims=True)
        out = dot(value, exponent.astype(BF16)) * (1.0 / total)
        mixed[pl.ds(at, head_dim), :] = out
        total_ref[0, pl.ds(h, 1), :] = top + jnp.log(total)
        return carry

    lax.fori_loop(0, HEADS, head, 0, unroll=True)
    heads_out = mixed[...].T.astype(BF16)
    own_out[0] = heads_out[:rows]
    far_out[0] = heads_out[rows:]


def attend(flag, inputs, image, far, gain, w_qkv_t, kept):
    unused, rows, width = far.shape
    seq_len = 2 * rows
    part = inputs.shape[0] // 2
    block = lambda k, *shape: pl.BlockSpec((1,) + shape, lambda i, flag_ref: (k,) + (0,) * len(shape))
    return pl.pallas_call(
        attend_kernel,
        grid_spec=pltpu.PrefetchScalarGridSpec(
            num_scalar_prefetch=1,
            grid=(1,),
            in_specs=[
                pl.BlockSpec(
                    (1, rows, width), lambda i, flag_ref: (image + flag_ref[0] * part, 0, 0)
                ),
                block(0, rows, width),
                whole(gain.shape),
                whole(w_qkv_t.shape),
            ]
            + [pl.BlockSpec(memory_space=pl.ANY)] * len(kept),
            out_specs=[
                block(0, rows, width),
                block(0, rows, width),
                block(image, 3 * width, seq_len),
                block(image, HEADS, seq_len),
            ],
            scratch_shapes=[pltpu.VMEM((width, seq_len), F32)],
        ),
        out_shape=[
            jax.ShapeDtypeStruct((1, rows, width), BF16),
            jax.ShapeDtypeStruct((1, rows, width), BF16),
            pltpu.HBM((part, 3 * width, seq_len), BF16),
            pltpu.HBM((part, HEADS, seq_len), F32),
        ],
        input_output_aliases={5 + i: 2 + i for i in range(len(kept))},
        compiler_params=params(28),
        cost_estimate=cost(8e9, 8 * MIB, HEADS * seq_len**2),
        name="attend",
    )(flag, in_hbm(inputs), far, gain, w_qkv_t, *kept)


def small_columns(small, gain):
    rest = jnp.zeros((SMALL - small.shape[0] - 1, small.shape[1]), F32)
    return jnp.concatenate([small, gain, rest], 0).T


def attend_back_kernel(
    flag_ref,
    own_ref,
    far_ref,
    gain_ref,
    wt_ref,
    proj_ref,
    total_ref,
    d_own_ref,
    d_far_ref,
    attn_ref,
    small_ref,
    own_out,
    far_out,
    keep_out,
    send_out,
    d_proj,
    d_mixed,
    weight_sum,
    gain_out,
):
    image, last = pl.program_id(0), pl.num_programs(0) - 1
    rows, width = own_ref.shape[1], own_ref.shape[2]
    head_dim = width // HEADS
    scale = head_dim ** (-0.5)
    d_mixed[...] = jnp.concatenate([d_own_ref[0], d_far_ref[0]], 0).astype(F32).T.astype(BF16)

    def head(h, carry):
        at = pl.multiple_of(h * head_dim, head_dim)
        query = proj_ref[0, pl.ds(at, head_dim), :]
        key = proj_ref[0, pl.ds(at + width, head_dim), :]
        value = proj_ref[0, pl.ds(at + 2 * width, head_dim), :]
        d_out = d_mixed[pl.ds(at, head_dim), :]
        weights = jnp.exp(dot(key, query * scale, 0, 0) - total_ref[0, pl.ds(h, 1), :])
        product = weights * dot(value, d_out, 0, 0)
        spread = jnp.sum(product, 0, keepdims=True)
        d_scores = (product - weights * spread).astype(BF16)
        d_proj[pl.ds(at, head_dim), :] = (dot(key, d_scores) * scale).astype(BF16)
        d_proj[pl.ds(at + width, head_dim), :] = (dot(query, d_scores, 1, 1) * scale).astype(BF16)
        d_proj[pl.ds(at + 2 * width, head_dim), :] = dot(d_out, weights.astype(BF16), 1, 1).astype(
            BF16
        )
        return carry

    lax.fori_loop(0, HEADS, head, 0, unroll=True)
    x_float = jnp.concatenate([own_ref[0], far_ref[0]], 0).astype(F32)
    normed, inverse = normalize(x_float)
    d_input = dot(d_proj[...], wt_ref[...], 0, 0)
    weight_term = dot((normed * gain_ref[...]).T.astype(BF16), d_proj[...], 1, 1)
    gain_term = jnp.sum(d_input * normed, 0, keepdims=True)
    d_x = norm_back(d_input * gain_ref[...], normed, inverse).astype(BF16)
    own_out[0] = d_x[:rows]
    far_out[0] = d_x[rows:]

    @pl.when(image == 0)
    def start():
        weight_sum[...] = weight_term
        gain_out[...] = gain_term

    @pl.when(image != 0)
    def add():
        weight_sum[...] += weight_term
        gain_out[...] += gain_term

    @pl.when(image == last)
    def finish():
        half = width // 2
        parts = ((weight_sum[...], 0), (attn_ref[...], 3 * width))
        parts += ((small_columns(small_ref[...], gain_out[...]), 4 * width),)
        upper = flag_ref[1] == 1
        for value, at in parts:
            at = slice(at, at + value.shape[1])
            keep_out[:, at] = jnp.where(upper, value[half:], value[:half])
            send_out[:, at] = jnp.where(upper, value[:half], value[half:]).astype(BF16)


def attend_back(flag, inputs, far, gain, w_qkv_t, proj, total, d_heads, d_far, attn_term, small):
    part, rows, width = far.shape
    seq_len = 2 * rows
    block = lambda *shape: pl.BlockSpec((1,) + shape, lambda i, flag_ref: (i,) + (0,) * len(shape))
    return pl.pallas_call(
        attend_back_kernel,
        grid_spec=pltpu.PrefetchScalarGridSpec(
            num_scalar_prefetch=1,
            grid=(part,),
            in_specs=[
                pl.BlockSpec((1, rows, width), lambda i, flag_ref: (i + flag_ref[0] * part, 0, 0)),
                block(rows, width),
                whole(gain.shape),
                whole(w_qkv_t.shape),
                block(3 * width, seq_len),
                block(HEADS, seq_len),
                block(rows, width),
                block(rows, width),
                whole(attn_term.shape),
                whole(small.shape),
            ],
            out_specs=[
                block(rows, width),
                block(rows, width),
                whole((width // 2, 4 * width + SMALL)),
                whole((width // 2, 4 * width + SMALL)),
            ],
            scratch_shapes=[
                pltpu.VMEM((3 * width, seq_len), BF16),
                pltpu.VMEM((width, seq_len), BF16),
                pltpu.VMEM((width, 3 * width), F32),
                pltpu.VMEM((1, width), F32),
            ],
        ),
        out_shape=[
            pltpu.HBM((part, rows, width), BF16),
            pltpu.HBM((part, rows, width), BF16),
            pltpu.HBM((width // 2, 4 * width + SMALL), F32),
            jax.ShapeDtypeStruct((width // 2, 4 * width + SMALL), BF16),
        ],
        compiler_params=params(36),
        cost_estimate=cost(part * 16e9, 12 * MIB, part * HEADS * seq_len**2),
        name="attend_back",
    )(
        flag,
        in_hbm(inputs),
        in_hbm(far),
        gain,
        in_hbm(w_qkv_t),
        in_hbm(proj),
        total,
        in_hbm(d_heads),
        d_far,
        in_hbm(attn_term),
        small,
    )


def pick_image(flag_ref, image, images, own_refs, far_refs):
    part = images // 2
    mine = (flag_ref[0] == 0) == (image < part)
    value = jnp.where(mine, own_refs[0][0], far_refs[0][0])
    for k in range(1, part):
        other = jnp.where(mine, own_refs[k][0], far_refs[k][0])
        value = jnp.where(lax.rem(image, part) == k, other, value)
    return value


def residual_kernel(images, flag_ref, *refs):
    own_refs, far_refs, refs = refs[: images // 2], refs[images // 2 : images], refs[images:]
    x_ref, w_out_ref, gain_ref, heads_out, resid_out, normed_out, moments_out = refs
    image = pl.program_id(0)
    heads = pick_image(flag_ref, image, images, own_refs, far_refs)
    attn = dot(heads, w_out_ref[...])
    resid = x_ref[0].astype(F32) + attn
    normed, unused = normalize(resid)
    heads_out[...] = heads
    resid_out[...] = resid
    normed_out[...] = (normed * gain_ref[...]).astype(BF16)
    moments = [jnp.sum(value * value, 0, keepdims=True) for value in (resid, attn)]
    moments_out[...] = jnp.where(image == 0, 0.0, moments_out[...]) + jnp.concatenate(moments, 0)


def residual_rows(flag, own, far, inputs, w_attn_out, gain):
    images, rows, width = inputs.shape
    tokens = images * rows
    block = pl.BlockSpec((rows, width), lambda i, flag_ref: (i, 0))
    return pl.pallas_call(
        functools.partial(residual_kernel, images),
        grid_spec=pltpu.PrefetchScalarGridSpec(
            num_scalar_prefetch=1,
            grid=(images,),
            in_specs=[whole((1, rows, width))] * images
            + [
                pl.BlockSpec((1, rows, width), lambda i, flag_ref: (i, 0, 0)),
                whole(w_attn_out.shape),
                whole(gain.shape),
            ],
            out_specs=[block, block, block, whole((2, width))],
        ),
        out_shape=[
            pltpu.HBM((tokens, width), BF16),
            pltpu.HBM((tokens, width), F32),
            jax.ShapeDtypeStruct((tokens, width), BF16),
            jax.ShapeDtypeStruct((2, width), F32),
        ],
        compiler_params=params(24),
        cost_estimate=cost(2 * width * tokens * width, 10 * MIB),
        name="residual_rows",
    )(flag, *own, *far, in_hbm(inputs), w_attn_out, gain)


def blocks_kernel(first, slots_ref, rows_ref, *out_refs):
    for k, out_ref in enumerate(out_refs):
        shape = (out_ref.shape[0], rows_ref.shape[0])
        places = lax.broadcasted_iota(jnp.int32, shape, 0) + (first + k) * out_ref.shape[0]
        hit = hits((slots_ref[0:1, :], slots_ref[1:2, :]), places)
        out_ref[...] = dot(hit, rows_ref[...]).astype(BF16)


def dispatch_blocks(slot_rows, rows, first, count, slots):
    tokens, width = rows.shape
    return pl.pallas_call(
        functools.partial(blocks_kernel, first),
        out_shape=[pltpu.HBM((slots, width), BF16)] * count,
        compiler_params=params(16),
        cost_estimate=cost(2 * count * slots * tokens * width, 4 * count * slots * width),
        name="dispatch_blocks",
    )(slot_rows, rows)


def expert_kernel(capacity, count, kept, me_ref, *refs):
    blocks, refs = refs[:count], refs[count:]
    up_ref, own_ref, router_ref, w_in_ref, b_in_ref, w_out_ref, b_out_ref, *refs = refs
    y_out, rows_out, act_out, d_hidden_out, d_y_out, b_in_sum, b_out_sum, *refs = refs[kept:]
    backs, pair = refs[:count], refs[count]
    slots, width = blocks[0].shape
    step = 2 * slots
    hidden_width = w_in_ref.shape[1]
    chunk = 512
    index = pl.program_id(0)
    odd = me_ref[0] % 2 == 1
    for i in range(count // 2):

        @pl.when(index == i)
        def load():
            both = [blocks[2 * i][...].astype(F32), blocks[2 * i + 1][...].astype(F32)]
            pair[...] = jnp.concatenate(both, 0).astype(BF16)

    rows = pair[...]
    rows_out[...] = rows
    logits = dot(rows, router_ref[...])
    gate = jnp.exp(logits - jnp.max(logits, -1, keepdims=True))
    gate = jnp.sum(gate * own_ref[...], -1, keepdims=True) / jnp.sum(gate, -1, keepdims=True)
    low, high = up_ref[0].astype(F32), up_ref[1].astype(F32)
    up_float = jnp.concatenate([jnp.where(odd, high, low), jnp.where(odd, low, high)], 0)
    d_y = (gate * up_float).astype(BF16)
    d_y_out[...] = d_y
    y = jnp.zeros((step, width), F32)
    back = jnp.zeros((step, width), F32)

    def accumulate(ref, at, value):
        ref[:, at] = jnp.where(index == 0, 0.0, ref[:, at]) + jnp.sum(
            value.astype(F32), 0, keepdims=True
        )

    for c in range(hidden_width // chunk):
        at = slice(c * chunk, (c + 1) * chunk)
        hidden = dot(rows, w_in_ref[:, at]) + b_in_ref[:, at]
        square = hidden * hidden
        root = math.sqrt(2.0 / math.pi)
        slope = jnp.tanh(hidden * (root + (root * 0.044715) * square))
        half = 0.5 * (1.0 + slope)
        act = (hidden * half).astype(BF16)
        d_gelu = half + (0.5 * hidden) * (1.0 - slope * slope) * (
            root + (3.0 * root * 0.044715) * square
        )
        d_hidden = (dot(d_y, w_out_ref[at, :], 1, 1) * d_gelu).astype(BF16)
        act_out[:, at] = act
        d_hidden_out[:, at] = d_hidden
        y += dot(act, w_out_ref[at, :])
        back += dot(d_hidden, w_in_ref[:, at], 1, 1)
        accumulate(b_in_sum, at, d_hidden)
    accumulate(b_out_sum, slice(0, width), d_y)
    y = (y + b_out_ref[...]).astype(BF16).astype(F32)
    d_weight = jnp.sum(y * up_float, -1, keepdims=True)
    y = y * gate
    y_out[0] = jnp.where(odd, y[slots:], y[:slots]).astype(BF16)
    y_out[1] = jnp.where(odd, y[:slots], y[slots:]).astype(BF16)
    row = lax.broadcasted_iota(jnp.int32, (step, width), 0)
    lane = lax.broadcasted_iota(jnp.int32, (step, width), 1)
    for s in range(2):
        line = jnp.sum(jnp.where(row - s * slots == lane, d_weight, 0.0), 0, keepdims=True)
        line = jnp.where(lane[:1] < capacity, line, 0.0)
        top = line.astype(BF16).astype(F32)
        back = jnp.where(row == s * slots + capacity, top, back)
        back = jnp.where(row == s * slots + capacity + 1, line - top, back)
    for i in range(count // 2):

        @pl.when(index == i)
        def store():
            backs[2 * i][...] = back[:slots].astype(BF16)
            backs[2 * i + 1][...] = back[slots:].astype(BF16)


def expert_group(me, blocks, first, up, own, w_router, w_in, b_in, w_out, b_out, capacity, kept):
    count = len(blocks)
    slots, width = blocks[0].shape
    sources = up.shape[0]
    total = sources * slots
    hidden_width = w_in.shape[1]
    step = 2 * slots
    begin = first // 2
    rows = lambda size: pl.BlockSpec((step, size), lambda i, me_ref: (i + begin, 0))
    sides = pl.BlockSpec((2, slots, width), lambda i, me_ref: ((me_ref[0] // 2) ^ (i + begin), 0, 0))
    anywhere = pl.BlockSpec(memory_space=pl.ANY)
    given = 1 + count + 7
    shapes = [
        pltpu.HBM((sources, slots, width), BF16),
        pltpu.HBM((total, width), BF16),
        pltpu.HBM((total, hidden_width), BF16),
        pltpu.HBM((total, hidden_width), BF16),
        pltpu.HBM((total, width), BF16),
    ]
    outs = pl.pallas_call(
        functools.partial(expert_kernel, capacity, count, len(kept)),
        grid_spec=pltpu.PrefetchScalarGridSpec(
            num_scalar_prefetch=1,
            grid=(count // 2,),
            in_specs=[whole((slots, width))] * count
            + [sides]
            + [whole(a.shape) for a in (own, w_router, w_in, b_in, w_out, b_out)]
            + [anywhere] * len(kept),
            out_specs=[sides, rows(width), rows(hidden_width), rows(hidden_width), rows(width)]
            + [whole((1, hidden_width)), whole((1, width))]
            + [whole((slots, width))] * count,
            scratch_shapes=[pltpu.VMEM((step, width), BF16)],
        ),
        out_shape=shapes
        + [jax.ShapeDtypeStruct((1, hidden_width), F32), jax.ShapeDtypeStruct((1, width), F32)]
        + [jax.ShapeDtypeStruct((slots, width), BF16)] * count,
        input_output_aliases={given + i: i for i in range(len(kept))},
        compiler_params=params(28),
        cost_estimate=cost(8 * count * slots * width * hidden_width, 8 * MIB),
        name="expert_group",
    )(me, *map(in_hbm, blocks), in_hbm(up), own, w_router, w_in, b_in, w_out, b_out, *kept)
    return outs[:5], outs[5:7], list(outs[7:])


def weight_kernel(left_ref, right_ref, out_ref, turned):
    @pl.when(pl.program_id(0) == 0)
    def turn():
        turned[...] = left_ref[...].T

    out_ref[...] = dot(turned[...], right_ref[...]).astype(BF16)


def weight_grad(left, right, part, block=512):
    total, width = left.shape
    blocks = right.shape[1] // (2 * block)
    return pl.pallas_call(
        weight_kernel,
        grid=(blocks,),
        in_specs=[
            whole(left.shape),
            pl.BlockSpec((total, block), lambda i: (0, i + part * blocks)),
        ],
        out_specs=pl.BlockSpec((width, block), lambda i: (0, i)),
        out_shape=jax.ShapeDtypeStruct((width, blocks * block), BF16),
        scratch_shapes=[pltpu.VMEM((width, total), BF16)],
        compiler_params=params(24),
        cost_estimate=cost(2 * total * width * blocks * block, 7 * MIB),
        name="weight_grad",
    )(in_hbm(left), in_hbm(right))


def sides_kernel(turned, low_ref, low_far_ref, high_ref, high_far_ref, out_ref):
    low = pl.program_id(0) < pl.num_programs(0) // 2
    own = jnp.where(low, low_ref[...], high_ref[...]).astype(F32)
    far = jnp.where(low, low_far_ref[...], high_far_ref[...]).astype(F32)
    out_ref[...] = (own + far).T if turned else own + far


def sides_sum(low, low_far, high, high_far, turned, block=512):
    width, half = low.shape
    blocks = half // block
    lows = pl.BlockSpec((width, block), lambda i: (0, jnp.minimum(i, blocks - 1)))
    highs = pl.BlockSpec((width, block), lambda i: (0, jnp.maximum(i - blocks, 0)))
    if turned:
        shape, out = (2 * half, width), pl.BlockSpec((block, width), lambda i: (i, 0))
    else:
        shape, out = (width, 2 * half), pl.BlockSpec((width, block), lambda i: (0, i))
    return pl.pallas_call(
        functools.partial(sides_kernel, turned),
        grid=(2 * blocks,),
        in_specs=[lows, lows, highs, highs],
        out_specs=out,
        out_shape=jax.ShapeDtypeStruct(shape, F32),
        compiler_params=params(20),
        cost_estimate=cost(2 * width * half, 16 * width * half),
        name="sides_sum",
    )(*map(in_hbm, (low, low_far, high, high_far)))


def combine_kernel(slots_ref, y_ref, resid_ref, out_ref, moment_ref):
    step, total = out_ref.shape[0], y_ref.shape[0]
    places = lax.broadcasted_iota(jnp.int32, (step, total), 1)
    moe = dot(hits((slots_ref[:, 0:1], slots_ref[:, 1:2]), places), y_ref[...])
    out_ref[...] = (resid_ref[...] + moe).astype(BF16)
    moment = jnp.sum(moe * moe, 0, keepdims=True)
    moment_ref[...] = jnp.where(pl.program_id(0) == 0, 0.0, moment_ref[...]) + moment


def combine_rows(slot_columns, y, resid, step):
    tokens, width = resid.shape
    total = y.shape[0]
    block = lambda size: pl.BlockSpec((step, size), lambda i: (i, 0))
    return pl.pallas_call(
        combine_kernel,
        grid=(tokens // step,),
        in_specs=[block(TOP), whole(y.shape), block(width)],
        out_specs=[block(width), whole((1, width))],
        out_shape=[
            jax.ShapeDtypeStruct((tokens, width), BF16),
            jax.ShapeDtypeStruct((1, width), F32),
        ],
        compiler_params=params(24),
        cost_estimate=cost(2 * total * tokens * width, 8 * MIB),
        name="combine_rows",
    )(slot_columns, y, in_hbm(resid))


def token_back_kernel(
    capacity,
    slots,
    experts,
    later,
    flag_ref,
    *refs,
):
    me = flag_ref[2]
    backs, refs = refs[:experts], refs[experts:]
    if later:
        unused, attn_ref, router_ref_sum, gain_ref_sum, *refs = refs
    (
        columns_ref,
        lines_ref,
        resid_ref,
        normed_ref,
        heads_ref,
        up_ref,
        w_out_ref,
        router_ref,
        gain_ref,
        d_resid_out,
        d_heads_out,
        attn_sum,
        gain_sum,
        router_out,
        d_weights,
        back_ref,
        near_router,
        router_sum,
    ) = refs
    step, width = resid_ref.shape
    total = back_ref.shape[0]
    first = pl.program_id(0) == 0

    @pl.when(first)
    def columns():
        near_router[...] = jnp.concatenate(
            [router_ref[pl.ds(e ^ me, 1), :] for e in range(experts)], 0
        ).astype(BF16)
        row = lax.broadcasted_iota(jnp.int32, (slots, 256), 0)
        lane = lax.broadcasted_iota(jnp.int32, (slots, 256), 1)
        for e in range(0, experts, 2):
            pair = [backs[e][...].astype(F32), backs[e + 1][...].astype(F32)]
            back_ref[e * slots : (e + 2) * slots, :] = jnp.concatenate(pair, 0).astype(BF16)
        for e in range(experts):
            block = backs[e][:, 0:256].astype(F32)
            line = jnp.sum(jnp.where(row >= capacity, block, 0.0), 0, keepdims=True)
            column = jnp.sum(jnp.where(row == lane, line, 0.0), -1, keepdims=True)
            d_weights[e * slots : (e + 1) * slots, :] = jnp.broadcast_to(column, (slots, step))

    def accumulate(ref, value, given_ref=None):
        given = 0.0 if given_ref is None else given_ref[...]
        ref[...] = jnp.where(first, given, ref[...]) + value

    line_slots = (lines_ref[0:1, :], lines_ref[1:2, :])
    d_gates = []
    for e in range(experts):
        places = lax.broadcasted_iota(jnp.int32, (slots, step), 0) + e * slots
        hit = (places == line_slots[0]) | (places == line_slots[1])
        d_gates.append(
            jnp.sum(
                jnp.where(hit, d_weights[e * slots : (e + 1) * slots, :], 0.0), 0, keepdims=True
            )
        )
    d_gates = jnp.concatenate(d_gates, 0)
    logits = dot(near_router[...], normed_ref[...], 1, 1)
    gates = jnp.exp(logits - jnp.max(logits, 0, keepdims=True))
    gates = gates / jnp.sum(gates, 0, keepdims=True)
    d_logits = (gates * (d_gates - jnp.sum(gates * d_gates, 0, keepdims=True))).astype(BF16)
    places = lax.broadcasted_iota(jnp.int32, (step, total), 1)
    d_normed = dot(hits((columns_ref[:, 0:1], columns_ref[:, 1:2]), places), back_ref[...])
    d_normed += dot(d_logits, near_router[...], 0, 0)
    normed, inverse = normalize(resid_ref[...])
    d_resid = up_ref[...].astype(F32) + norm_back(d_normed * gain_ref[...], normed, inverse)
    d_attn = d_resid.astype(BF16)
    d_resid_out[...] = d_resid
    d_heads_out[...] = dot(d_attn, w_out_ref[...], 1, 1).astype(BF16)
    accumulate(attn_sum, dot(heads_ref[...], d_attn, 0, 0), attn_ref if later else None)
    accumulate(router_sum, dot(d_logits, normed_ref[...]))
    gain_term = jnp.sum(d_normed * normed, 0, keepdims=True)
    accumulate(gain_sum, gain_term, gain_ref_sum if later else None)

    @pl.when(pl.program_id(0) == pl.num_programs(0) - 1)
    def finish():
        for e in range(experts):
            at = pl.ds(e ^ me, 1)
            given = router_ref_sum[at, :] if later else 0.0
            router_out[at, :] = router_sum[e : e + 1, :] + given


def token_back(
    flag,
    mine,
    kept,
    slot_columns,
    slot_rows,
    backs,
    resid,
    normed,
    heads,
    up,
    w_attn_out,
    w_router_t,
    gain,
    capacity,
    slots,
    step,
):
    tokens, width = resid.shape
    experts = w_router_t.shape[0]
    total = experts * slots
    part = tokens // step // 2
    image = lambda i, flag_ref: i + (flag_ref[0] if mine else 1 - flag_ref[0]) * part
    block = lambda size: pl.BlockSpec((step, size), lambda i, flag_ref: (image(i, flag_ref), 0))
    sums = [(width, width), (1, width), (experts, width)]
    given = [kept[0], kept[2], kept[4], kept[3]] if kept else []
    return pl.pallas_call(
        functools.partial(token_back_kernel, capacity, slots, experts, bool(kept)),
        grid_spec=pltpu.PrefetchScalarGridSpec(
            num_scalar_prefetch=1,
            grid=(part,),
            in_specs=[whole((slots, width))] * experts
            + [pl.BlockSpec(memory_space=pl.ANY)] * (len(given) > 0)
            + [whole(value.shape) for value in given[1:]]
            + [
                block(TOP),
                pl.BlockSpec((TOP, step), lambda i, flag_ref: (0, image(i, flag_ref))),
                block(width),
                block(width),
                block(width),
                block(width),
                whole(w_attn_out.shape),
                whole(w_router_t.shape),
                whole(gain.shape),
            ],
            out_specs=[block(width), pl.BlockSpec((step, width), lambda i, flag_ref: (i, 0))]
            + [whole(shape) for shape in sums],
            scratch_shapes=[
                pltpu.VMEM((total, step), F32),
                pltpu.VMEM((total, width), BF16),
                pltpu.VMEM((experts, width), BF16),
                pltpu.VMEM((experts, width), F32),
            ],
        ),
        out_shape=[
            pltpu.HBM((tokens, width), F32),
            pltpu.HBM((part * step, width), BF16),
            pltpu.HBM((width, width), F32),
            jax.ShapeDtypeStruct((1, width), F32),
            jax.ShapeDtypeStruct((experts, width), F32),
        ],
        input_output_aliases={1 + experts: 0} if kept else {},
        compiler_params=params(30),
        cost_estimate=cost((total + 2 * width) * tokens * width, 7 * MIB),
        name="token_back",
    )(
        flag,
        *map(in_hbm, backs),
        *given,
        slot_columns,
        slot_rows,
        in_hbm(resid),
        in_hbm(normed),
        in_hbm(heads),
        in_hbm(up),
        w_attn_out,
        w_router_t,
        gain,
    )


def grad_sum_kernel(flag_ref, resid_ref, own_ref, far_ref, out_ref):
    mine = (flag_ref[0] == 0) == (pl.program_id(0) < pl.num_programs(0) // 2)
    out_ref[...] = resid_ref[...] + jnp.where(mine, own_ref[0], far_ref[0]).astype(F32)


def grad_sum(flag, d_resid, own, far):
    part, rows, width = own.shape
    tokens = d_resid.shape[0]
    pick = pl.BlockSpec((1, rows, width), lambda i, flag_ref: (lax.rem(i, part), 0, 0))
    return pl.pallas_call(
        grad_sum_kernel,
        grid_spec=pltpu.PrefetchScalarGridSpec(
            num_scalar_prefetch=1,
            grid=(tokens // rows,),
            in_specs=[pl.BlockSpec((rows, width), lambda i, flag_ref: (i, 0)), pick, pick],
            out_specs=pl.BlockSpec((rows, width), lambda i, flag_ref: (i, 0)),
        ),
        out_shape=jax.ShapeDtypeStruct((tokens, width), F32),
        compiler_params=params(16),
        cost_estimate=cost(tokens * width, 6 * MIB),
        name="grad_sum",
    )(flag, in_hbm(d_resid), own, far)


AXES = ("wide", "narrow")


def device_bits():
    n_narrow = lax.axis_size("narrow")
    masks = [1 << b for b in range((n_narrow * lax.axis_size("wide")).bit_length() - 1)]
    masks.remove(n_narrow)
    return [n_narrow] + masks


def sum_steps():
    first, *rest = device_bits()
    return [(first,)] + [tuple(rest[i : i + 2]) for i in range(0, len(rest), 2)]


def swap(value, mask, axes=AXES):
    size = math.prod(lax.axis_size(axis) for axis in axes)
    return lax.ppermute(value, axes, [(i, i ^ mask) for i in range(size)])


def partners(bits):
    me = lax.axis_index(AXES)
    place = sum(((me // bit) % 2) << b for b, bit in enumerate(bits))
    masks = [
        sum(bit for b, bit in enumerate(bits) if (j >> b) & 1) for j in range(1 << len(bits))
    ]
    return masks, place


def fold_kernel(given, members, place_ref, keep_ref, *refs):
    del place_ref
    step = pl.program_id(0)
    total = keep_ref[...]
    for far_ref in refs[:given]:
        total += far_ref[...].astype(F32)
    own_out, *send_outs = refs[given:]

    @pl.when(step == 0)
    def keep():
        own_out[...] = total

    for j, send_out in enumerate(send_outs):

        @pl.when(step == j + 1)
        def send():
            send_out[...] = total.astype(BF16)


def fold(keep, far, bits):
    masks, place = partners(bits)
    members = len(masks)
    rows, size = keep.shape
    part = rows // members
    pick = pl.BlockSpec((part, size), lambda j, place_ref: (place_ref[0] ^ j, 0))
    own, *send = pl.pallas_call(
        functools.partial(fold_kernel, len(far), members),
        grid_spec=pltpu.PrefetchScalarGridSpec(
            num_scalar_prefetch=1,
            grid=(members,),
            in_specs=[pick] * (1 + len(far)),
            out_specs=[whole((part, size))] * members,
        ),
        out_shape=[jax.ShapeDtypeStruct((part, size), F32)]
        + [jax.ShapeDtypeStruct((part, size), BF16)] * (members - 1),
        compiler_params=params(32),
        cost_estimate=cost(0, 8 * rows * size),
        name="fold",
    )(place.reshape(1).astype(jnp.int32), in_hbm(keep), *far)
    return own, [swap(value, mask) for value, mask in zip(send, masks[1:])]


def sum_parts(value, bits):
    masks, place = partners(bits)
    part = value.shape[0] // len(masks)
    pick = lambda j: lax.dynamic_slice_in_dim(value, (place ^ j) * part, part, 0)
    far = [swap(pick(j).astype(BF16), masks[j]) for j in range(1, len(masks))]
    total = pick(0)
    for term in far:
        total = total + term.astype(F32)
    return total


def spread_parts(value, bits):
    masks, place = partners(bits)
    parts = [value] + [swap(value, mask) for mask in masks[1:]]
    for b in range(len(bits)):
        side = (place >> b) % 2 == 0
        parts = [
            jnp.where(
                side,
                jnp.concatenate([parts[i], parts[i + 1]], 0),
                jnp.concatenate([parts[i + 1], parts[i]], 0),
            )
            for i in range(0, len(parts), 2)
        ]
    return parts[0]


def close_kernel(keep_ref, moment_ref, *refs):
    total = keep_ref[...]
    for far_ref in refs[:-1]:
        total += far_ref[...].astype(F32)
    row = lax.broadcasted_iota(jnp.int32, total.shape, 0)
    lane = lax.broadcasted_iota(jnp.int32, total.shape, 1) - (total.shape[1] - 2)
    moment = jnp.sum(moment_ref[...], 1, keepdims=True)
    high = moment.astype(BF16).astype(F32)
    extra = jnp.where(lane == 0, high, moment - high)
    refs[-1][...] = jnp.where((row == 0) & (lane >= 0), extra, total).astype(BF16)


def close(keep, far, moment):
    return pl.pallas_call(
        close_kernel,
        out_shape=jax.ShapeDtypeStruct(keep.shape, BF16),
        compiler_params=params(16),
        cost_estimate=cost(0, 8 * keep.size),
        name="close",
    )(keep, moment, *far)


def add_kernel(*refs):
    terms = [ref[...].astype(F32) for ref in refs[:-1]]
    while len(terms) > 1:
        terms = [terms[i] + terms[i + 1] for i in range(0, len(terms), 2)]
    refs[-1][...] = terms[0].astype(BF16)


def add(terms):
    return pl.pallas_call(
        add_kernel,
        out_shape=jax.ShapeDtypeStruct(terms[0].shape, BF16),
        compiler_params=params(16),
        cost_estimate=cost(0, 2 * len(terms) * terms[0].size),
        name="add",
    )(*terms)


def apart_kernel(experts, count, flag_ref, own_ref, far_ref, qkv_out, attn_out, router_out, *outs):
    gain_one_out, gain_two_out, stats_out, small = outs
    half, width = own_ref.shape[0], attn_out.shape[1]
    upper = flag_ref[1] == 1
    own, far = own_ref[...].astype(F32), far_ref[...].astype(F32)
    for rows, value in ((0, jnp.where(upper, far, own)), (half, jnp.where(upper, own, far))):
        rows = slice(rows, rows + half)
        qkv_out[rows, :] = value[:, : 3 * width]
        attn_out[rows, :] = value[:, 3 * width : 4 * width]
        small[rows, :] = value[:, 4 * width :]
    values = small[...]
    router_out[...] = values[:, :experts]
    lines = values.T
    gain_two_out[...] = lines[experts : experts + 1, :]
    gain_one_out[...] = lines[experts + 3 : experts + 4, :]
    sums = jnp.sum(lines, 1, keepdims=True)
    moments = (
        sums[experts + 1 : experts + 2],
        sums[experts + 2 : experts + 3],
        sums[SMALL - 2 : SMALL - 1] + sums[SMALL - 1 :],
    )
    lane = lax.broadcasted_iota(jnp.int32, stats_out.shape, 1)
    stats = jnp.where(lane == 0, moments[0], jnp.where(lane == 1, moments[1], moments[2]))
    stats_out[...] = jnp.sqrt(stats / count + EPS)


def sums_apart(flag, own, far, experts, count):
    width = 2 * own.shape[0]
    shapes = [(width, 3 * width), (width, width), (width, experts), (1, width), (1, width), (1, 128)]
    return pl.pallas_call(
        functools.partial(apart_kernel, experts, count),
        grid_spec=pltpu.PrefetchScalarGridSpec(
            num_scalar_prefetch=1,
            grid=(1,),
            in_specs=[whole(own.shape), whole(far.shape)],
            out_specs=[whole(shape) for shape in shapes],
            scratch_shapes=[pltpu.VMEM((width, SMALL), F32)],
        ),
        out_shape=[jax.ShapeDtypeStruct(shape, F32) for shape in shapes],
        compiler_params=params(32),
        cost_estimate=cost(0, 8 * MIB),
        name="sums_apart",
    )(flag, own, far)


def gathered_attention(inputs, gain_one, w_qkv):
    images, rows_dev, width = inputs.shape
    tokens = images * rows_dev
    head_dim = width // HEADS
    scale = head_dim ** (-0.5)
    seq_len = rows_dev * lax.axis_size("narrow")
    group = math.gcd(images, max(1, 512 // rows_dev))
    blocks = images // group
    normed_one, inverse_one = normalize(inputs.astype(F32).reshape(tokens, width))
    input_one = (normed_one * gain_one).astype(BF16)
    projected = jnp.dot(input_one, w_qkv, preferred_element_type=F32).astype(BF16)
    queries = projected[:, :width].reshape(images, rows_dev, width)
    keys_own = projected[:, width : 2 * width].reshape(images, rows_dev, width)
    values_own = projected[:, 2 * width :].reshape(images, rows_dev, width)
    keys_all = lax.all_gather(keys_own, "narrow", axis=1, tiled=True)
    values_all = lax.all_gather(values_own, "narrow", axis=1, tiled=True)
    query_blocks = queries.reshape(blocks, group, rows_dev, HEADS, head_dim)
    key_blocks = keys_all.reshape(blocks, group, seq_len, HEADS, head_dim)
    value_blocks = values_all.reshape(blocks, group, seq_len, HEADS, head_dim)

    def attend_block(operands):
        query_b, key_b, value_b = operands
        scores = jnp.einsum("gqhd,gkhd->ghqk", query_b, key_b, preferred_element_type=F32) * scale
        top_score = jnp.max(scores, -1, keepdims=True)
        exponent = jnp.exp(scores - top_score)
        total = jnp.sum(exponent, -1, keepdims=True)
        weights = (exponent / total).astype(BF16)
        mixed = jnp.einsum("ghqk,gkhd->gqhd", weights, value_b, preferred_element_type=F32)
        return (mixed.astype(BF16), (top_score + jnp.log(total))[..., 0])

    heads_out, log_total = lax.map(attend_block, (query_blocks, key_blocks, value_blocks))

    def back_block(operands):
        query_b, key_b, value_b, total_b, d_head_b = operands
        scores = jnp.einsum("gqhd,gkhd->ghqk", query_b, key_b, preferred_element_type=F32) * scale
        weights = jnp.exp(scores - total_b[..., None])
        d_weights = jnp.einsum("gqhd,gkhd->ghqk", d_head_b, value_b, preferred_element_type=F32)
        spread = jnp.sum(weights * d_weights, -1, keepdims=True)
        d_scores = (weights * (d_weights - spread)).astype(BF16)
        d_query = jnp.einsum("ghqk,gkhd->gqhd", d_scores, key_b, preferred_element_type=F32) * scale
        d_key = jnp.einsum("ghqk,gqhd->gkhd", d_scores, query_b, preferred_element_type=F32) * scale
        d_value = jnp.einsum(
            "ghqk,gqhd->gkhd", weights.astype(BF16), d_head_b, preferred_element_type=F32
        )
        return (d_query.astype(BF16), d_key, d_value)

    def back(d_heads, d_resid):
        d_head_blocks = d_heads.reshape(blocks, group, rows_dev, HEADS, head_dim)
        d_queries, key_terms, value_terms = lax.map(
            back_block, (query_blocks, key_blocks, value_blocks, log_total, d_head_blocks)
        )
        d_keys, d_values = (
            lax.psum_scatter(
                terms.reshape(images, seq_len, width), "narrow", scatter_dimension=1, tiled=True
            )
            .astype(BF16)
            .reshape(tokens, width)
            for terms in (key_terms, value_terms)
        )
        d_projected = jnp.concatenate([d_queries.reshape(tokens, width), d_keys, d_values], 1)
        d_weight = jnp.dot(input_one.T, d_projected, preferred_element_type=F32)
        d_input = jnp.dot(d_projected, w_qkv.T, preferred_element_type=F32)
        d_gain = jnp.sum(d_input * normed_one, 0, keepdims=True)
        return (
            d_resid + norm_back(d_input * gain_one, normed_one, inverse_one),
            d_weight,
            d_gain,
        )

    return heads_out.reshape(images, rows_dev, width), back


def shards(
    inputs,
    cotangent,
    ln1_gain,
    w_qkv,
    w_attn_out,
    ln2_gain,
    w_router,
    expert_in,
    expert_in_bias,
    expert_out,
    expert_out_bias,
    route_ids,
    route_slots,
    route_dropped,
):
    images, rows_dev, width = inputs.shape
    tokens = images * rows_dev
    experts = w_router.shape[1]
    n_wide = lax.axis_size("wide")
    n_narrow = lax.axis_size("narrow")
    capacity = max(2, 42 * tokens // (20 * experts))
    slots = -(-(capacity + 2) // 8) * 8
    total = experts * slots
    gain_one = ln1_gain.astype(F32).reshape(1, width)
    gain_two = ln2_gain.astype(F32).reshape(1, width)
    paired = n_narrow == 2 and images % 2 == 0
    part = images // 2
    place = lax.axis_index("narrow") if paired else jnp.int32(0)
    me = lax.axis_index("wide")
    flag = jnp.stack([place, me % 2, me])

    slot_columns = jnp.where(
        route_dropped == 0, route_ids * slots + route_slots, -1
    ).reshape(tokens, TOP)
    slot_rows = slot_columns.T
    near_columns = jnp.where(
        route_dropped == 0, (route_ids ^ me) * slots + route_slots, -1
    ).reshape(tokens, TOP)
    near_rows = near_columns.T
    up = cotangent.reshape(tokens, width)

    def exchange(rows):
        return lax.all_to_all(
            rows.reshape(experts, slots, width), "wide", split_axis=0, concat_axis=0, tiled=True
        ).reshape(total, width)

    up_rows = dispatch_rows(slot_rows, up, total)
    if paired:
        pick = lambda k: lax.dynamic_slice_in_dim(inputs, (1 - place) * part + k, 1, 0)
        far_inputs = [swap(pick(0), 1)]
        far_inputs[0], up_rows = lax.optimization_barrier((far_inputs[0], up_rows))
        far_inputs += [swap(pick(k), 1) for k in range(1, part)]
    up_here = exchange(up_rows)

    if paired:
        w_qkv_t = w_qkv.T
        heads_own, heads_far, saved = [], [], []
        for k, far in enumerate(far_inputs):
            own_heads, far_heads, *saved = attend(
                flag, inputs, k, far, gain_one, w_qkv_t, saved
            )
            heads_own.append(own_heads)
            heads_far.append(swap(far_heads, 1))
        proj, log_total = saved
    else:
        heads_own, attention_back = gathered_attention(inputs, gain_one, w_qkv)
        heads_own = [heads_own[k : k + 1] for k in range(images)]
        heads_own, heads_far = heads_own[:part], heads_own[part:]

    heads, resid, normed_two, moments = residual_rows(
        flag, heads_own, heads_far, inputs, w_attn_out, gain_two
    )
    w_in, w_out = expert_in[0], expert_out[0]
    up_here = up_here.reshape(experts, slots, width)
    own = (jnp.arange(experts) == me).astype(F32).reshape(1, experts)

    def expert(blocks, first, kept):
        return expert_group(
            me.reshape(1),
            blocks,
            first,
            up_here,
            own,
            w_router,
            w_in,
            expert_in_bias.astype(F32),
            w_out,
            expert_out_bias.astype(F32),
            capacity,
            kept,
        )

    def after(value, *others):
        return lax.optimization_barrier((value,) + others)[0]

    half = experts // 2
    quarter = half // 2
    send = lambda block, k: swap(block, k, ("wide",)) if k else block
    blocks = dispatch_blocks(near_rows, normed_two, half, half, slots)
    cross = [send(block, half + k) for k, block in enumerate(blocks[:2])]
    local = []
    for k, block in enumerate(
        dispatch_blocks(near_rows, after(normed_two, blocks[0]), 0, half, slots)
    ):
        local.append(send(after(block, local[k - 3]) if k > 3 else block, k))
    kept, sums_a, backs_a = expert(local, 0, [])
    for k in range(2, half):
        gate = local[k + half - EARLY] if k < EARLY else sums_a[1]
        cross.append(send(after(blocks[k], gate), half + k))
    backs_a = [send(block, k) for k, block in enumerate(backs_a)]
    kept, sums_b, backs_b = expert(cross[:quarter], half, kept)
    backs_b = [send(block, half + k) for k, block in enumerate(backs_b)]
    last = cross[quarter:]
    last[0] = after(last[0], *backs_a[1:6])
    kept, sums_c, backs_c = expert(last, half + quarter, kept)
    backs_c = [send(block, half + quarter + k) for k, block in enumerate(backs_c)]
    y, rows_here, act, d_hidden, d_y = kept
    y = y.reshape(total, width)
    grad_out = [weight_grad(after(d_y, *backs_b[:2], *backs_a[6:]), act, 0)]
    grad_out.append(weight_grad(after(d_y, grad_out[0], *backs_b[2:]), act, 1))
    grad_in = [weight_grad(after(rows_here, grad_out[1], *backs_c[:2]), d_hidden, 0)]
    grad_in.append(weight_grad(after(rows_here, grad_in[0]), d_hidden, 1))
    b_in_sum, b_out_sum = (sum(terms) for terms in zip(sums_a, sums_b, sums_c))
    backs = backs_a + backs_b + backs_c
    backs[-1] = after(backs[-1], *grad_in)
    if n_narrow == 2:
        far_out = [swap(part_grad, 1) for part_grad in grad_out]

    def back_to_tokens(mine, kept):
        return token_back(
            flag,
            mine,
            kept,
            near_columns,
            near_rows,
            backs,
            resid,
            normed_two,
            heads,
            up,
            w_attn_out,
            w_router.T.astype(F32),
            gain_two,
            capacity,
            slots,
            rows_dev,
        )

    first = back_to_tokens(False, [])
    sent = first[1]
    d_resid, d_heads, attn_term, gain_two_term, router_term = back_to_tokens(True, first)
    sent, grad_in[0] = lax.optimization_barrier((sent, grad_in[0]))
    biases = jnp.concatenate([b_in_sum, b_out_sum], 1)
    small = jnp.concatenate([router_term, gain_two_term, moments], 0)
    count = tokens * width * n_wide * n_narrow
    steps = sum_steps()
    if paired:
        d_far = swap(sent.reshape(part, rows_dev, width), 1)
        far_in = [swap(grad_in[0], 1)]
        far_biases = swap(biases, 1)
        y = exchange(after(y, sent))
        d_far, *far_out = lax.optimization_barrier((d_far, *far_out))
        d_own, d_far, keep, send = attend_back(
            flag,
            inputs,
            jnp.concatenate(far_inputs, 0),
            gain_one,
            w_qkv_t,
            proj,
            log_total,
            d_heads.reshape(part, rows_dev, width),
            d_far,
            attn_term,
            small,
        )
        keep, send, far_in[0] = lax.optimization_barrier((keep, send, far_in[0]))
        sums, far = fold(keep, [swap(send, steps[0][0])], steps[1])
        block_out, moe_moment = combine_rows(slot_columns, after(y, sums), resid, rows_dev)
        far[0], moe_moment, far_biases, grad_in[1] = lax.optimization_barrier(
            (far[0], moe_moment, far_biases, grad_in[1])
        )
        biases = biases + far_biases
        bias_outs = (biases[:, : w_in.shape[1]], biases[:, w_in.shape[1] :])
        sums = close(sums, far, moe_moment)
        far_in.append(swap(after(grad_in[1], sums), 1))
        d_far = swap(after(d_far, sums), 1)
        for bits in steps[2:]:
            masks, unused = partners(bits)
            terms = [sums] + [swap(sums, mask) for mask in masks[1:]]
            grad_expert_out = sides_sum(
                grad_out[0], far_out[0], grad_out[1], after(far_out[1], sums), True
            )
            terms[1], grad_expert_out, *bias_outs = lax.optimization_barrier(
                (terms[1], grad_expert_out, *bias_outs)
            )
            sums = add(terms)
        sums, d_far, far_in[1] = lax.optimization_barrier((sums, d_far, far_in[1]))
        input_grad = grad_sum(flag, d_resid, d_own, d_far)
        grad_expert_in = sides_sum(grad_in[0], far_in[0], grad_in[1], far_in[1], False)
        sums = spread_parts(sums, steps[1])
        sums, input_grad, grad_expert_in = lax.optimization_barrier(
            (sums, input_grad, grad_expert_in)
        )
    else:
        y = exchange(y)
        grad_out, grad_in = lax.psum((grad_out, grad_in), "narrow")
        grad_expert_out = jnp.concatenate(grad_out, 1).astype(F32).T
        grad_expert_in = jnp.concatenate(grad_in, 1).astype(F32)
        biases = lax.psum(biases, "narrow")
        bias_outs = (biases[:, : w_in.shape[1]], biases[:, w_in.shape[1] :])
        d_heads = jnp.concatenate([d_heads, sent], 0)
        input_grad, qkv_term, gain_one_term = attention_back(d_heads, d_resid)
        small = small_columns(small, gain_one_term)
        sums = jnp.concatenate([qkv_term, attn_term, small], 1)
        for bits in steps:
            sums = sum_parts(sums, bits)
        block_out, moe_moment = combine_rows(slot_columns, y, resid, rows_dev)
        sums = close(sums, [], moe_moment)
        for bits in reversed(steps[1:]):
            sums = spread_parts(sums, bits)
    grad_qkv, grad_attn_out, grad_router, grad_gain_one, grad_gain_two, stats = sums_apart(
        flag, sums, swap(sums, steps[0][0]), experts, count
    )
    return (
        block_out.reshape(images, rows_dev, width),
        input_grad.reshape(images, rows_dev, width),
        grad_gain_one.reshape(width),
        grad_qkv,
        grad_attn_out,
        grad_gain_two.reshape(width),
        grad_router,
        grad_expert_in[None],
        bias_outs[0],
        grad_expert_out[None],
        bias_outs[1],
        stats[0, :3],
    )


def solution(mesh):
    return jax.shard_map(
        shards,
        mesh=mesh,
        in_specs=(
            P("wide", "narrow", None),
            P("wide", "narrow", None),
            P(),
            P(),
            P(),
            P(),
            P(),
            P("wide", None, None),
            P("wide", None),
            P("wide", None, None),
            P("wide", None),
            P("wide", "narrow", None),
            P("wide", "narrow", None),
            P("wide", "narrow", None),
        ),
        out_specs=(
            P("wide", "narrow", None),
            P("wide", "narrow", None),
            P(),
            P(),
            P(),
            P(),
            P(),
            P("wide", None, None),
            P("wide", None),
            P("wide", None, None),
            P("wide", None),
            P(),
        ),
        check_vma=False,
    )
```

```python
import functools
import math

import jax
import jax.numpy as jnp
from jax import lax
from jax.experimental import pallas as pl
from jax.experimental.pallas import tpu as pltpu
from jax.sharding import PartitionSpec as P

HEADS = 8
TOP = 2


EPS = 1e-06
BF16 = jnp.bfloat16
F32 = jnp.float32
MIB = 1 << 20
SMALL = 128
EARLY = 5
MIDDLE = 2
LATE = 3


def normalize(values):
    centre = jnp.mean(values, -1, keepdims=True)
    shifted = values - centre
    inverse = lax.rsqrt(jnp.mean(shifted * shifted, -1, keepdims=True) + EPS)
    return (shifted * inverse, inverse)


def norm_back(d_normed, normed, inverse):
    return inverse * (
        d_normed
        - jnp.mean(d_normed, -1, keepdims=True)
        - normed * jnp.mean(d_normed * normed, -1, keepdims=True)
    )


def dot(left, right, left_dim=1, right_dim=0):
    return lax.dot_general(
        left, right, (((left_dim,), (right_dim,)), ((), ())), preferred_element_type=F32
    )


def params(mib):
    return pltpu.CompilerParams(vmem_limit_bytes=mib * MIB)


def in_hbm(value):
    return pltpu.with_memory_space_constraint(value, pltpu.HBM)


def in_vmem(value):
    return pltpu.with_memory_space_constraint(value, pltpu.VMEM)


def cost(flops, bytes_accessed, transcendentals=0):
    return pl.CostEstimate(
        flops=int(flops), bytes_accessed=int(bytes_accessed), transcendentals=int(transcendentals)
    )


def whole(shape):
    return pl.BlockSpec(shape, lambda *unused: (0,) * len(shape))


def hits(slots, places):
    first, second = slots
    return jnp.where((places == first) | (places == second), 1.0, 0.0).astype(BF16)


def put_rows(slots_ref, rows_ref, out_ref):
    step = out_ref.shape[0]
    places = lax.broadcasted_iota(jnp.int32, (step, rows_ref.shape[0]), 0) + pl.program_id(0) * step
    out_ref[...] = dot(hits((slots_ref[0:1, :], slots_ref[1:2, :]), places), rows_ref[...]).astype(
        BF16
    )


def dispatch_rows(slot_rows, rows, total, steps=8):
    tokens, width = rows.shape
    step = total // steps
    return pl.pallas_call(
        put_rows,
        grid=(steps,),
        in_specs=[whole(slot_rows.shape), whole(rows.shape)],
        out_specs=pl.BlockSpec((step, width), lambda i: (i, 0)),
        out_shape=jax.ShapeDtypeStruct((total, width), BF16),
        compiler_params=params(20),
        cost_estimate=cost(2 * total * tokens * width, 4 * total * width),
        name="dispatch_rows",
    )(slot_rows, rows)


def attend_kernel(flag_ref, own_ref, far_ref, gain_ref, wt_ref, *refs):
    del flag_ref
    own_out, far_out, proj_ref, total_ref, mixed = refs[-5:]
    rows, width = own_ref.shape[1], own_ref.shape[2]
    head_dim = width // HEADS
    scale = head_dim ** (-0.5)
    x_float = jnp.concatenate([own_ref[0], far_ref[0]], 0).astype(F32)
    normed, unused = normalize(x_float)
    normed = (normed * gain_ref[...]).astype(BF16)
    proj_ref[0] = dot(wt_ref[...], normed, 1, 1).astype(BF16)

    def head(h, carry):
        at = pl.multiple_of(h * head_dim, head_dim)
        query = proj_ref[0, pl.ds(at, head_dim), :]
        key = proj_ref[0, pl.ds(at + width, head_dim), :]
        value = proj_ref[0, pl.ds(at + 2 * width, head_dim), :]
        scores = dot(key, query * scale, 0, 0)
        top = jnp.max(scores, 0, keepdims=True)
        exponent = jnp.exp(scores - top)
        total = jnp.sum(exponent, 0, keepdims=True)
        out = dot(value, exponent.astype(BF16)) * (1.0 / total)
        mixed[pl.ds(at, head_dim), :] = out
        total_ref[0, pl.ds(h, 1), :] = top + jnp.log(total)
        return carry

    lax.fori_loop(0, HEADS, head, 0, unroll=4)
    heads_out = mixed[...].T.astype(BF16)
    own_out[0] = heads_out[:rows]
    far_out[0] = heads_out[rows:]


def attend(flag, inputs, image, far, gain, w_qkv_t, kept):
    unused, rows, width = far.shape
    seq_len = 2 * rows
    part = inputs.shape[0] // 2
    block = lambda k, *shape: pl.BlockSpec((1,) + shape, lambda i, flag_ref: (k,) + (0,) * len(shape))
    return pl.pallas_call(
        attend_kernel,
        grid_spec=pltpu.PrefetchScalarGridSpec(
            num_scalar_prefetch=1,
            grid=(1,),
            in_specs=[
                pl.BlockSpec(
                    (1, rows, width), lambda i, flag_ref: (image + flag_ref[0] * part, 0, 0)
                ),
                block(0, rows, width),
                whole(gain.shape),
                whole(w_qkv_t.shape),
            ]
            + [pl.BlockSpec(memory_space=pl.ANY)] * len(kept),
            out_specs=[
                block(0, rows, width),
                block(0, rows, width),
                block(image, 3 * width, seq_len),
                block(image, HEADS, seq_len),
            ],
            scratch_shapes=[pltpu.VMEM((width, seq_len), F32)],
        ),
        out_shape=[
            jax.ShapeDtypeStruct((1, rows, width), BF16),
            jax.ShapeDtypeStruct((1, rows, width), BF16),
            pltpu.HBM((part, 3 * width, seq_len), BF16),
            pltpu.HBM((part, HEADS, seq_len), F32),
        ],
        input_output_aliases={5 + i: 2 + i for i in range(len(kept))},
        compiler_params=params(28),
        cost_estimate=cost(8e9, 8 * MIB, HEADS * seq_len**2),
        name="attend",
    )(flag, in_hbm(inputs), far, gain, w_qkv_t, *kept)


def small_columns(small, gain):
    rest = jnp.zeros((SMALL - small.shape[0] - 1, small.shape[1]), F32)
    return jnp.concatenate([small, gain, rest], 0).T


def attend_back_kernel(
    part,
    flag_ref,
    own_ref,
    *refs,
):
    far_refs, refs = refs[:part], refs[part:]
    attend_back_body(flag_ref, own_ref, far_refs, *refs)


def attend_back_body(
    flag_ref,
    own_ref,
    far_refs,
    gain_ref,
    wt_ref,
    proj_ref,
    total_ref,
    d_own_ref,
    d_far_ref,
    attn_ref,
    small_ref,
    own_out,
    far_out,
    keep_out,
    send_out,
    d_proj,
    d_mixed,
    weight_sum,
    gain_out,
):
    image, last = pl.program_id(0), pl.num_programs(0) - 1
    rows, width = own_ref.shape[1], own_ref.shape[2]
    head_dim = width // HEADS
    scale = head_dim ** (-0.5)
    d_mixed[...] = jnp.concatenate([d_own_ref[0], d_far_ref[0]], 0).astype(F32).T.astype(BF16)

    def head(h, carry):
        at = pl.multiple_of(h * head_dim, head_dim)
        query = proj_ref[0, pl.ds(at, head_dim), :]
        key = proj_ref[0, pl.ds(at + width, head_dim), :]
        value = proj_ref[0, pl.ds(at + 2 * width, head_dim), :]
        d_out = d_mixed[pl.ds(at, head_dim), :]
        weights = jnp.exp(dot(key, query * scale, 0, 0) - total_ref[0, pl.ds(h, 1), :])
        product = weights * dot(value, d_out, 0, 0)
        spread = jnp.sum(product, 0, keepdims=True)
        d_scores = (product - weights * spread).astype(BF16)
        d_proj[pl.ds(at, head_dim), :] = (dot(key, d_scores) * scale).astype(BF16)
        d_proj[pl.ds(at + width, head_dim), :] = (dot(query, d_scores, 1, 1) * scale).astype(BF16)
        d_proj[pl.ds(at + 2 * width, head_dim), :] = dot(d_out, weights.astype(BF16), 1, 1).astype(
            BF16
        )
        return carry

    lax.fori_loop(0, HEADS, head, 0, unroll=4)
    far = far_refs[0][0]
    for k, far_ref in enumerate(far_refs[1:]):
        far = jnp.where(image == k + 1, far_ref[0], far)
    x_float = jnp.concatenate([own_ref[0], far], 0).astype(F32)
    normed, inverse = normalize(x_float)
    d_input = dot(d_proj[...], wt_ref[...], 0, 0)
    weight_term = dot((normed * gain_ref[...]).T.astype(BF16), d_proj[...], 1, 1)
    gain_term = jnp.sum(d_input * normed, 0, keepdims=True)
    d_x = norm_back(d_input * gain_ref[...], normed, inverse).astype(BF16)
    own_out[0] = d_x[:rows]
    far_out[0] = d_x[rows:]

    @pl.when(image == 0)
    def start():
        weight_sum[...] = weight_term
        gain_out[...] = gain_term

    @pl.when(image != 0)
    def add():
        weight_sum[...] += weight_term
        gain_out[...] += gain_term

    @pl.when(image == last)
    def finish():
        half = width // 2
        parts = ((weight_sum[...], 0), (attn_ref[...], 3 * width))
        parts += ((small_columns(small_ref[...], gain_out[...]), 4 * width),)
        upper = flag_ref[1] == 1
        for value, at in parts:
            at = slice(at, at + value.shape[1])
            keep_out[:, at] = jnp.where(upper, value[half:], value[:half])
            send_out[:, at] = jnp.where(upper, value[:half], value[half:]).astype(BF16)


def attend_back(flag, inputs, far, gain, w_qkv_t, proj, total, d_heads, d_far, attn_term, small):
    part = len(far)
    unused, rows, width = far[0].shape
    seq_len = 2 * rows
    block = lambda *shape: pl.BlockSpec((1,) + shape, lambda i, flag_ref: (i,) + (0,) * len(shape))
    return pl.pallas_call(
        functools.partial(attend_back_kernel, part),
        grid_spec=pltpu.PrefetchScalarGridSpec(
            num_scalar_prefetch=1,
            grid=(part,),
            in_specs=[
                pl.BlockSpec((1, rows, width), lambda i, flag_ref: (i + flag_ref[0] * part, 0, 0)),
            ]
            + [whole((1, rows, width))] * part
            + [
                whole(gain.shape),
                whole(w_qkv_t.shape),
                block(3 * width, seq_len),
                block(HEADS, seq_len),
                block(rows, width),
                block(rows, width),
                whole(attn_term.shape),
                whole(small.shape),
            ],
            out_specs=[
                block(rows, width),
                block(rows, width),
                whole((width // 2, 4 * width + SMALL)),
                whole((width // 2, 4 * width + SMALL)),
            ],
            scratch_shapes=[
                pltpu.VMEM((3 * width, seq_len), BF16),
                pltpu.VMEM((width, seq_len), BF16),
                pltpu.VMEM((width, 3 * width), F32),
                pltpu.VMEM((1, width), F32),
            ],
        ),
        out_shape=[
            pltpu.HBM((part, rows, width), BF16),
            pltpu.HBM((part, rows, width), BF16),
            pltpu.HBM((width // 2, 4 * width + SMALL), F32),
            jax.ShapeDtypeStruct((width // 2, 4 * width + SMALL), BF16),
        ],
        compiler_params=params(36),
        cost_estimate=cost(part * 16e9, 12 * MIB, part * HEADS * seq_len**2),
        name="attend_back",
    )(
        flag,
        in_hbm(inputs),
        *map(in_hbm, far),
        gain,
        in_hbm(w_qkv_t),
        in_hbm(proj),
        total,
        in_hbm(d_heads),
        d_far,
        in_hbm(attn_term),
        small,
    )


def pick_image(flag_ref, image, images, own_refs, far_refs):
    part = images // 2
    mine = (flag_ref[0] == 0) == (image < part)
    value = jnp.where(mine, own_refs[0][0], far_refs[0][0])
    for k in range(1, part):
        other = jnp.where(mine, own_refs[k][0], far_refs[k][0])
        value = jnp.where(lax.rem(image, part) == k, other, value)
    return value


def residual_kernel(images, flag_ref, *refs):
    own_refs, far_refs, refs = refs[: images // 2], refs[images // 2 : images], refs[images:]
    x_ref, w_out_ref, gain_ref, heads_out, resid_out, normed_out, moments_out = refs
    image = pl.program_id(0)
    heads = pick_image(flag_ref, image, images, own_refs, far_refs)
    attn = dot(heads, w_out_ref[...])
    resid = x_ref[0].astype(F32) + attn
    normed, unused = normalize(resid)
    heads_out[...] = heads
    resid_out[...] = resid
    normed_out[...] = (normed * gain_ref[...]).astype(BF16)
    moments = [jnp.sum(value * value, 0, keepdims=True) for value in (resid, attn)]
    moments_out[...] = jnp.where(image == 0, 0.0, moments_out[...]) + jnp.concatenate(moments, 0)


def residual_rows(flag, own, far, inputs, w_attn_out, gain):
    images, rows, width = inputs.shape
    tokens = images * rows
    block = pl.BlockSpec((rows, width), lambda i, flag_ref: (i, 0))
    return pl.pallas_call(
        functools.partial(residual_kernel, images),
        grid_spec=pltpu.PrefetchScalarGridSpec(
            num_scalar_prefetch=1,
            grid=(images,),
            in_specs=[whole((1, rows, width))] * images
            + [
                pl.BlockSpec((1, rows, width), lambda i, flag_ref: (i, 0, 0)),
                whole(w_attn_out.shape),
                whole(gain.shape),
            ],
            out_specs=[block, block, block, whole((2, width))],
        ),
        out_shape=[
            pltpu.HBM((tokens, width), BF16),
            pltpu.HBM((tokens, width), F32),
            jax.ShapeDtypeStruct((tokens, width), BF16),
            jax.ShapeDtypeStruct((2, width), F32),
        ],
        compiler_params=params(24),
        cost_estimate=cost(2 * width * tokens * width, 10 * MIB),
        name="residual_rows",
    )(flag, *own, *far, in_hbm(inputs), w_attn_out, gain)


def blocks_kernel(first, slots_ref, rows_ref, *out_refs):
    for k, out_ref in enumerate(out_refs):
        shape = (out_ref.shape[0], rows_ref.shape[0])
        places = lax.broadcasted_iota(jnp.int32, shape, 0) + (first + k) * out_ref.shape[0]
        hit = hits((slots_ref[0:1, :], slots_ref[1:2, :]), places)
        out_ref[...] = dot(hit, rows_ref[...]).astype(BF16)


def dispatch_blocks(slot_rows, rows, first, count, slots):
    tokens, width = rows.shape
    return pl.pallas_call(
        functools.partial(blocks_kernel, first),
        out_shape=[pltpu.HBM((slots, width), BF16)] * count,
        compiler_params=params(16),
        cost_estimate=cost(2 * count * slots * tokens * width, 4 * count * slots * width),
        name="dispatch_blocks",
    )(slot_rows, rows)


def expert_kernel(capacity, count, kept, me_ref, *refs):
    blocks, refs = refs[:count], refs[count:]
    up_ref, router_ref, w_in_ref, b_in_ref, w_out_ref, b_out_ref, *refs = refs
    y_out, rows_out, act_out, d_hidden_out, d_y_out, b_in_sum, b_out_sum, *refs = refs[kept:]
    backs, pair = refs[:count], refs[count]
    slots, width = blocks[0].shape
    step = 2 * slots
    hidden_width = w_in_ref.shape[1]
    chunk = 512
    index = pl.program_id(0)
    odd = me_ref[0] % 2 == 1
    for i in range(count // 2):

        @pl.when(index == i)
        def load():
            both = [blocks[2 * i][...].astype(F32), blocks[2 * i + 1][...].astype(F32)]
            pair[...] = jnp.concatenate(both, 0).astype(BF16)

    rows = pair[...]
    rows_out[...] = rows
    logits = dot(rows, router_ref[...], 1, 1)
    gate = jnp.exp(logits - jnp.max(logits, -1, keepdims=True))
    mine = lax.broadcasted_iota(jnp.int32, gate.shape, 1) == me_ref[0]
    total = jnp.sum(gate, -1, keepdims=True)
    gate = jnp.sum(jnp.where(mine, gate, 0.0), -1, keepdims=True) / total
    low, high = up_ref[0].astype(F32), up_ref[1].astype(F32)
    up_float = jnp.concatenate([jnp.where(odd, high, low), jnp.where(odd, low, high)], 0)
    d_y = (gate * up_float).astype(BF16)
    d_y_out[...] = d_y
    y = jnp.zeros((step, width), F32)
    back = jnp.zeros((step, width), F32)

    def accumulate(ref, at, value):
        ref[:, at] = jnp.where(index == 0, 0.0, ref[:, at]) + jnp.sum(
            value.astype(F32), 0, keepdims=True
        )

    for c in range(hidden_width // chunk):
        at = slice(c * chunk, (c + 1) * chunk)
        hidden = dot(rows, w_in_ref[:, at]) + b_in_ref[:, at].astype(F32)
        square = hidden * hidden
        root = math.sqrt(2.0 / math.pi)
        slope = jnp.tanh(hidden * (root + (root * 0.044715) * square))
        half = 0.5 * (1.0 + slope)
        act = (hidden * half).astype(BF16)
        d_gelu = half + (0.5 * hidden) * (1.0 - slope * slope) * (
            root + (3.0 * root * 0.044715) * square
        )
        d_hidden = (dot(d_y, w_out_ref[at, :], 1, 1) * d_gelu).astype(BF16)
        act_out[:, at] = act
        d_hidden_out[:, at] = d_hidden
        y += dot(act, w_out_ref[at, :])
        back += dot(d_hidden, w_in_ref[:, at], 1, 1)
        accumulate(b_in_sum, at, d_hidden)
    accumulate(b_out_sum, slice(0, width), d_y)
    y = (y + b_out_ref[...].astype(F32)).astype(BF16).astype(F32)
    d_weight = jnp.sum(y * up_float, -1, keepdims=True)
    y = y * gate
    y_out[0] = jnp.where(odd, y[slots:], y[:slots]).astype(BF16)
    y_out[1] = jnp.where(odd, y[:slots], y[slots:]).astype(BF16)
    row = lax.broadcasted_iota(jnp.int32, (step, width), 0)
    lane = lax.broadcasted_iota(jnp.int32, (step, width), 1)
    for s in range(2):
        line = jnp.sum(jnp.where(row - s * slots == lane, d_weight, 0.0), 0, keepdims=True)
        line = jnp.where(lane[:1] < capacity, line, 0.0)
        top = line.astype(BF16).astype(F32)
        back = jnp.where(row == s * slots + capacity, top, back)
        back = jnp.where(row == s * slots + capacity + 1, line - top, back)
    for i in range(count // 2):

        @pl.when(index == i)
        def store():
            backs[2 * i][...] = back[:slots].astype(BF16)
            backs[2 * i + 1][...] = back[slots:].astype(BF16)


def expert_group(me, blocks, first, up, w_router, w_in, b_in, w_out, b_out, capacity, kept):
    count = len(blocks)
    slots, width = blocks[0].shape
    sources = up.shape[0]
    total = sources * slots
    hidden_width = w_in.shape[1]
    step = 2 * slots
    begin = first // 2
    rows = lambda size: pl.BlockSpec((step, size), lambda i, me_ref: (i + begin, 0))
    sides = pl.BlockSpec((2, slots, width), lambda i, me_ref: ((me_ref[0] // 2) ^ (i + begin), 0, 0))
    anywhere = pl.BlockSpec(memory_space=pl.ANY)
    given = 1 + count + 6
    shapes = [
        pltpu.HBM((sources, slots, width), BF16),
        pltpu.HBM((total, width), BF16),
        pltpu.HBM((total, hidden_width), BF16),
        pltpu.HBM((total, hidden_width), BF16),
        pltpu.HBM((total, width), BF16),
    ]
    outs = pl.pallas_call(
        functools.partial(expert_kernel, capacity, count, len(kept)),
        grid_spec=pltpu.PrefetchScalarGridSpec(
            num_scalar_prefetch=1,
            grid=(count // 2,),
            in_specs=[whole((slots, width))] * count
            + [sides]
            + [whole(a.shape) for a in (w_router, w_in, b_in, w_out, b_out)]
            + [anywhere] * len(kept),
            out_specs=[sides, rows(width), rows(hidden_width), rows(hidden_width), rows(width)]
            + [whole((1, hidden_width)), whole((1, width))]
            + [whole((slots, width))] * count,
            scratch_shapes=[pltpu.VMEM((step, width), BF16)],
        ),
        out_shape=shapes
        + [jax.ShapeDtypeStruct((1, hidden_width), F32), jax.ShapeDtypeStruct((1, width), F32)]
        + [jax.ShapeDtypeStruct((slots, width), BF16)] * count,
        input_output_aliases={given + i: i for i in range(len(kept))},
        compiler_params=params(28),
        cost_estimate=cost(8 * count * slots * width * hidden_width, 8 * MIB),
        name="expert_group",
    )(me, *map(in_hbm, blocks), in_hbm(up), w_router, w_in, b_in, w_out, b_out, *kept)
    return outs[:5], outs[5:7], list(outs[7:])


def weight_kernel(left_ref, right_ref, out_ref, turned):
    @pl.when(pl.program_id(0) == 0)
    def turn():
        turned[...] = left_ref[...].T

    out_ref[...] = dot(turned[...], right_ref[...]).astype(BF16)


def weight_grad(left, right, begin, end, block=512):
    total, width = left.shape
    blocks = end - begin
    return pl.pallas_call(
        weight_kernel,
        grid=(blocks,),
        in_specs=[
            whole(left.shape),
            pl.BlockSpec((total, block), lambda i: (0, i + begin)),
        ],
        out_specs=pl.BlockSpec((width, block), lambda i: (0, i)),
        out_shape=jax.ShapeDtypeStruct((width, blocks * block), BF16),
        scratch_shapes=[pltpu.VMEM((width, total), BF16)],
        compiler_params=params(24),
        cost_estimate=cost(2 * total * width * blocks * block, 7 * MIB),
        name="weight_grad",
    )(in_hbm(left), in_hbm(right))


def sides_kernel(turned, lows, low_ref, low_far_ref, high_ref, high_far_ref, out_ref):
    low = pl.program_id(0) < lows
    own = jnp.where(low, low_ref[...], high_ref[...]).astype(F32)
    far = jnp.where(low, low_far_ref[...], high_far_ref[...]).astype(F32)
    out_ref[...] = (own + far).T if turned else own + far


def sides_sum(low, low_far, high, high_far, turned, block=512):
    width, columns = low.shape[0], low.shape[1] + high.shape[1]
    blocks = low.shape[1] // block
    lows = pl.BlockSpec((width, block), lambda i: (0, jnp.minimum(i, blocks - 1)))
    highs = pl.BlockSpec((width, block), lambda i: (0, jnp.maximum(i - blocks, 0)))
    if turned:
        shape, out = (columns, width), pl.BlockSpec((block, width), lambda i: (i, 0))
    else:
        shape, out = (width, columns), pl.BlockSpec((width, block), lambda i: (0, i))
    return pl.pallas_call(
        functools.partial(sides_kernel, turned, blocks),
        grid=(columns // block,),
        in_specs=[lows, lows, highs, highs],
        out_specs=out,
        out_shape=jax.ShapeDtypeStruct(shape, F32),
        compiler_params=params(20),
        cost_estimate=cost(width * columns, 8 * width * columns),
        name="sides_sum",
    )(in_hbm(low), low_far, in_hbm(high), high_far)


def combine_kernel(slots_ref, y_ref, resid_ref, out_ref, moment_ref):
    step, total = out_ref.shape[0], y_ref.shape[0]
    places = lax.broadcasted_iota(jnp.int32, (step, total), 1)
    moe = dot(hits((slots_ref[:, 0:1], slots_ref[:, 1:2]), places), y_ref[...])
    out_ref[...] = (resid_ref[...] + moe).astype(BF16)
    moment = jnp.sum(moe * moe, 0, keepdims=True)
    moment_ref[...] = jnp.where(pl.program_id(0) == 0, 0.0, moment_ref[...]) + moment


def combine_rows(slot_columns, y, resid, step):
    tokens, width = resid.shape
    total = y.shape[0]
    block = lambda size: pl.BlockSpec((step, size), lambda i: (i, 0))
    return pl.pallas_call(
        combine_kernel,
        grid=(tokens // step,),
        in_specs=[block(TOP), whole(y.shape), block(width)],
        out_specs=[block(width), whole((1, width))],
        out_shape=[
            jax.ShapeDtypeStruct((tokens, width), BF16),
            jax.ShapeDtypeStruct((1, width), F32),
        ],
        compiler_params=params(24),
        cost_estimate=cost(2 * total * tokens * width, 8 * MIB),
        name="combine_rows",
    )(slot_columns, y, in_hbm(resid))


def token_back_kernel(
    capacity,
    slots,
    experts,
    later,
    flag_ref,
    *refs,
):
    me = flag_ref[2]
    backs, refs = refs[:experts], refs[experts:]
    if later:
        unused, attn_ref, router_ref_sum, gain_ref_sum, *refs = refs
    (
        columns_ref,
        lines_ref,
        resid_ref,
        normed_ref,
        heads_ref,
        up_ref,
        w_out_ref,
        router_ref,
        gain_ref,
        d_resid_out,
        d_heads_out,
        attn_sum,
        gain_sum,
        router_out,
        d_weights,
        back_ref,
        near_router,
        router_sum,
    ) = refs
    step, width = resid_ref.shape
    total = back_ref.shape[0]
    first = pl.program_id(0) == 0

    @pl.when(first)
    def columns():
        near_router[...] = jnp.concatenate(
            [router_ref[pl.ds(e ^ me, 1), :] for e in range(experts)], 0
        ).astype(BF16)
        row = lax.broadcasted_iota(jnp.int32, (slots, 256), 0)
        lane = lax.broadcasted_iota(jnp.int32, (slots, 256), 1)
        for e in range(0, experts, 2):
            pair = [backs[e][...].astype(F32), backs[e + 1][...].astype(F32)]
            back_ref[e * slots : (e + 2) * slots, :] = jnp.concatenate(pair, 0).astype(BF16)
        for e in range(experts):
            block = backs[e][:, 0:256].astype(F32)
            line = jnp.sum(jnp.where(row >= capacity, block, 0.0), 0, keepdims=True)
            column = jnp.sum(jnp.where(row == lane, line, 0.0), -1, keepdims=True)
            d_weights[e * slots : (e + 1) * slots, :] = jnp.broadcast_to(column, (slots, step))

    def accumulate(ref, value, given_ref=None):
        given = 0.0 if given_ref is None else given_ref[...]
        ref[...] = jnp.where(first, given, ref[...]) + value

    line_slots = (lines_ref[0:1, :], lines_ref[1:2, :])
    d_gates = []
    for e in range(experts):
        places = lax.broadcasted_iota(jnp.int32, (slots, step), 0) + e * slots
        hit = (places == line_slots[0]) | (places == line_slots[1])
        d_gates.append(
            jnp.sum(
                jnp.where(hit, d_weights[e * slots : (e + 1) * slots, :], 0.0), 0, keepdims=True
            )
        )
    d_gates = jnp.concatenate(d_gates, 0)
    logits = dot(near_router[...], normed_ref[...], 1, 1)
    gates = jnp.exp(logits - jnp.max(logits, 0, keepdims=True))
    gates = gates / jnp.sum(gates, 0, keepdims=True)
    d_logits = (gates * (d_gates - jnp.sum(gates * d_gates, 0, keepdims=True))).astype(BF16)
    places = lax.broadcasted_iota(jnp.int32, (step, total), 1)
    d_normed = dot(hits((columns_ref[:, 0:1], columns_ref[:, 1:2]), places), back_ref[...])
    d_normed += dot(d_logits, near_router[...], 0, 0)
    normed, inverse = normalize(resid_ref[...])
    d_resid = up_ref[...].astype(F32) + norm_back(d_normed * gain_ref[...], normed, inverse)
    d_attn = d_resid.astype(BF16)
    d_resid_out[...] = d_resid
    d_heads_out[...] = dot(d_attn, w_out_ref[...], 1, 1).astype(BF16)
    accumulate(attn_sum, dot(heads_ref[...], d_attn, 0, 0), attn_ref if later else None)
    accumulate(router_sum, dot(d_logits, normed_ref[...]))
    gain_term = jnp.sum(d_normed * normed, 0, keepdims=True)
    accumulate(gain_sum, gain_term, gain_ref_sum if later else None)

    @pl.when(pl.program_id(0) == pl.num_programs(0) - 1)
    def finish():
        for e in range(experts):
            at = pl.ds(e ^ me, 1)
            given = router_ref_sum[at, :] if later else 0.0
            router_out[at, :] = router_sum[e : e + 1, :] + given


def token_back(
    flag,
    mine,
    kept,
    slot_columns,
    slot_rows,
    backs,
    resid,
    normed,
    heads,
    up,
    w_attn_out,
    w_router_t,
    gain,
    capacity,
    slots,
    step,
):
    tokens, width = resid.shape
    experts = w_router_t.shape[0]
    total = experts * slots
    part = tokens // step // 2
    image = lambda i, flag_ref: i + (flag_ref[0] if mine else 1 - flag_ref[0]) * part
    block = lambda size: pl.BlockSpec((step, size), lambda i, flag_ref: (image(i, flag_ref), 0))
    sums = [(width, width), (1, width), (experts, width)]
    given = [kept[0], kept[2], kept[4], kept[3]] if kept else []
    return pl.pallas_call(
        functools.partial(token_back_kernel, capacity, slots, experts, bool(kept)),
        grid_spec=pltpu.PrefetchScalarGridSpec(
            num_scalar_prefetch=1,
            grid=(part,),
            in_specs=[whole((slots, width))] * experts
            + [pl.BlockSpec(memory_space=pl.ANY)] * (len(given) > 0)
            + [whole(value.shape) for value in given[1:]]
            + [
                block(TOP),
                pl.BlockSpec((TOP, step), lambda i, flag_ref: (0, image(i, flag_ref))),
                block(width),
                block(width),
                block(width),
                block(width),
                whole(w_attn_out.shape),
                whole(w_router_t.shape),
                whole(gain.shape),
            ],
            out_specs=[block(width), pl.BlockSpec((step, width), lambda i, flag_ref: (i, 0))]
            + [whole(shape) for shape in sums],
            scratch_shapes=[
                pltpu.VMEM((total, step), F32),
                pltpu.VMEM((total, width), BF16),
                pltpu.VMEM((experts, width), BF16),
                pltpu.VMEM((experts, width), F32),
            ],
        ),
        out_shape=[
            pltpu.HBM((tokens, width), F32),
            pltpu.HBM((part * step, width), BF16),
            pltpu.HBM((width, width), F32),
            jax.ShapeDtypeStruct((1, width), F32),
            jax.ShapeDtypeStruct((experts, width), F32),
        ],
        input_output_aliases={1 + experts: 0} if kept else {},
        compiler_params=params(30),
        cost_estimate=cost((total + 2 * width) * tokens * width, 7 * MIB),
        name="token_back",
    )(
        flag,
        *map(in_hbm, backs),
        *map(in_hbm, given),
        slot_columns,
        slot_rows,
        in_hbm(resid),
        in_hbm(normed),
        in_hbm(heads),
        in_hbm(up),
        w_attn_out,
        w_router_t,
        gain,
    )


def grad_sum_kernel(flag_ref, resid_ref, own_ref, far_ref, out_ref):
    mine = (flag_ref[0] == 0) == (pl.program_id(0) < pl.num_programs(0) // 2)
    out_ref[...] = resid_ref[...] + jnp.where(mine, own_ref[0], far_ref[0]).astype(F32)


def grad_sum(flag, d_resid, own, far):
    part, rows, width = own.shape
    tokens = d_resid.shape[0]
    pick = pl.BlockSpec((1, rows, width), lambda i, flag_ref: (lax.rem(i, part), 0, 0))
    return pl.pallas_call(
        grad_sum_kernel,
        grid_spec=pltpu.PrefetchScalarGridSpec(
            num_scalar_prefetch=1,
            grid=(tokens // rows,),
            in_specs=[pl.BlockSpec((rows, width), lambda i, flag_ref: (i, 0)), pick, pick],
            out_specs=pl.BlockSpec((rows, width), lambda i, flag_ref: (i, 0)),
        ),
        out_shape=jax.ShapeDtypeStruct((tokens, width), F32),
        compiler_params=params(16),
        cost_estimate=cost(tokens * width, 6 * MIB),
        name="grad_sum",
    )(flag, in_hbm(d_resid), own, far)


AXES = ("wide", "narrow")


def device_bits():
    n_narrow = lax.axis_size("narrow")
    masks = [1 << b for b in range((n_narrow * lax.axis_size("wide")).bit_length() - 1)]
    masks.remove(n_narrow)
    return [n_narrow] + masks


def sum_steps():
    first, *rest = device_bits()
    return [(first,)] + [tuple(rest[i : i + 2]) for i in range(0, len(rest), 2)]


def swap(value, mask, axes=AXES):
    size = math.prod(lax.axis_size(axis) for axis in axes)
    return lax.ppermute(value, axes, [(i, i ^ mask) for i in range(size)])


def partners(bits):
    me = lax.axis_index(AXES)
    place = sum(((me // bit) % 2) << b for b, bit in enumerate(bits))
    masks = [
        sum(bit for b, bit in enumerate(bits) if (j >> b) & 1) for j in range(1 << len(bits))
    ]
    return masks, place


def fold_kernel(given, members, place_ref, keep_ref, *refs):
    del place_ref
    step = pl.program_id(0)
    total = keep_ref[...]
    for far_ref in refs[:given]:
        total += far_ref[...].astype(F32)
    own_out, *send_outs = refs[given:]

    @pl.when(step == 0)
    def keep():
        own_out[...] = total

    for j, send_out in enumerate(send_outs):

        @pl.when(step == j + 1)
        def send():
            send_out[...] = total.astype(BF16)


def fold(keep, far, bits):
    masks, place = partners(bits)
    members = len(masks)
    rows, size = keep.shape
    part = rows // members
    pick = pl.BlockSpec((part, size), lambda j, place_ref: (place_ref[0] ^ j, 0))
    own, *send = pl.pallas_call(
        functools.partial(fold_kernel, len(far), members),
        grid_spec=pltpu.PrefetchScalarGridSpec(
            num_scalar_prefetch=1,
            grid=(members,),
            in_specs=[pick] * (1 + len(far)),
            out_specs=[whole((part, size))] * members,
        ),
        out_shape=[jax.ShapeDtypeStruct((part, size), F32)]
        + [jax.ShapeDtypeStruct((part, size), BF16)] * (members - 1),
        compiler_params=params(32),
        cost_estimate=cost(0, 8 * rows * size),
        name="fold",
    )(place.reshape(1).astype(jnp.int32), in_hbm(keep), *far)
    return own, [swap(value, mask) for value, mask in zip(send, masks[1:])]


def sum_parts(value, bits):
    masks, place = partners(bits)
    part = value.shape[0] // len(masks)
    pick = lambda j: lax.dynamic_slice_in_dim(value, (place ^ j) * part, part, 0)
    far = [swap(pick(j).astype(BF16), masks[j]) for j in range(1, len(masks))]
    total = pick(0)
    for term in far:
        total = total + term.astype(F32)
    return total


def spread_parts(value, bits):
    masks, place = partners(bits)
    parts = [value] + [swap(value, mask) for mask in masks[1:]]
    for b in range(len(bits)):
        side = (place >> b) % 2 == 0
        parts = [
            jnp.where(
                side,
                jnp.concatenate([parts[i], parts[i + 1]], 0),
                jnp.concatenate([parts[i + 1], parts[i]], 0),
            )
            for i in range(0, len(parts), 2)
        ]
    return parts[0]


def close_kernel(keep_ref, moment_ref, *refs):
    total = keep_ref[...]
    for far_ref in refs[:-1]:
        total += far_ref[...].astype(F32)
    row = lax.broadcasted_iota(jnp.int32, total.shape, 0)
    lane = lax.broadcasted_iota(jnp.int32, total.shape, 1) - (total.shape[1] - 2)
    moment = jnp.sum(moment_ref[...], 1, keepdims=True)
    high = moment.astype(BF16).astype(F32)
    extra = jnp.where(lane == 0, high, moment - high)
    refs[-1][...] = jnp.where((row == 0) & (lane >= 0), extra, total).astype(BF16)


def close(keep, far, moment):
    return pl.pallas_call(
        close_kernel,
        out_shape=jax.ShapeDtypeStruct(keep.shape, BF16),
        compiler_params=params(16),
        cost_estimate=cost(0, 8 * keep.size),
        name="close",
    )(keep, moment, *far)


def add_kernel(*refs):
    terms = [ref[...].astype(F32) for ref in refs[:-1]]
    while len(terms) > 1:
        terms = [terms[i] + terms[i + 1] for i in range(0, len(terms), 2)]
    refs[-1][...] = terms[0].astype(BF16)


def add(terms):
    return pl.pallas_call(
        add_kernel,
        out_shape=jax.ShapeDtypeStruct(terms[0].shape, BF16),
        compiler_params=params(16),
        cost_estimate=cost(0, 2 * len(terms) * terms[0].size),
        name="add",
    )(*terms)


def apart_kernel(experts, count, flag_ref, own_ref, far_ref, qkv_out, attn_out, router_out, *outs):
    gain_one_out, gain_two_out, stats_out, small = outs
    half, width = own_ref.shape[0], attn_out.shape[1]
    upper = flag_ref[1] == 1
    own, far = own_ref[...].astype(F32), far_ref[...].astype(F32)
    for rows, value in ((0, jnp.where(upper, far, own)), (half, jnp.where(upper, own, far))):
        rows = slice(rows, rows + half)
        qkv_out[rows, :] = value[:, : 3 * width]
        attn_out[rows, :] = value[:, 3 * width : 4 * width]
        small[rows, :] = value[:, 4 * width :]
    values = small[...]
    lines = values.T
    router_out[...] = lines[:experts]
    gain_two_out[...] = lines[experts : experts + 1, :]
    gain_one_out[...] = lines[experts + 3 : experts + 4, :]
    sums = jnp.sum(lines, 1, keepdims=True)
    moments = (
        sums[experts + 1 : experts + 2],
        sums[experts + 2 : experts + 3],
        sums[SMALL - 2 : SMALL - 1] + sums[SMALL - 1 :],
    )
    lane = lax.broadcasted_iota(jnp.int32, stats_out.shape, 1)
    stats = jnp.where(lane == 0, moments[0], jnp.where(lane == 1, moments[1], moments[2]))
    stats_out[...] = jnp.sqrt(stats / count + EPS)


def sums_apart(flag, own, far, experts, count):
    width = 2 * own.shape[0]
    shapes = [(width, 3 * width), (width, width), (experts, width), (1, width), (1, width), (1, 128)]
    return pl.pallas_call(
        functools.partial(apart_kernel, experts, count),
        grid_spec=pltpu.PrefetchScalarGridSpec(
            num_scalar_prefetch=1,
            grid=(1,),
            in_specs=[whole(own.shape), whole(far.shape)],
            out_specs=[whole(shape) for shape in shapes],
            scratch_shapes=[pltpu.VMEM((width, SMALL), F32)],
        ),
        out_shape=[jax.ShapeDtypeStruct(shape, F32) for shape in shapes],
        compiler_params=params(32),
        cost_estimate=cost(0, 8 * MIB),
        name="sums_apart",
    )(flag, own, far)


def gathered_attention(inputs, gain_one, w_qkv):
    images, rows_dev, width = inputs.shape
    tokens = images * rows_dev
    head_dim = width // HEADS
    scale = head_dim ** (-0.5)
    seq_len = rows_dev * lax.axis_size("narrow")
    group = math.gcd(images, max(1, 512 // rows_dev))
    blocks = images // group
    normed_one, inverse_one = normalize(inputs.astype(F32).reshape(tokens, width))
    input_one = (normed_one * gain_one).astype(BF16)
    projected = jnp.dot(input_one, w_qkv, preferred_element_type=F32).astype(BF16)
    queries = projected[:, :width].reshape(images, rows_dev, width)
    keys_own = projected[:, width : 2 * width].reshape(images, rows_dev, width)
    values_own = projected[:, 2 * width :].reshape(images, rows_dev, width)
    keys_all = lax.all_gather(keys_own, "narrow", axis=1, tiled=True)
    values_all = lax.all_gather(values_own, "narrow", axis=1, tiled=True)
    query_blocks = queries.reshape(blocks, group, rows_dev, HEADS, head_dim)
    key_blocks = keys_all.reshape(blocks, group, seq_len, HEADS, head_dim)
    value_blocks = values_all.reshape(blocks, group, seq_len, HEADS, head_dim)

    def attend_block(operands):
        query_b, key_b, value_b = operands
        scores = jnp.einsum("gqhd,gkhd->ghqk", query_b, key_b, preferred_element_type=F32) * scale
        top_score = jnp.max(scores, -1, keepdims=True)
        exponent = jnp.exp(scores - top_score)
        total = jnp.sum(exponent, -1, keepdims=True)
        weights = (exponent / total).astype(BF16)
        mixed = jnp.einsum("ghqk,gkhd->gqhd", weights, value_b, preferred_element_type=F32)
        return (mixed.astype(BF16), (top_score + jnp.log(total))[..., 0])

    heads_out, log_total = lax.map(attend_block, (query_blocks, key_blocks, value_blocks))

    def back_block(operands):
        query_b, key_b, value_b, total_b, d_head_b = operands
        scores = jnp.einsum("gqhd,gkhd->ghqk", query_b, key_b, preferred_element_type=F32) * scale
        weights = jnp.exp(scores - total_b[..., None])
        d_weights = jnp.einsum("gqhd,gkhd->ghqk", d_head_b, value_b, preferred_element_type=F32)
        spread = jnp.sum(weights * d_weights, -1, keepdims=True)
        d_scores = (weights * (d_weights - spread)).astype(BF16)
        d_query = jnp.einsum("ghqk,gkhd->gqhd", d_scores, key_b, preferred_element_type=F32) * scale
        d_key = jnp.einsum("ghqk,gqhd->gkhd", d_scores, query_b, preferred_element_type=F32) * scale
        d_value = jnp.einsum(
            "ghqk,gqhd->gkhd", weights.astype(BF16), d_head_b, preferred_element_type=F32
        )
        return (d_query.astype(BF16), d_key, d_value)

    def back(d_heads, d_resid):
        d_head_blocks = d_heads.reshape(blocks, group, rows_dev, HEADS, head_dim)
        d_queries, key_terms, value_terms = lax.map(
            back_block, (query_blocks, key_blocks, value_blocks, log_total, d_head_blocks)
        )
        d_keys, d_values = (
            lax.psum_scatter(
                terms.reshape(images, seq_len, width), "narrow", scatter_dimension=1, tiled=True
            )
            .astype(BF16)
            .reshape(tokens, width)
            for terms in (key_terms, value_terms)
        )
        d_projected = jnp.concatenate([d_queries.reshape(tokens, width), d_keys, d_values], 1)
        d_weight = jnp.dot(input_one.T, d_projected, preferred_element_type=F32)
        d_input = jnp.dot(d_projected, w_qkv.T, preferred_element_type=F32)
        d_gain = jnp.sum(d_input * normed_one, 0, keepdims=True)
        return (
            d_resid + norm_back(d_input * gain_one, normed_one, inverse_one),
            d_weight,
            d_gain,
        )

    return heads_out.reshape(images, rows_dev, width), back


def shards(
    inputs,
    cotangent,
    ln1_gain,
    w_qkv,
    w_attn_out,
    ln2_gain,
    w_router,
    expert_in,
    expert_in_bias,
    expert_out,
    expert_out_bias,
    route_ids,
    route_slots,
    route_dropped,
):
    images, rows_dev, width = inputs.shape
    tokens = images * rows_dev
    experts = w_router.shape[1]
    n_wide = lax.axis_size("wide")
    n_narrow = lax.axis_size("narrow")
    capacity = max(2, 42 * tokens // (20 * experts))
    slots = -(-(capacity + 2) // 8) * 8
    total = experts * slots
    gain_one = ln1_gain.astype(F32).reshape(1, width)
    gain_two = ln2_gain.astype(F32).reshape(1, width)
    paired = n_narrow == 2 and images % 2 == 0
    part = images // 2
    place = lax.axis_index("narrow") if paired else jnp.int32(0)
    me = lax.axis_index("wide")
    flag = jnp.stack([place, me % 2, me])

    slot_columns = jnp.where(
        route_dropped == 0, route_ids * slots + route_slots, -1
    ).reshape(tokens, TOP)
    slot_rows = slot_columns.T
    near_columns = jnp.where(
        route_dropped == 0, (route_ids ^ me) * slots + route_slots, -1
    ).reshape(tokens, TOP)
    near_rows = near_columns.T
    up = cotangent.reshape(tokens, width)

    def exchange(rows):
        return lax.all_to_all(
            rows.reshape(experts, slots, width), "wide", split_axis=0, concat_axis=0, tiled=True
        ).reshape(total, width)

    up_rows = dispatch_rows(slot_rows, up, total)
    if paired:
        pick = lambda k: lax.dynamic_slice_in_dim(inputs, (1 - place) * part + k, 1, 0)
        far_inputs = [swap(pick(0), 1)]
        far_inputs[0], up_rows = lax.optimization_barrier((far_inputs[0], up_rows))
        far_inputs += [swap(pick(k), 1) for k in range(1, part)]
    up_here = exchange(up_rows)

    if paired:
        w_qkv_t = w_qkv.T
        heads_own, heads_far, saved = [], [], []
        for k, far in enumerate(far_inputs):
            own_heads, far_heads, *saved = attend(
                flag, inputs, k, far, gain_one, w_qkv_t, saved
            )
            heads_own.append(own_heads)
            heads_far.append(swap(far_heads, 1))
        proj, log_total = saved
    else:
        heads_own, attention_back = gathered_attention(inputs, gain_one, w_qkv)
        heads_own = [heads_own[k : k + 1] for k in range(images)]
        heads_own, heads_far = heads_own[:part], heads_own[part:]

    heads, resid, normed_two, moments = residual_rows(
        flag, heads_own, heads_far, inputs, w_attn_out, gain_two
    )
    w_in, w_out = expert_in[0], expert_out[0]
    up_here = up_here.reshape(experts, slots, width)

    def expert(blocks, first, kept):
        return expert_group(
            me.reshape(1),
            blocks,
            first,
            up_here,
            w_router.T,
            w_in,
            expert_in_bias,
            w_out,
            expert_out_bias,
            capacity,
            kept,
        )

    def after(value, *others):
        return lax.optimization_barrier((value,) + others)[0]

    half = experts // 2
    quarter = half // 2
    send = lambda block, k: swap(block, k, ("wide",)) if k else block
    blocks = dispatch_blocks(near_rows, normed_two, half, half, slots)
    cross = [send(block, half + k) for k, block in enumerate(blocks[:2])]
    local = []
    for k, block in enumerate(
        dispatch_blocks(near_rows, after(normed_two, blocks[0]), 0, half, slots)
    ):
        local.append(send(after(block, local[k - 3]) if k > 3 else block, k))
    kept, sums_a, backs_a = expert(local, 0, [])
    for k in range(2, half):
        gate = local[k + half - EARLY] if k < EARLY else sums_a[1]
        cross.append(send(after(blocks[k], gate), half + k))
    backs_a = [send(block, k) for k, block in enumerate(backs_a)]
    kept, sums_b, backs_b = expert(cross[:quarter], half, kept)
    backs_b = [send(block, half + k) for k, block in enumerate(backs_b)]
    last = cross[quarter:]
    last[0] = after(last[0], *backs_a[1:6])
    kept, sums_c, backs_c = expert(last, half + quarter, kept)
    y, rows_here, act, d_hidden, d_y = kept
    y = y.reshape(total, width)
    last_block = w_in.shape[1] // 512
    grad_out = [weight_grad(after(d_y, *backs_b[:2]), act, 0, MIDDLE)]
    backs_c = [
        send(after(block, grad_out[0]), half + quarter + k) for k, block in enumerate(backs_c)
    ]
    grad_out.append(weight_grad(after(d_y, grad_out[0], *backs_b[2:], *backs_a[6:]), act, MIDDLE, last_block))
    grad_in = [weight_grad(after(rows_here, grad_out[1], *backs_c[:2]), d_hidden, 0, LATE)]
    b_in_sum, b_out_sum = (sum(terms) for terms in zip(sums_a, sums_b, sums_c))
    backs = backs_a + backs_b + backs_c
    far_out = [swap(part_grad, 1) for part_grad in grad_out] if n_narrow == 2 else []
    backs[-1] = after(backs[-1], *grad_in)

    def back_to_tokens(mine, kept):
        return token_back(
            flag,
            mine,
            kept,
            near_columns,
            near_rows,
            backs,
            resid,
            normed_two,
            heads,
            up,
            w_attn_out,
            w_router.T.astype(F32),
            gain_two,
            capacity,
            slots,
            rows_dev,
        )

    first = back_to_tokens(False, [])
    sent = first[1]
    d_resid, d_heads, attn_term, gain_two_term, router_term = back_to_tokens(True, first)
    sent, grad_in[0] = lax.optimization_barrier((sent, grad_in[0]))
    biases = jnp.concatenate([b_in_sum, b_out_sum], 1)
    small = jnp.concatenate([router_term, gain_two_term, moments], 0)
    count = tokens * width * n_wide * n_narrow
    steps = sum_steps()
    if paired:
        d_far = swap(sent.reshape(part, rows_dev, width), 1)
        far_in = [swap(grad_in[0], 1)]
        far_biases = swap(biases, 1)
        y = exchange(after(y, sent))
        d_far, *far_out = lax.optimization_barrier((d_far, *far_out))
        d_own, d_far, keep, send = attend_back(
            flag,
            inputs,
            far_inputs,
            gain_one,
            w_qkv_t,
            proj,
            log_total,
            d_heads.reshape(part, rows_dev, width),
            d_far,
            attn_term,
            small,
        )
        sums, far = fold(keep, [swap(send, steps[0][0])], steps[1])
        block_out, moe_moment = combine_rows(slot_columns, after(y, sums), resid, rows_dev)
        grad_in.append(weight_grad(after(rows_here, sums), d_hidden, LATE, last_block))
        far_in.append(swap(grad_in[1], 1))
        far[0], moe_moment, far_biases, far_in[0], *unused = lax.optimization_barrier(
            (far[0], moe_moment, far_biases, far_in[0], grad_in[1])
        )
        biases = biases + far_biases
        bias_outs = (biases[:, : w_in.shape[1]], biases[:, w_in.shape[1] :])
        sums = close(sums, far, moe_moment)
        d_far = swap(after(d_far, sums), 1)
        for bits in steps[2:]:
            masks, unused = partners(bits)
            terms = [sums] + [swap(sums, mask) for mask in masks[1:]]
            grad_expert_out = sides_sum(
                grad_out[0], far_out[0], grad_out[1], after(far_out[1], sums), True
            )
            terms[1], grad_expert_out, *bias_outs = lax.optimization_barrier(
                (terms[1], grad_expert_out, *bias_outs)
            )
            sums = add(terms)
        sums, d_far, far_in[1] = lax.optimization_barrier((sums, d_far, far_in[1]))
        input_grad = grad_sum(flag, d_resid, d_own, d_far)
        grad_expert_in = sides_sum(grad_in[0], far_in[0], grad_in[1], far_in[1], False)
        sums = spread_parts(sums, steps[1])
        sums, input_grad, grad_expert_in = lax.optimization_barrier(
            (sums, input_grad, grad_expert_in)
        )
    else:
        y = exchange(y)
        grad_in.append(weight_grad(rows_here, d_hidden, LATE, last_block))
        grad_out, grad_in = lax.psum((grad_out, grad_in), "narrow")
        grad_expert_out = jnp.concatenate(grad_out, 1).astype(F32).T
        grad_expert_in = jnp.concatenate(grad_in, 1).astype(F32)
        biases = lax.psum(biases, "narrow")
        bias_outs = (biases[:, : w_in.shape[1]], biases[:, w_in.shape[1] :])
        d_heads = jnp.concatenate([d_heads, sent], 0)
        input_grad, qkv_term, gain_one_term = attention_back(d_heads, d_resid)
        small = small_columns(small, gain_one_term)
        sums = jnp.concatenate([qkv_term, attn_term, small], 1)
        for bits in steps:
            sums = sum_parts(sums, bits)
        block_out, moe_moment = combine_rows(slot_columns, y, resid, rows_dev)
        sums = close(sums, [], moe_moment)
        for bits in reversed(steps[1:]):
            sums = spread_parts(sums, bits)
    grad_qkv, grad_attn_out, grad_router, grad_gain_one, grad_gain_two, stats = sums_apart(
        flag, sums, swap(sums, steps[0][0]), experts, count
    )
    return (
        block_out.reshape(images, rows_dev, width),
        input_grad.reshape(images, rows_dev, width),
        grad_gain_one.reshape(width),
        grad_qkv,
        grad_attn_out,
        grad_gain_two.reshape(width),
        grad_router.T,
        grad_expert_in[None],
        bias_outs[0],
        grad_expert_out[None],
        bias_outs[1],
        stats[0, :3],
    )


def solution(mesh):
    return jax.shard_map(
        shards,
        mesh=mesh,
        in_specs=(
            P("wide", "narrow", None),
            P("wide", "narrow", None),
            P(),
            P(),
            P(),
            P(),
            P(),
            P("wide", None, None),
            P("wide", None),
            P("wide", None, None),
            P("wide", None),
            P("wide", "narrow", None),
            P("wide", "narrow", None),
            P("wide", "narrow", None),
        ),
        out_specs=(
            P("wide", "narrow", None),
            P("wide", "narrow", None),
            P(),
            P(),
            P(),
            P(),
            P(),
            P("wide", None, None),
            P("wide", None),
            P("wide", None, None),
            P("wide", None),
            P(),
        ),
        check_vma=False,
    )
```

```python
import functools
import math

import jax
import jax.numpy as jnp
from jax import lax
from jax.experimental import pallas as pl
from jax.experimental.pallas import tpu as pltpu
from jax.sharding import PartitionSpec as P

HEADS = 8
TOP = 2


EPS = 1e-06
BF16 = jnp.bfloat16
F32 = jnp.float32
MIB = 1 << 20
SMALL = 128
EARLY = 5
MIDDLE = 2
LATE = 3


def normalize(values):
    centre = jnp.mean(values, -1, keepdims=True)
    shifted = values - centre
    inverse = lax.rsqrt(jnp.mean(shifted * shifted, -1, keepdims=True) + EPS)
    return (shifted * inverse, inverse)


def norm_back(d_normed, normed, inverse):
    return inverse * (
        d_normed
        - jnp.mean(d_normed, -1, keepdims=True)
        - normed * jnp.mean(d_normed * normed, -1, keepdims=True)
    )


def dot(left, right, left_dim=1, right_dim=0):
    return lax.dot_general(
        left, right, (((left_dim,), (right_dim,)), ((), ())), preferred_element_type=F32
    )


def params(mib):
    return pltpu.CompilerParams(vmem_limit_bytes=mib * MIB)


def in_hbm(value):
    return pltpu.with_memory_space_constraint(value, pltpu.HBM)


def in_vmem(value):
    return pltpu.with_memory_space_constraint(value, pltpu.VMEM)


def cost(flops, bytes_accessed, transcendentals=0):
    return pl.CostEstimate(
        flops=int(flops), bytes_accessed=int(bytes_accessed), transcendentals=int(transcendentals)
    )


def whole(shape):
    return pl.BlockSpec(shape, lambda *unused: (0,) * len(shape))


def hits(slots, places):
    first, second = slots
    return jnp.where((places == first) | (places == second), 1.0, 0.0).astype(BF16)


def put_rows(slots_ref, rows_ref, out_ref):
    step = out_ref.shape[0]
    places = lax.broadcasted_iota(jnp.int32, (step, rows_ref.shape[0]), 0) + pl.program_id(0) * step
    out_ref[...] = dot(hits((slots_ref[0:1, :], slots_ref[1:2, :]), places), rows_ref[...]).astype(
        BF16
    )


def dispatch_rows(slot_rows, rows, total, steps=8):
    tokens, width = rows.shape
    step = total // steps
    return pl.pallas_call(
        put_rows,
        grid=(steps,),
        in_specs=[whole(slot_rows.shape), whole(rows.shape)],
        out_specs=pl.BlockSpec((step, width), lambda i: (i, 0)),
        out_shape=jax.ShapeDtypeStruct((total, width), BF16),
        compiler_params=params(20),
        cost_estimate=cost(2 * total * tokens * width, 4 * total * width),
        name="dispatch_rows",
    )(slot_rows, rows)


def attend_kernel(flag_ref, own_ref, far_ref, gain_ref, wt_ref, *refs):
    del flag_ref
    own_out, far_out, proj_ref, total_ref, mixed = refs[-5:]
    rows, width = own_ref.shape[1], own_ref.shape[2]
    head_dim = width // HEADS
    scale = head_dim ** (-0.5)
    x_float = jnp.concatenate([own_ref[0], far_ref[0]], 0).astype(F32)
    normed, unused = normalize(x_float)
    normed = (normed * gain_ref[...]).astype(BF16)
    proj_ref[0] = dot(wt_ref[...], normed, 1, 1).astype(BF16)

    def head(h, carry):
        at = pl.multiple_of(h * head_dim, head_dim)
        query = proj_ref[0, pl.ds(at, head_dim), :]
        key = proj_ref[0, pl.ds(at + width, head_dim), :]
        value = proj_ref[0, pl.ds(at + 2 * width, head_dim), :]
        scores = dot(key, query * scale, 0, 0)
        top = jnp.max(scores, 0, keepdims=True)
        exponent = jnp.exp(scores - top)
        total = jnp.sum(exponent, 0, keepdims=True)
        out = dot(value, exponent.astype(BF16)) * (1.0 / total)
        mixed[pl.ds(at, head_dim), :] = out
        total_ref[0, pl.ds(h, 1), :] = top + jnp.log(total)
        return carry

    lax.fori_loop(0, HEADS, head, 0, unroll=2)
    heads_out = mixed[...].T.astype(BF16)
    own_out[0] = heads_out[:rows]
    far_out[0] = heads_out[rows:]


def attend(flag, inputs, image, far, gain, w_qkv_t, kept):
    unused, rows, width = far.shape
    seq_len = 2 * rows
    part = inputs.shape[0] // 2
    block = lambda k, *shape: pl.BlockSpec((1,) + shape, lambda i, flag_ref: (k,) + (0,) * len(shape))
    return pl.pallas_call(
        attend_kernel,
        grid_spec=pltpu.PrefetchScalarGridSpec(
            num_scalar_prefetch=1,
            grid=(1,),
            in_specs=[
                pl.BlockSpec(
                    (1, rows, width), lambda i, flag_ref: (image + flag_ref[0] * part, 0, 0)
                ),
                block(0, rows, width),
                whole(gain.shape),
                whole(w_qkv_t.shape),
            ]
            + [pl.BlockSpec(memory_space=pl.ANY)] * len(kept),
            out_specs=[
                block(0, rows, width),
                block(0, rows, width),
                block(image, 3 * width, seq_len),
                block(image, HEADS, seq_len),
            ],
            scratch_shapes=[pltpu.VMEM((width, seq_len), F32)],
        ),
        out_shape=[
            jax.ShapeDtypeStruct((1, rows, width), BF16),
            jax.ShapeDtypeStruct((1, rows, width), BF16),
            pltpu.HBM((part, 3 * width, seq_len), BF16),
            pltpu.HBM((part, HEADS, seq_len), F32),
        ],
        input_output_aliases={5 + i: 2 + i for i in range(len(kept))},
        compiler_params=params(28),
        cost_estimate=cost(8e9, 8 * MIB, HEADS * seq_len**2),
        name="attend",
    )(flag, in_hbm(inputs), far, gain, w_qkv_t, *kept)


def small_columns(small, gain):
    rest = jnp.zeros((SMALL - small.shape[0] - 1, small.shape[1]), F32)
    return jnp.concatenate([small, gain, rest], 0).T


def attend_back_kernel(
    part,
    flag_ref,
    own_ref,
    *refs,
):
    far_refs, refs = refs[:part], refs[part:]
    attend_back_body(flag_ref, own_ref, far_refs, *refs)


def attend_back_body(
    flag_ref,
    own_ref,
    far_refs,
    gain_ref,
    wt_ref,
    proj_ref,
    total_ref,
    d_own_ref,
    d_far_ref,
    attn_ref,
    small_ref,
    own_out,
    far_out,
    keep_out,
    send_out,
    d_proj,
    d_mixed,
    weight_sum,
    gain_out,
):
    image, last = pl.program_id(0), pl.num_programs(0) - 1
    rows, width = own_ref.shape[1], own_ref.shape[2]
    head_dim = width // HEADS
    scale = head_dim ** (-0.5)
    d_mixed[...] = jnp.concatenate([d_own_ref[0], d_far_ref[0]], 0).astype(F32).T.astype(BF16)

    def head(h, carry):
        at = pl.multiple_of(h * head_dim, head_dim)
        query = proj_ref[0, pl.ds(at, head_dim), :]
        key = proj_ref[0, pl.ds(at + width, head_dim), :]
        value = proj_ref[0, pl.ds(at + 2 * width, head_dim), :]
        d_out = d_mixed[pl.ds(at, head_dim), :]
        weights = jnp.exp(dot(key, query * scale, 0, 0) - total_ref[0, pl.ds(h, 1), :])
        product = weights * dot(value, d_out, 0, 0)
        spread = jnp.sum(product, 0, keepdims=True)
        d_scores = (product - weights * spread).astype(BF16)
        d_proj[pl.ds(at, head_dim), :] = (dot(key, d_scores) * scale).astype(BF16)
        d_proj[pl.ds(at + width, head_dim), :] = (dot(query, d_scores, 1, 1) * scale).astype(BF16)
        d_proj[pl.ds(at + 2 * width, head_dim), :] = dot(d_out, weights.astype(BF16), 1, 1).astype(
            BF16
        )
        return carry

    lax.fori_loop(0, HEADS, head, 0, unroll=2)
    far = far_refs[0][0]
    for k, far_ref in enumerate(far_refs[1:]):
        far = jnp.where(image == k + 1, far_ref[0], far)
    x_float = jnp.concatenate([own_ref[0], far], 0).astype(F32)
    normed, inverse = normalize(x_float)
    d_input = dot(d_proj[...], wt_ref[...], 0, 0)
    weight_term = dot((normed * gain_ref[...]).T.astype(BF16), d_proj[...], 1, 1)
    gain_term = jnp.sum(d_input * normed, 0, keepdims=True)
    d_x = norm_back(d_input * gain_ref[...], normed, inverse).astype(BF16)
    own_out[0] = d_x[:rows]
    far_out[0] = d_x[rows:]

    @pl.when(image == 0)
    def start():
        weight_sum[...] = weight_term
        gain_out[...] = gain_term

    @pl.when(image != 0)
    def add():
        weight_sum[...] += weight_term
        gain_out[...] += gain_term

    @pl.when(image == last)
    def finish():
        half = width // 2
        parts = ((weight_sum[...], 0), (attn_ref[...], 3 * width))
        parts += ((small_columns(small_ref[...], gain_out[...]), 4 * width),)
        upper = flag_ref[1] == 1
        for value, at in parts:
            at = slice(at, at + value.shape[1])
            keep_out[:, at] = jnp.where(upper, value[half:], value[:half])
            send_out[:, at] = jnp.where(upper, value[:half], value[half:]).astype(BF16)


def attend_back(flag, inputs, far, gain, w_qkv_t, proj, total, d_heads, d_far, attn_term, small):
    part = len(far)
    unused, rows, width = far[0].shape
    seq_len = 2 * rows
    block = lambda *shape: pl.BlockSpec((1,) + shape, lambda i, flag_ref: (i,) + (0,) * len(shape))
    return pl.pallas_call(
        functools.partial(attend_back_kernel, part),
        grid_spec=pltpu.PrefetchScalarGridSpec(
            num_scalar_prefetch=1,
            grid=(part,),
            in_specs=[
                pl.BlockSpec((1, rows, width), lambda i, flag_ref: (i + flag_ref[0] * part, 0, 0)),
            ]
            + [whole((1, rows, width))] * part
            + [
                whole(gain.shape),
                whole(w_qkv_t.shape),
                block(3 * width, seq_len),
                block(HEADS, seq_len),
                block(rows, width),
                block(rows, width),
                whole(attn_term.shape),
                whole(small.shape),
            ],
            out_specs=[
                block(rows, width),
                block(rows, width),
                whole((width // 2, 4 * width + SMALL)),
                whole((width // 2, 4 * width + SMALL)),
            ],
            scratch_shapes=[
                pltpu.VMEM((3 * width, seq_len), BF16),
                pltpu.VMEM((width, seq_len), BF16),
                pltpu.VMEM((width, 3 * width), F32),
                pltpu.VMEM((1, width), F32),
            ],
        ),
        out_shape=[
            pltpu.HBM((part, rows, width), BF16),
            pltpu.HBM((part, rows, width), BF16),
            pltpu.HBM((width // 2, 4 * width + SMALL), F32),
            jax.ShapeDtypeStruct((width // 2, 4 * width + SMALL), BF16),
        ],
        compiler_params=params(36),
        cost_estimate=cost(part * 16e9, 12 * MIB, part * HEADS * seq_len**2),
        name="attend_back",
    )(
        flag,
        in_hbm(inputs),
        *map(in_hbm, far),
        gain,
        in_hbm(w_qkv_t),
        in_hbm(proj),
        total,
        in_hbm(d_heads),
        d_far,
        in_hbm(attn_term),
        small,
    )


def pick_image(flag_ref, image, images, own_refs, far_refs):
    part = images // 2
    mine = (flag_ref[0] == 0) == (image < part)
    value = jnp.where(mine, own_refs[0][0], far_refs[0][0])
    for k in range(1, part):
        other = jnp.where(mine, own_refs[k][0], far_refs[k][0])
        value = jnp.where(lax.rem(image, part) == k, other, value)
    return value


def residual_kernel(images, flag_ref, *refs):
    own_refs, far_refs, refs = refs[: images // 2], refs[images // 2 : images], refs[images:]
    x_ref, w_out_ref, gain_ref, heads_out, resid_out, normed_out, moments_out = refs
    image = pl.program_id(0)
    heads = pick_image(flag_ref, image, images, own_refs, far_refs)
    attn = dot(heads, w_out_ref[...])
    resid = x_ref[0].astype(F32) + attn
    normed, unused = normalize(resid)
    heads_out[...] = heads
    resid_out[...] = resid
    normed_out[...] = (normed * gain_ref[...]).astype(BF16)
    moments = [jnp.sum(value * value, 0, keepdims=True) for value in (resid, attn)]
    moments_out[...] = jnp.where(image == 0, 0.0, moments_out[...]) + jnp.concatenate(moments, 0)


def residual_rows(flag, own, far, inputs, w_attn_out, gain):
    images, rows, width = inputs.shape
    tokens = images * rows
    block = pl.BlockSpec((rows, width), lambda i, flag_ref: (i, 0))
    return pl.pallas_call(
        functools.partial(residual_kernel, images),
        grid_spec=pltpu.PrefetchScalarGridSpec(
            num_scalar_prefetch=1,
            grid=(images,),
            in_specs=[whole((1, rows, width))] * images
            + [
                pl.BlockSpec((1, rows, width), lambda i, flag_ref: (i, 0, 0)),
                whole(w_attn_out.shape),
                whole(gain.shape),
            ],
            out_specs=[block, block, block, whole((2, width))],
        ),
        out_shape=[
            pltpu.HBM((tokens, width), BF16),
            pltpu.HBM((tokens, width), F32),
            jax.ShapeDtypeStruct((tokens, width), BF16),
            jax.ShapeDtypeStruct((2, width), F32),
        ],
        compiler_params=params(24),
        cost_estimate=cost(2 * width * tokens * width, 10 * MIB),
        name="residual_rows",
    )(flag, *own, *far, in_hbm(inputs), w_attn_out, gain)


def blocks_kernel(first, slots_ref, rows_ref, *out_refs):
    for k, out_ref in enumerate(out_refs):
        shape = (out_ref.shape[0], rows_ref.shape[0])
        places = lax.broadcasted_iota(jnp.int32, shape, 0) + (first + k) * out_ref.shape[0]
        hit = hits((slots_ref[0:1, :], slots_ref[1:2, :]), places)
        out_ref[...] = dot(hit, rows_ref[...]).astype(BF16)


def dispatch_blocks(slot_rows, rows, first, count, slots):
    tokens, width = rows.shape
    return pl.pallas_call(
        functools.partial(blocks_kernel, first),
        out_shape=[pltpu.HBM((slots, width), BF16)] * count,
        compiler_params=params(16),
        cost_estimate=cost(2 * count * slots * tokens * width, 4 * count * slots * width),
        name="dispatch_blocks",
    )(slot_rows, rows)


def expert_kernel(capacity, count, kept, me_ref, *refs):
    blocks, refs = refs[:count], refs[count:]
    up_ref, router_ref, w_in_ref, b_in_ref, w_out_ref, b_out_ref, *refs = refs
    y_out, rows_out, act_out, d_hidden_out, d_y_out, b_in_sum, b_out_sum, *refs = refs[kept:]
    backs, pair = refs[:count], refs[count]
    slots, width = blocks[0].shape
    step = 2 * slots
    hidden_width = w_in_ref.shape[1]
    chunk = 512
    index = pl.program_id(0)
    odd = me_ref[0] % 2 == 1
    for i in range(count // 2):

        @pl.when(index == i)
        def load():
            both = [blocks[2 * i][...].astype(F32), blocks[2 * i + 1][...].astype(F32)]
            pair[...] = jnp.concatenate(both, 0).astype(BF16)

    rows = pair[...]
    rows_out[...] = rows
    logits = dot(rows, router_ref[...], 1, 1)
    gate = jnp.exp(logits - jnp.max(logits, -1, keepdims=True))
    mine = lax.broadcasted_iota(jnp.int32, gate.shape, 1) == me_ref[0]
    total = jnp.sum(gate, -1, keepdims=True)
    gate = jnp.sum(jnp.where(mine, gate, 0.0), -1, keepdims=True) / total
    low, high = up_ref[0].astype(F32), up_ref[1].astype(F32)
    up_float = jnp.concatenate([jnp.where(odd, high, low), jnp.where(odd, low, high)], 0)
    d_y = (gate * up_float).astype(BF16)
    d_y_out[...] = d_y
    y = jnp.zeros((step, width), F32)
    back = jnp.zeros((step, width), F32)

    def accumulate(ref, at, value):
        ref[:, at] = jnp.where(index == 0, 0.0, ref[:, at]) + jnp.sum(
            value.astype(F32), 0, keepdims=True
        )

    for c in range(hidden_width // chunk):
        at = slice(c * chunk, (c + 1) * chunk)
        hidden = dot(rows, w_in_ref[:, at]) + b_in_ref[:, at].astype(F32)
        square = hidden * hidden
        root = math.sqrt(2.0 / math.pi)
        slope = jnp.tanh(hidden * (root + (root * 0.044715) * square))
        half = 0.5 * (1.0 + slope)
        act = (hidden * half).astype(BF16)
        d_gelu = half + (0.5 * hidden) * (1.0 - slope * slope) * (
            root + (3.0 * root * 0.044715) * square
        )
        d_hidden = (dot(d_y, w_out_ref[at, :], 1, 1) * d_gelu).astype(BF16)
        act_out[:, at] = act
        d_hidden_out[:, at] = d_hidden
        y += dot(act, w_out_ref[at, :])
        back += dot(d_hidden, w_in_ref[:, at], 1, 1)
        accumulate(b_in_sum, at, d_hidden)
    accumulate(b_out_sum, slice(0, width), d_y)
    y = (y + b_out_ref[...].astype(F32)).astype(BF16).astype(F32)
    d_weight = jnp.sum(y * up_float, -1, keepdims=True)
    y = y * gate
    y_out[0] = jnp.where(odd, y[slots:], y[:slots]).astype(BF16)
    y_out[1] = jnp.where(odd, y[:slots], y[slots:]).astype(BF16)
    row = lax.broadcasted_iota(jnp.int32, (step, width), 0)
    lane = lax.broadcasted_iota(jnp.int32, (step, width), 1)
    for s in range(2):
        line = jnp.sum(jnp.where(row - s * slots == lane, d_weight, 0.0), 0, keepdims=True)
        line = jnp.where(lane[:1] < capacity, line, 0.0)
        top = line.astype(BF16).astype(F32)
        back = jnp.where(row == s * slots + capacity, top, back)
        back = jnp.where(row == s * slots + capacity + 1, line - top, back)
    for i in range(count // 2):

        @pl.when(index == i)
        def store():
            backs[2 * i][...] = back[:slots].astype(BF16)
            backs[2 * i + 1][...] = back[slots:].astype(BF16)


def expert_group(me, blocks, first, up, w_router, w_in, b_in, w_out, b_out, capacity, kept):
    count = len(blocks)
    slots, width = blocks[0].shape
    sources = up.shape[0]
    total = sources * slots
    hidden_width = w_in.shape[1]
    step = 2 * slots
    begin = first // 2
    rows = lambda size: pl.BlockSpec((step, size), lambda i, me_ref: (i + begin, 0))
    sides = pl.BlockSpec((2, slots, width), lambda i, me_ref: ((me_ref[0] // 2) ^ (i + begin), 0, 0))
    anywhere = pl.BlockSpec(memory_space=pl.ANY)
    given = 1 + count + 6
    shapes = [
        pltpu.HBM((sources, slots, width), BF16),
        pltpu.HBM((total, width), BF16),
        pltpu.HBM((total, hidden_width), BF16),
        pltpu.HBM((total, hidden_width), BF16),
        pltpu.HBM((total, width), BF16),
    ]
    outs = pl.pallas_call(
        functools.partial(expert_kernel, capacity, count, len(kept)),
        grid_spec=pltpu.PrefetchScalarGridSpec(
            num_scalar_prefetch=1,
            grid=(count // 2,),
            in_specs=[whole((slots, width))] * count
            + [sides]
            + [whole(a.shape) for a in (w_router, w_in, b_in, w_out, b_out)]
            + [anywhere] * len(kept),
            out_specs=[sides, rows(width), rows(hidden_width), rows(hidden_width), rows(width)]
            + [whole((1, hidden_width)), whole((1, width))]
            + [whole((slots, width))] * count,
            scratch_shapes=[pltpu.VMEM((step, width), BF16)],
        ),
        out_shape=shapes
        + [jax.ShapeDtypeStruct((1, hidden_width), F32), jax.ShapeDtypeStruct((1, width), F32)]
        + [jax.ShapeDtypeStruct((slots, width), BF16)] * count,
        input_output_aliases={given + i: i for i in range(len(kept))},
        compiler_params=params(28),
        cost_estimate=cost(8 * count * slots * width * hidden_width, 8 * MIB),
        name="expert_group",
    )(me, *map(in_hbm, blocks), in_hbm(up), w_router, w_in, b_in, w_out, b_out, *kept)
    return outs[:5], outs[5:7], list(outs[7:])


def weight_kernel(left_ref, right_ref, out_ref, turned_ref):
    @pl.when(pl.program_id(0) == 0)
    def turn():
        turned_ref[...] = left_ref[...].T

    out_ref[...] = dot(turned_ref[...], right_ref[...]).astype(BF16)


def turned_weight_kernel(turned_ref, right_ref, out_ref):
    out_ref[...] = dot(turned_ref[...], right_ref[...]).astype(BF16)


def weight_grad(left, right, begin, end, turned=False, block=512):
    total = right.shape[0]
    width = left.shape[0] if turned else left.shape[1]
    blocks = end - begin
    out = pl.BlockSpec((width, block), lambda i: (0, i))
    shapes = [jax.ShapeDtypeStruct((width, blocks * block), BF16), pltpu.HBM((width, total), BF16)]
    outs = pl.pallas_call(
        turned_weight_kernel if turned else weight_kernel,
        grid=(blocks,),
        in_specs=[
            whole(left.shape),
            pl.BlockSpec((total, block), lambda i: (0, i + begin)),
        ],
        out_specs=[out] if turned else [out, whole((width, total))],
        out_shape=shapes[:1] if turned else shapes,
        compiler_params=params(24),
        cost_estimate=cost(2 * total * width * blocks * block, 7 * MIB),
        name="weight_grad",
    )(in_hbm(left), in_hbm(right))
    return outs[0] if turned else outs


def sides_kernel(turned, lows, low_ref, low_far_ref, high_ref, high_far_ref, out_ref):
    low = pl.program_id(0) < lows
    own = jnp.where(low, low_ref[...], high_ref[...]).astype(F32)
    far = jnp.where(low, low_far_ref[...], high_far_ref[...]).astype(F32)
    out_ref[...] = (own + far).T if turned else own + far


def sides_sum(low, low_far, high, high_far, turned, block=512):
    width, columns = low.shape[0], low.shape[1] + high.shape[1]
    blocks = low.shape[1] // block
    lows = pl.BlockSpec((width, block), lambda i: (0, jnp.minimum(i, blocks - 1)))
    highs = pl.BlockSpec((width, block), lambda i: (0, jnp.maximum(i - blocks, 0)))
    if turned:
        shape, out = (columns, width), pl.BlockSpec((block, width), lambda i: (i, 0))
    else:
        shape, out = (width, columns), pl.BlockSpec((width, block), lambda i: (0, i))
    return pl.pallas_call(
        functools.partial(sides_kernel, turned, blocks),
        grid=(columns // block,),
        in_specs=[lows, lows, highs, highs],
        out_specs=out,
        out_shape=jax.ShapeDtypeStruct(shape, F32),
        compiler_params=params(20),
        cost_estimate=cost(width * columns, 8 * width * columns),
        name="sides_sum",
    )(in_hbm(low), low_far, in_hbm(high), high_far)


def combine_kernel(slots_ref, y_ref, resid_ref, out_ref, moment_ref):
    step, total = out_ref.shape[0], y_ref.shape[0]
    places = lax.broadcasted_iota(jnp.int32, (step, total), 1)
    moe = dot(hits((slots_ref[:, 0:1], slots_ref[:, 1:2]), places), y_ref[...])
    out_ref[...] = (resid_ref[...] + moe).astype(BF16)
    moment = jnp.sum(moe * moe, 0, keepdims=True)
    moment_ref[...] = jnp.where(pl.program_id(0) == 0, 0.0, moment_ref[...]) + moment


def combine_rows(slot_columns, y, resid, step):
    tokens, width = resid.shape
    total = y.shape[0]
    block = lambda size: pl.BlockSpec((step, size), lambda i: (i, 0))
    return pl.pallas_call(
        combine_kernel,
        grid=(tokens // step,),
        in_specs=[block(TOP), whole(y.shape), block(width)],
        out_specs=[block(width), whole((1, width))],
        out_shape=[
            jax.ShapeDtypeStruct((tokens, width), BF16),
            jax.ShapeDtypeStruct((1, width), F32),
        ],
        compiler_params=params(24),
        cost_estimate=cost(2 * total * tokens * width, 8 * MIB),
        name="combine_rows",
    )(slot_columns, y, in_hbm(resid))


def token_back_kernel(
    capacity,
    slots,
    experts,
    later,
    flag_ref,
    *refs,
):
    me = flag_ref[2]
    backs, refs = refs[:experts], refs[experts:]
    if later:
        unused, attn_ref, router_ref_sum, gain_ref_sum, *refs = refs
    (
        columns_ref,
        lines_ref,
        resid_ref,
        normed_ref,
        heads_ref,
        up_ref,
        w_out_ref,
        router_ref,
        gain_ref,
        d_resid_out,
        d_heads_out,
        attn_sum,
        gain_sum,
        router_out,
        d_weights,
        back_ref,
        near_router,
        router_sum,
    ) = refs
    step, width = resid_ref.shape
    total = back_ref.shape[0]
    first = pl.program_id(0) == 0

    @pl.when(first)
    def columns():
        near_router[...] = jnp.concatenate(
            [router_ref[pl.ds(e ^ me, 1), :] for e in range(experts)], 0
        ).astype(BF16)
        row = lax.broadcasted_iota(jnp.int32, (slots, 256), 0)
        lane = lax.broadcasted_iota(jnp.int32, (slots, 256), 1)
        for e in range(0, experts, 2):
            pair = [backs[e][...].astype(F32), backs[e + 1][...].astype(F32)]
            back_ref[e * slots : (e + 2) * slots, :] = jnp.concatenate(pair, 0).astype(BF16)
        for e in range(experts):
            block = backs[e][:, 0:256].astype(F32)
            line = jnp.sum(jnp.where(row >= capacity, block, 0.0), 0, keepdims=True)
            column = jnp.sum(jnp.where(row == lane, line, 0.0), -1, keepdims=True)
            d_weights[e * slots : (e + 1) * slots, :] = jnp.broadcast_to(column, (slots, step))

    def accumulate(ref, value, given_ref=None):
        given = 0.0 if given_ref is None else given_ref[...]
        ref[...] = jnp.where(first, given, ref[...]) + value

    line_slots = (lines_ref[0:1, :], lines_ref[1:2, :])
    d_gates = []
    for e in range(experts):
        places = lax.broadcasted_iota(jnp.int32, (slots, step), 0) + e * slots
        hit = (places == line_slots[0]) | (places == line_slots[1])
        d_gates.append(
            jnp.sum(
                jnp.where(hit, d_weights[e * slots : (e + 1) * slots, :], 0.0), 0, keepdims=True
            )
        )
    d_gates = jnp.concatenate(d_gates, 0)
    logits = dot(near_router[...], normed_ref[...], 1, 1)
    gates = jnp.exp(logits - jnp.max(logits, 0, keepdims=True))
    gates = gates / jnp.sum(gates, 0, keepdims=True)
    d_logits = (gates * (d_gates - jnp.sum(gates * d_gates, 0, keepdims=True))).astype(BF16)
    places = lax.broadcasted_iota(jnp.int32, (step, total), 1)
    d_normed = dot(hits((columns_ref[:, 0:1], columns_ref[:, 1:2]), places), back_ref[...])
    d_normed += dot(d_logits, near_router[...], 0, 0)
    normed, inverse = normalize(resid_ref[...])
    d_resid = up_ref[...].astype(F32) + norm_back(d_normed * gain_ref[...], normed, inverse)
    d_attn = d_resid.astype(BF16)
    d_resid_out[...] = d_resid
    d_heads_out[...] = dot(d_attn, w_out_ref[...], 1, 1).astype(BF16)
    accumulate(attn_sum, dot(heads_ref[...], d_attn, 0, 0), attn_ref if later else None)
    accumulate(router_sum, dot(d_logits, normed_ref[...]))
    gain_term = jnp.sum(d_normed * normed, 0, keepdims=True)
    accumulate(gain_sum, gain_term, gain_ref_sum if later else None)

    @pl.when(pl.program_id(0) == pl.num_programs(0) - 1)
    def finish():
        for e in range(experts):
            at = pl.ds(e ^ me, 1)
            given = router_ref_sum[at, :] if later else 0.0
            router_out[at, :] = router_sum[e : e + 1, :] + given


def token_back(
    flag,
    mine,
    kept,
    slot_columns,
    slot_rows,
    backs,
    resid,
    normed,
    heads,
    up,
    w_attn_out,
    w_router_t,
    gain,
    capacity,
    slots,
    step,
):
    tokens, width = resid.shape
    experts = w_router_t.shape[0]
    total = experts * slots
    part = tokens // step // 2
    image = lambda i, flag_ref: i + (flag_ref[0] if mine else 1 - flag_ref[0]) * part
    block = lambda size: pl.BlockSpec((step, size), lambda i, flag_ref: (image(i, flag_ref), 0))
    sums = [(width, width), (1, width), (experts, width)]
    given = [kept[0], kept[2], kept[4], kept[3]] if kept else []
    return pl.pallas_call(
        functools.partial(token_back_kernel, capacity, slots, experts, bool(kept)),
        grid_spec=pltpu.PrefetchScalarGridSpec(
            num_scalar_prefetch=1,
            grid=(part,),
            in_specs=[whole((slots, width))] * experts
            + [pl.BlockSpec(memory_space=pl.ANY)] * (len(given) > 0)
            + [whole(value.shape) for value in given[1:]]
            + [
                block(TOP),
                pl.BlockSpec((TOP, step), lambda i, flag_ref: (0, image(i, flag_ref))),
                block(width),
                block(width),
                block(width),
                block(width),
                whole(w_attn_out.shape),
                whole(w_router_t.shape),
                whole(gain.shape),
            ],
            out_specs=[block(width), pl.BlockSpec((step, width), lambda i, flag_ref: (i, 0))]
            + [whole(shape) for shape in sums],
            scratch_shapes=[
                pltpu.VMEM((total, step), F32),
                pltpu.VMEM((total, width), BF16),
                pltpu.VMEM((experts, width), BF16),
                pltpu.VMEM((experts, width), F32),
            ],
        ),
        out_shape=[
            pltpu.HBM((tokens, width), F32),
            pltpu.HBM((part * step, width), BF16),
            pltpu.HBM((width, width), F32),
            jax.ShapeDtypeStruct((1, width), F32),
            jax.ShapeDtypeStruct((experts, width), F32),
        ],
        input_output_aliases={1 + experts: 0} if kept else {},
        compiler_params=params(30),
        cost_estimate=cost((total + 2 * width) * tokens * width, 7 * MIB),
        name="token_back",
    )(
        flag,
        *map(in_hbm, backs),
        *map(in_hbm, given),
        slot_columns,
        slot_rows,
        in_hbm(resid),
        in_hbm(normed),
        in_hbm(heads),
        in_hbm(up),
        w_attn_out,
        w_router_t,
        gain,
    )


def grad_sum_kernel(flag_ref, resid_ref, own_ref, far_ref, out_ref):
    mine = (flag_ref[0] == 0) == (pl.program_id(0) < pl.num_programs(0) // 2)
    out_ref[...] = resid_ref[...] + jnp.where(mine, own_ref[0], far_ref[0]).astype(F32)


def grad_sum(flag, d_resid, own, far):
    part, rows, width = own.shape
    tokens = d_resid.shape[0]
    pick = pl.BlockSpec((1, rows, width), lambda i, flag_ref: (lax.rem(i, part), 0, 0))
    return pl.pallas_call(
        grad_sum_kernel,
        grid_spec=pltpu.PrefetchScalarGridSpec(
            num_scalar_prefetch=1,
            grid=(tokens // rows,),
            in_specs=[pl.BlockSpec((rows, width), lambda i, flag_ref: (i, 0)), pick, pick],
            out_specs=pl.BlockSpec((rows, width), lambda i, flag_ref: (i, 0)),
        ),
        out_shape=jax.ShapeDtypeStruct((tokens, width), F32),
        compiler_params=params(16),
        cost_estimate=cost(tokens * width, 6 * MIB),
        name="grad_sum",
    )(flag, in_hbm(d_resid), own, far)


AXES = ("wide", "narrow")


def device_bits():
    n_narrow = lax.axis_size("narrow")
    masks = [1 << b for b in range((n_narrow * lax.axis_size("wide")).bit_length() - 1)]
    masks.remove(n_narrow)
    return [n_narrow] + masks


def sum_steps():
    first, *rest = device_bits()
    return [(first,)] + [tuple(rest[i : i + 2]) for i in range(0, len(rest), 2)]


def swap(value, mask, axes=AXES):
    size = math.prod(lax.axis_size(axis) for axis in axes)
    return lax.ppermute(value, axes, [(i, i ^ mask) for i in range(size)])


def partners(bits):
    me = lax.axis_index(AXES)
    place = sum(((me // bit) % 2) << b for b, bit in enumerate(bits))
    masks = [
        sum(bit for b, bit in enumerate(bits) if (j >> b) & 1) for j in range(1 << len(bits))
    ]
    return masks, place


def fold_kernel(given, members, place_ref, keep_ref, *refs):
    del place_ref
    step = pl.program_id(0)
    total = keep_ref[...]
    for far_ref in refs[:given]:
        total += far_ref[...].astype(F32)
    own_out, *send_outs = refs[given:]

    @pl.when(step == 0)
    def keep():
        own_out[...] = total

    for j, send_out in enumerate(send_outs):

        @pl.when(step == j + 1)
        def send():
            send_out[...] = total.astype(BF16)


def fold(keep, far, bits):
    masks, place = partners(bits)
    members = len(masks)
    rows, size = keep.shape
    part = rows // members
    pick = pl.BlockSpec((part, size), lambda j, place_ref: (place_ref[0] ^ j, 0))
    own, *send = pl.pallas_call(
        functools.partial(fold_kernel, len(far), members),
        grid_spec=pltpu.PrefetchScalarGridSpec(
            num_scalar_prefetch=1,
            grid=(members,),
            in_specs=[pick] * (1 + len(far)),
            out_specs=[whole((part, size))] * members,
        ),
        out_shape=[jax.ShapeDtypeStruct((part, size), F32)]
        + [jax.ShapeDtypeStruct((part, size), BF16)] * (members - 1),
        compiler_params=params(32),
        cost_estimate=cost(0, 8 * rows * size),
        name="fold",
    )(place.reshape(1).astype(jnp.int32), in_hbm(keep), *far)
    return own, [swap(value, mask) for value, mask in zip(send, masks[1:])]


def sum_parts(value, bits):
    masks, place = partners(bits)
    part = value.shape[0] // len(masks)
    pick = lambda j: lax.dynamic_slice_in_dim(value, (place ^ j) * part, part, 0)
    far = [swap(pick(j).astype(BF16), masks[j]) for j in range(1, len(masks))]
    total = pick(0)
    for term in far:
        total = total + term.astype(F32)
    return total


def spread_parts(value, bits):
    masks, place = partners(bits)
    parts = [value] + [swap(value, mask) for mask in masks[1:]]
    for b in range(len(bits)):
        side = (place >> b) % 2 == 0
        parts = [
            jnp.where(
                side,
                jnp.concatenate([parts[i], parts[i + 1]], 0),
                jnp.concatenate([parts[i + 1], parts[i]], 0),
            )
            for i in range(0, len(parts), 2)
        ]
    return parts[0]


def close_kernel(keep_ref, moment_ref, *refs):
    total = keep_ref[...]
    for far_ref in refs[:-1]:
        total += far_ref[...].astype(F32)
    row = lax.broadcasted_iota(jnp.int32, total.shape, 0)
    lane = lax.broadcasted_iota(jnp.int32, total.shape, 1) - (total.shape[1] - 2)
    moment = jnp.sum(moment_ref[...], 1, keepdims=True)
    high = moment.astype(BF16).astype(F32)
    extra = jnp.where(lane == 0, high, moment - high)
    refs[-1][...] = jnp.where((row == 0) & (lane >= 0), extra, total).astype(BF16)


def close(keep, far, moment):
    return pl.pallas_call(
        close_kernel,
        out_shape=jax.ShapeDtypeStruct(keep.shape, BF16),
        compiler_params=params(16),
        cost_estimate=cost(0, 8 * keep.size),
        name="close",
    )(keep, moment, *far)


def add_kernel(*refs):
    terms = [ref[...].astype(F32) for ref in refs[:-1]]
    while len(terms) > 1:
        terms = [terms[i] + terms[i + 1] for i in range(0, len(terms), 2)]
    refs[-1][...] = terms[0].astype(BF16)


def add(terms):
    return pl.pallas_call(
        add_kernel,
        out_shape=jax.ShapeDtypeStruct(terms[0].shape, BF16),
        compiler_params=params(16),
        cost_estimate=cost(0, 2 * len(terms) * terms[0].size),
        name="add",
    )(*terms)


def apart_kernel(experts, count, flag_ref, own_ref, far_ref, qkv_out, attn_out, router_out, *outs):
    gain_one_out, gain_two_out, stats_out, small = outs
    half, width = own_ref.shape[0], attn_out.shape[1]
    upper = flag_ref[1] == 1
    own, far = own_ref[...].astype(F32), far_ref[...].astype(F32)
    for rows, value in ((0, jnp.where(upper, far, own)), (half, jnp.where(upper, own, far))):
        rows = slice(rows, rows + half)
        qkv_out[rows, :] = value[:, : 3 * width]
        attn_out[rows, :] = value[:, 3 * width : 4 * width]
        small[rows, :] = value[:, 4 * width :]
    values = small[...]
    lines = values.T
    router_out[...] = lines[:experts]
    gain_two_out[...] = lines[experts : experts + 1, :]
    gain_one_out[...] = lines[experts + 3 : experts + 4, :]
    sums = jnp.sum(lines, 1, keepdims=True)
    moments = (
        sums[experts + 1 : experts + 2],
        sums[experts + 2 : experts + 3],
        sums[SMALL - 2 : SMALL - 1] + sums[SMALL - 1 :],
    )
    lane = lax.broadcasted_iota(jnp.int32, stats_out.shape, 1)
    stats = jnp.where(lane == 0, moments[0], jnp.where(lane == 1, moments[1], moments[2]))
    stats_out[...] = jnp.sqrt(stats / count + EPS)


def sums_apart(flag, own, far, experts, count):
    width = 2 * own.shape[0]
    shapes = [(width, 3 * width), (width, width), (experts, width), (1, width), (1, width), (1, 128)]
    return pl.pallas_call(
        functools.partial(apart_kernel, experts, count),
        grid_spec=pltpu.PrefetchScalarGridSpec(
            num_scalar_prefetch=1,
            grid=(1,),
            in_specs=[whole(own.shape), whole(far.shape)],
            out_specs=[whole(shape) for shape in shapes],
            scratch_shapes=[pltpu.VMEM((width, SMALL), F32)],
        ),
        out_shape=[jax.ShapeDtypeStruct(shape, F32) for shape in shapes],
        compiler_params=params(32),
        cost_estimate=cost(0, 8 * MIB),
        name="sums_apart",
    )(flag, own, far)


def gathered_attention(inputs, gain_one, w_qkv):
    images, rows_dev, width = inputs.shape
    tokens = images * rows_dev
    head_dim = width // HEADS
    scale = head_dim ** (-0.5)
    seq_len = rows_dev * lax.axis_size("narrow")
    group = math.gcd(images, max(1, 512 // rows_dev))
    blocks = images // group
    normed_one, inverse_one = normalize(inputs.astype(F32).reshape(tokens, width))
    input_one = (normed_one * gain_one).astype(BF16)
    projected = jnp.dot(input_one, w_qkv, preferred_element_type=F32).astype(BF16)
    queries = projected[:, :width].reshape(images, rows_dev, width)
    keys_own = projected[:, width : 2 * width].reshape(images, rows_dev, width)
    values_own = projected[:, 2 * width :].reshape(images, rows_dev, width)
    keys_all = lax.all_gather(keys_own, "narrow", axis=1, tiled=True)
    values_all = lax.all_gather(values_own, "narrow", axis=1, tiled=True)
    query_blocks = queries.reshape(blocks, group, rows_dev, HEADS, head_dim)
    key_blocks = keys_all.reshape(blocks, group, seq_len, HEADS, head_dim)
    value_blocks = values_all.reshape(blocks, group, seq_len, HEADS, head_dim)

    def attend_block(operands):
        query_b, key_b, value_b = operands
        scores = jnp.einsum("gqhd,gkhd->ghqk", query_b, key_b, preferred_element_type=F32) * scale
        top_score = jnp.max(scores, -1, keepdims=True)
        exponent = jnp.exp(scores - top_score)
        total = jnp.sum(exponent, -1, keepdims=True)
        weights = (exponent / total).astype(BF16)
        mixed = jnp.einsum("ghqk,gkhd->gqhd", weights, value_b, preferred_element_type=F32)
        return (mixed.astype(BF16), (top_score + jnp.log(total))[..., 0])

    heads_out, log_total = lax.map(attend_block, (query_blocks, key_blocks, value_blocks))

    def back_block(operands):
        query_b, key_b, value_b, total_b, d_head_b = operands
        scores = jnp.einsum("gqhd,gkhd->ghqk", query_b, key_b, preferred_element_type=F32) * scale
        weights = jnp.exp(scores - total_b[..., None])
        d_weights = jnp.einsum("gqhd,gkhd->ghqk", d_head_b, value_b, preferred_element_type=F32)
        spread = jnp.sum(weights * d_weights, -1, keepdims=True)
        d_scores = (weights * (d_weights - spread)).astype(BF16)
        d_query = jnp.einsum("ghqk,gkhd->gqhd", d_scores, key_b, preferred_element_type=F32) * scale
        d_key = jnp.einsum("ghqk,gqhd->gkhd", d_scores, query_b, preferred_element_type=F32) * scale
        d_value = jnp.einsum(
            "ghqk,gqhd->gkhd", weights.astype(BF16), d_head_b, preferred_element_type=F32
        )
        return (d_query.astype(BF16), d_key, d_value)

    def back(d_heads, d_resid):
        d_head_blocks = d_heads.reshape(blocks, group, rows_dev, HEADS, head_dim)
        d_queries, key_terms, value_terms = lax.map(
            back_block, (query_blocks, key_blocks, value_blocks, log_total, d_head_blocks)
        )
        d_keys, d_values = (
            lax.psum_scatter(
                terms.reshape(images, seq_len, width), "narrow", scatter_dimension=1, tiled=True
            )
            .astype(BF16)
            .reshape(tokens, width)
            for terms in (key_terms, value_terms)
        )
        d_projected = jnp.concatenate([d_queries.reshape(tokens, width), d_keys, d_values], 1)
        d_weight = jnp.dot(input_one.T, d_projected, preferred_element_type=F32)
        d_input = jnp.dot(d_projected, w_qkv.T, preferred_element_type=F32)
        d_gain = jnp.sum(d_input * normed_one, 0, keepdims=True)
        return (
            d_resid + norm_back(d_input * gain_one, normed_one, inverse_one),
            d_weight,
            d_gain,
        )

    return heads_out.reshape(images, rows_dev, width), back


def shards(
    inputs,
    cotangent,
    ln1_gain,
    w_qkv,
    w_attn_out,
    ln2_gain,
    w_router,
    expert_in,
    expert_in_bias,
    expert_out,
    expert_out_bias,
    route_ids,
    route_slots,
    route_dropped,
):
    images, rows_dev, width = inputs.shape
    tokens = images * rows_dev
    experts = w_router.shape[1]
    n_wide = lax.axis_size("wide")
    n_narrow = lax.axis_size("narrow")
    capacity = max(2, 42 * tokens // (20 * experts))
    slots = -(-(capacity + 2) // 8) * 8
    total = experts * slots
    gain_one = ln1_gain.astype(F32).reshape(1, width)
    gain_two = ln2_gain.astype(F32).reshape(1, width)
    paired = n_narrow == 2 and images % 2 == 0
    part = images // 2
    place = lax.axis_index("narrow") if paired else jnp.int32(0)
    me = lax.axis_index("wide")
    flag = jnp.stack([place, me % 2, me])

    slot_columns = jnp.where(
        route_dropped == 0, route_ids * slots + route_slots, -1
    ).reshape(tokens, TOP)
    slot_rows = slot_columns.T
    near_columns = jnp.where(
        route_dropped == 0, (route_ids ^ me) * slots + route_slots, -1
    ).reshape(tokens, TOP)
    near_rows = near_columns.T
    up = cotangent.reshape(tokens, width)

    def exchange(rows):
        return lax.all_to_all(
            rows.reshape(experts, slots, width), "wide", split_axis=0, concat_axis=0, tiled=True
        ).reshape(total, width)

    up_rows = dispatch_rows(slot_rows, up, total)
    if paired:
        pick = lambda k: lax.dynamic_slice_in_dim(inputs, (1 - place) * part + k, 1, 0)
        far_inputs = [swap(pick(0), 1)]
        far_inputs[0], up_rows = lax.optimization_barrier((far_inputs[0], up_rows))
        far_inputs += [swap(pick(k), 1) for k in range(1, part)]
    up_here = exchange(up_rows)

    if paired:
        w_qkv_t = w_qkv.T
        heads_own, heads_far, saved = [], [], []
        for k, far in enumerate(far_inputs):
            own_heads, far_heads, *saved = attend(
                flag, inputs, k, far, gain_one, w_qkv_t, saved
            )
            heads_own.append(own_heads)
            heads_far.append(swap(far_heads, 1))
        proj, log_total = saved
    else:
        heads_own, attention_back = gathered_attention(inputs, gain_one, w_qkv)
        heads_own = [heads_own[k : k + 1] for k in range(images)]
        heads_own, heads_far = heads_own[:part], heads_own[part:]

    heads, resid, normed_two, moments = residual_rows(
        flag, heads_own, heads_far, inputs, w_attn_out, gain_two
    )
    w_in, w_out = expert_in[0], expert_out[0]
    up_here = up_here.reshape(experts, slots, width)

    def expert(blocks, first, kept):
        return expert_group(
            me.reshape(1),
            blocks,
            first,
            up_here,
            w_router.T,
            w_in,
            expert_in_bias,
            w_out,
            expert_out_bias,
            capacity,
            kept,
        )

    def after(value, *others):
        return lax.optimization_barrier((value,) + others)[0]

    half = experts // 2
    quarter = half // 2
    send = lambda block, k: swap(block, k, ("wide",)) if k else block
    near_blocks = dispatch_blocks(near_rows, normed_two, 0, half, slots)
    blocks = dispatch_blocks(near_rows, after(normed_two, near_blocks[0]), half, half, slots)
    cross = [send(block, half + k) for k, block in enumerate(blocks[:2])]
    local = []
    for k, block in enumerate(near_blocks):
        local.append(send(after(block, local[k - 3]) if k > 3 else block, k))
    kept, sums_a, backs_a = expert(local, 0, [])
    for k in range(2, half):
        gate = local[k + half - EARLY] if k < EARLY else sums_a[1]
        cross.append(send(after(blocks[k], gate), half + k))
    backs_a = [send(block, k) for k, block in enumerate(backs_a)]
    kept, sums_b, backs_b = expert(cross[:quarter], half, kept)
    backs_b = [send(block, half + k) for k, block in enumerate(backs_b)]
    last = cross[quarter:]
    last[0] = after(last[0], *backs_a[1:6])
    kept, sums_c, backs_c = expert(last, half + quarter, kept)
    y, rows_here, act, d_hidden, d_y = kept
    y = y.reshape(total, width)
    last_block = w_in.shape[1] // 512
    low_out, d_y_t = weight_grad(after(d_y, *backs_b[:2]), act, 0, MIDDLE)
    grad_out = [low_out]
    backs_c = [
        send(after(block, grad_out[0]), half + quarter + k) for k, block in enumerate(backs_c)
    ]
    d_y_t = after(d_y_t, grad_out[0], *backs_b[2:], *backs_a[6:])
    grad_out.append(weight_grad(d_y_t, act, MIDDLE, last_block, True))
    rows_here = after(rows_here, grad_out[1], *backs_c[:2])
    low_in, rows_t = weight_grad(rows_here, d_hidden, 0, LATE)
    grad_in = [low_in]
    b_in_sum, b_out_sum = (sum(terms) for terms in zip(sums_a, sums_b, sums_c))
    backs = backs_a + backs_b + backs_c
    far_out = [swap(part_grad, 1) for part_grad in grad_out] if n_narrow == 2 else []
    backs[-1] = after(backs[-1], *grad_in)

    def back_to_tokens(mine, kept):
        return token_back(
            flag,
            mine,
            kept,
            near_columns,
            near_rows,
            backs,
            resid,
            normed_two,
            heads,
            up,
            w_attn_out,
            w_router.T.astype(F32),
            gain_two,
            capacity,
            slots,
            rows_dev,
        )

    first = back_to_tokens(False, [])
    sent = first[1]
    d_resid, d_heads, attn_term, gain_two_term, router_term = back_to_tokens(True, first)
    sent, grad_in[0] = lax.optimization_barrier((sent, grad_in[0]))
    biases = jnp.concatenate([b_in_sum, b_out_sum], 1)
    small = jnp.concatenate([router_term, gain_two_term, moments], 0)
    count = tokens * width * n_wide * n_narrow
    steps = sum_steps()
    if paired:
        d_far = swap(sent.reshape(part, rows_dev, width), 1)
        far_in = [swap(grad_in[0], 1)]
        far_biases = swap(biases, 1)
        y = exchange(after(y, sent))
        d_far, *far_out = lax.optimization_barrier((d_far, *far_out))
        d_own, d_far, keep, send = attend_back(
            flag,
            inputs,
            far_inputs,
            gain_one,
            w_qkv_t,
            proj,
            log_total,
            d_heads.reshape(part, rows_dev, width),
            d_far,
            attn_term,
            small,
        )
        sums, far = fold(keep, [swap(send, steps[0][0])], steps[1])
        block_out, moe_moment = combine_rows(slot_columns, after(y, sums), resid, rows_dev)
        grad_in.append(weight_grad(after(rows_t, sums), d_hidden, LATE, last_block, True))
        far_in.append(swap(grad_in[1], 1))
        far[0], moe_moment, far_biases, far_in[0], *unused = lax.optimization_barrier(
            (far[0], moe_moment, far_biases, far_in[0], grad_in[1])
        )
        biases = biases + far_biases
        bias_outs = (biases[:, : w_in.shape[1]], biases[:, w_in.shape[1] :])
        sums = close(sums, far, moe_moment)
        d_far = swap(after(d_far, sums), 1)
        for bits in steps[2:]:
            masks, unused = partners(bits)
            terms = [sums] + [swap(sums, mask) for mask in masks[1:]]
            grad_expert_out = sides_sum(
                grad_out[0], far_out[0], grad_out[1], after(far_out[1], sums), True
            )
            terms[1], grad_expert_out, *bias_outs = lax.optimization_barrier(
                (terms[1], grad_expert_out, *bias_outs)
            )
            sums = add(terms)
        sums, d_far, far_in[1] = lax.optimization_barrier((sums, d_far, far_in[1]))
        input_grad = grad_sum(flag, d_resid, d_own, d_far)
        grad_expert_in = sides_sum(grad_in[0], far_in[0], grad_in[1], far_in[1], False)
        sums = spread_parts(sums, steps[1])
        sums, input_grad, grad_expert_in = lax.optimization_barrier(
            (sums, input_grad, grad_expert_in)
        )
    else:
        y = exchange(y)
        grad_in.append(weight_grad(rows_t, d_hidden, LATE, last_block, True))
        grad_out, grad_in = lax.psum((grad_out, grad_in), "narrow")
        grad_expert_out = jnp.concatenate(grad_out, 1).astype(F32).T
        grad_expert_in = jnp.concatenate(grad_in, 1).astype(F32)
        biases = lax.psum(biases, "narrow")
        bias_outs = (biases[:, : w_in.shape[1]], biases[:, w_in.shape[1] :])
        d_heads = jnp.concatenate([d_heads, sent], 0)
        input_grad, qkv_term, gain_one_term = attention_back(d_heads, d_resid)
        small = small_columns(small, gain_one_term)
        sums = jnp.concatenate([qkv_term, attn_term, small], 1)
        for bits in steps:
            sums = sum_parts(sums, bits)
        block_out, moe_moment = combine_rows(slot_columns, y, resid, rows_dev)
        sums = close(sums, [], moe_moment)
        for bits in reversed(steps[1:]):
            sums = spread_parts(sums, bits)
    grad_qkv, grad_attn_out, grad_router, grad_gain_one, grad_gain_two, stats = sums_apart(
        flag, sums, swap(sums, steps[0][0]), experts, count
    )
    return (
        block_out.reshape(images, rows_dev, width),
        input_grad.reshape(images, rows_dev, width),
        grad_gain_one.reshape(width),
        grad_qkv,
        grad_attn_out,
        grad_gain_two.reshape(width),
        grad_router.T,
        grad_expert_in[None],
        bias_outs[0],
        grad_expert_out[None],
        bias_outs[1],
        stats[0, :3],
    )


def solution(mesh):
    return jax.shard_map(
        shards,
        mesh=mesh,
        in_specs=(
            P("wide", "narrow", None),
            P("wide", "narrow", None),
            P(),
            P(),
            P(),
            P(),
            P(),
            P("wide", None, None),
            P("wide", None),
            P("wide", None, None),
            P("wide", None),
            P("wide", "narrow", None),
            P("wide", "narrow", None),
            P("wide", "narrow", None),
        ),
        out_specs=(
            P("wide", "narrow", None),
            P("wide", "narrow", None),
            P(),
            P(),
            P(),
            P(),
            P(),
            P("wide", None, None),
            P("wide", None),
            P("wide", None, None),
            P("wide", None),
            P(),
        ),
        check_vma=False,
    )
```

```python
import functools
import math

import jax
import jax.numpy as jnp
from jax import lax
from jax.experimental import pallas as pl
from jax.experimental.pallas import tpu as pltpu
from jax.sharding import PartitionSpec as P

HEADS = 8
TOP = 2


EPS = 1e-06
BF16 = jnp.bfloat16
F32 = jnp.float32
MIB = 1 << 20
SMALL = 128
EARLY = 5
MIDDLE = 2
LATE = 3


def normalize(values):
    centre = jnp.mean(values, -1, keepdims=True)
    shifted = values - centre
    inverse = lax.rsqrt(jnp.mean(shifted * shifted, -1, keepdims=True) + EPS)
    return (shifted * inverse, inverse)


def norm_back(d_normed, normed, inverse):
    return inverse * (
        d_normed
        - jnp.mean(d_normed, -1, keepdims=True)
        - normed * jnp.mean(d_normed * normed, -1, keepdims=True)
    )


def dot(left, right, left_dim=1, right_dim=0):
    return lax.dot_general(
        left, right, (((left_dim,), (right_dim,)), ((), ())), preferred_element_type=F32
    )


def params(mib):
    return pltpu.CompilerParams(vmem_limit_bytes=mib * MIB)


def in_hbm(value):
    return pltpu.with_memory_space_constraint(value, pltpu.HBM)


def in_vmem(value):
    return pltpu.with_memory_space_constraint(value, pltpu.VMEM)


def cost(flops, bytes_accessed, transcendentals=0):
    return pl.CostEstimate(
        flops=int(flops), bytes_accessed=int(bytes_accessed), transcendentals=int(transcendentals)
    )


def whole(shape):
    return pl.BlockSpec(shape, lambda *unused: (0,) * len(shape))


def hits(slots, places):
    first, second = slots
    return jnp.where((places == first) | (places == second), 1.0, 0.0).astype(BF16)


def put_rows(slots_ref, rows_ref, out_ref):
    step = out_ref.shape[0]
    places = lax.broadcasted_iota(jnp.int32, (step, rows_ref.shape[0]), 0) + pl.program_id(0) * step
    out_ref[...] = dot(hits((slots_ref[0:1, :], slots_ref[1:2, :]), places), rows_ref[...]).astype(
        BF16
    )


def dispatch_rows(slot_rows, rows, total, steps=8):
    tokens, width = rows.shape
    step = total // steps
    return pl.pallas_call(
        put_rows,
        grid=(steps,),
        in_specs=[whole(slot_rows.shape), whole(rows.shape)],
        out_specs=pl.BlockSpec((step, width), lambda i: (i, 0)),
        out_shape=jax.ShapeDtypeStruct((total, width), BF16),
        compiler_params=params(20),
        cost_estimate=cost(2 * total * tokens * width, 4 * total * width),
        name="dispatch_rows",
    )(slot_rows, rows)


def attend_kernel(flag_ref, own_ref, far_ref, gain_ref, wt_ref, *refs):
    del flag_ref
    own_out, far_out, proj_ref, total_ref, mixed = refs[-5:]
    rows, width = own_ref.shape[1], own_ref.shape[2]
    head_dim = width // HEADS
    scale = head_dim ** (-0.5)
    x_float = jnp.concatenate([own_ref[0], far_ref[0]], 0).astype(F32)
    normed, unused = normalize(x_float)
    normed = (normed * gain_ref[...]).astype(BF16)
    proj_ref[0] = dot(wt_ref[...], normed, 1, 1).astype(BF16)

    def head(h, carry):
        at = pl.multiple_of(h * head_dim, head_dim)
        query = proj_ref[0, pl.ds(at, head_dim), :]
        key = proj_ref[0, pl.ds(at + width, head_dim), :]
        value = proj_ref[0, pl.ds(at + 2 * width, head_dim), :]
        scores = dot(key, query * scale, 0, 0)
        top = jnp.max(scores, 0, keepdims=True)
        exponent = jnp.exp(scores - top)
        total = jnp.sum(exponent, 0, keepdims=True)
        out = dot(value, exponent.astype(BF16)) * (1.0 / total)
        mixed[pl.ds(at, head_dim), :] = out
        total_ref[0, pl.ds(h, 1), :] = top + jnp.log(total)
        return carry

    lax.fori_loop(0, HEADS, head, 0, unroll=4)
    heads_out = mixed[...].T.astype(BF16)
    own_out[0] = heads_out[:rows]
    far_out[0] = heads_out[rows:]


def attend(flag, inputs, image, far, gain, w_qkv_t, kept):
    unused, rows, width = far.shape
    seq_len = 2 * rows
    part = inputs.shape[0] // 2
    block = lambda k, *shape: pl.BlockSpec((1,) + shape, lambda i, flag_ref: (k,) + (0,) * len(shape))
    return pl.pallas_call(
        attend_kernel,
        grid_spec=pltpu.PrefetchScalarGridSpec(
            num_scalar_prefetch=1,
            grid=(1,),
            in_specs=[
                pl.BlockSpec(
                    (1, rows, width), lambda i, flag_ref: (image + flag_ref[0] * part, 0, 0)
                ),
                block(0, rows, width),
                whole(gain.shape),
                whole(w_qkv_t.shape),
            ]
            + [pl.BlockSpec(memory_space=pl.ANY)] * len(kept),
            out_specs=[
                block(0, rows, width),
                block(0, rows, width),
                block(image, 3 * width, seq_len),
                block(image, HEADS, seq_len),
            ],
            scratch_shapes=[pltpu.VMEM((width, seq_len), F32)],
        ),
        out_shape=[
            jax.ShapeDtypeStruct((1, rows, width), BF16),
            jax.ShapeDtypeStruct((1, rows, width), BF16),
            pltpu.HBM((part, 3 * width, seq_len), BF16),
            pltpu.HBM((part, HEADS, seq_len), F32),
        ],
        input_output_aliases={5 + i: 2 + i for i in range(len(kept))},
        compiler_params=params(28),
        cost_estimate=cost(8e9, 8 * MIB, HEADS * seq_len**2),
        name="attend",
    )(flag, in_hbm(inputs), far, gain, w_qkv_t, *kept)


def small_columns(small, gain):
    rest = jnp.zeros((SMALL - small.shape[0] - 1, small.shape[1]), F32)
    return jnp.concatenate([small, gain, rest], 0).T


def attend_back_kernel(
    part,
    flag_ref,
    own_ref,
    *refs,
):
    far_refs, refs = refs[:part], refs[part:]
    attend_back_body(flag_ref, own_ref, far_refs, *refs)


def attend_back_body(
    flag_ref,
    own_ref,
    far_refs,
    gain_ref,
    wt_ref,
    proj_ref,
    total_ref,
    d_own_ref,
    d_far_ref,
    attn_ref,
    small_ref,
    own_out,
    far_out,
    keep_out,
    send_out,
    d_proj,
    d_mixed,
    weight_sum,
    gain_out,
    small_sum,
):
    image, last = pl.program_id(0), pl.num_programs(0) - 1
    rows, width = own_ref.shape[1], own_ref.shape[2]
    head_dim = width // HEADS
    scale = head_dim ** (-0.5)
    d_mixed[...] = jnp.concatenate([d_own_ref[0], d_far_ref[0]], 0).astype(F32).T.astype(BF16)

    def head(h, carry):
        at = pl.multiple_of(h * head_dim, head_dim)
        query = proj_ref[0, pl.ds(at, head_dim), :]
        key = proj_ref[0, pl.ds(at + width, head_dim), :]
        value = proj_ref[0, pl.ds(at + 2 * width, head_dim), :]
        d_out = d_mixed[pl.ds(at, head_dim), :]
        weights = jnp.exp(dot(key, query * scale, 0, 0) - total_ref[0, pl.ds(h, 1), :])
        product = weights * dot(value, d_out, 0, 0)
        spread = jnp.sum(product, 0, keepdims=True)
        d_scores = (product - weights * spread).astype(BF16)
        d_proj[pl.ds(at, head_dim), :] = (dot(key, d_scores) * scale).astype(BF16)
        d_proj[pl.ds(at + width, head_dim), :] = (dot(query, d_scores, 1, 1) * scale).astype(BF16)
        d_proj[pl.ds(at + 2 * width, head_dim), :] = dot(d_out, weights.astype(BF16), 1, 1).astype(
            BF16
        )
        return carry

    lax.fori_loop(0, HEADS, head, 0, unroll=1)
    far = far_refs[0][0]
    for k, far_ref in enumerate(far_refs[1:]):
        far = jnp.where(image == k + 1, far_ref[0], far)
    x_float = jnp.concatenate([own_ref[0], far], 0).astype(F32)
    normed, inverse = normalize(x_float)
    d_input = dot(d_proj[...], wt_ref[...], 0, 0)
    weight_term = dot((normed * gain_ref[...]).T.astype(BF16), d_proj[...], 1, 1)
    gain_term = jnp.sum(d_input * normed, 0, keepdims=True)
    d_x = norm_back(d_input * gain_ref[...], normed, inverse).astype(BF16)
    own_out[0] = d_x[:rows]
    far_out[0] = d_x[rows:]

    @pl.when(image == 0)
    def start():
        weight_sum[...] = weight_term
        gain_out[...] = gain_term

    @pl.when(image != 0)
    def add():
        weight_sum[...] += weight_term
        gain_out[...] += gain_term

    @pl.when(image == last)
    def finish():
        half = width // 2
        small_sum[...] = small_columns(small_ref[...], gain_out[...])
        near = pl.ds(pl.multiple_of(flag_ref[1] * half, half), half)
        away = pl.ds(pl.multiple_of((1 - flag_ref[1]) * half, half), half)
        for ref, at in ((weight_sum, 0), (attn_ref, 3 * width), (small_sum, 4 * width)):
            at = slice(at, at + ref.shape[1])
            keep_out[:, at] = ref[near, :]
            send_out[:, at] = ref[away, :].astype(BF16)


def attend_back(flag, inputs, far, gain, w_qkv_t, proj, total, d_heads, d_far, attn_term, small):
    part = len(far)
    unused, rows, width = far[0].shape
    seq_len = 2 * rows
    block = lambda *shape: pl.BlockSpec((1,) + shape, lambda i, flag_ref: (i,) + (0,) * len(shape))
    return pl.pallas_call(
        functools.partial(attend_back_kernel, part),
        grid_spec=pltpu.PrefetchScalarGridSpec(
            num_scalar_prefetch=1,
            grid=(part,),
            in_specs=[
                pl.BlockSpec((1, rows, width), lambda i, flag_ref: (i + flag_ref[0] * part, 0, 0)),
            ]
            + [whole((1, rows, width))] * part
            + [
                whole(gain.shape),
                whole(w_qkv_t.shape),
                block(3 * width, seq_len),
                block(HEADS, seq_len),
                block(rows, width),
                block(rows, width),
                whole(attn_term.shape),
                whole(small.shape),
            ],
            out_specs=[
                block(rows, width),
                block(rows, width),
                whole((width // 2, 4 * width + SMALL)),
                whole((width // 2, 4 * width + SMALL)),
            ],
            scratch_shapes=[
                pltpu.VMEM((3 * width, seq_len), BF16),
                pltpu.VMEM((width, seq_len), BF16),
                pltpu.VMEM((width, 3 * width), F32),
                pltpu.VMEM((1, width), F32),
                pltpu.VMEM((width, SMALL), F32),
            ],
        ),
        out_shape=[
            pltpu.HBM((part, rows, width), BF16),
            pltpu.HBM((part, rows, width), BF16),
            pltpu.HBM((width // 2, 4 * width + SMALL), F32),
            jax.ShapeDtypeStruct((width // 2, 4 * width + SMALL), BF16),
        ],
        compiler_params=params(36),
        cost_estimate=cost(part * 16e9, 12 * MIB, part * HEADS * seq_len**2),
        name="attend_back",
    )(
        flag,
        in_hbm(inputs),
        *map(in_hbm, far),
        gain,
        in_hbm(w_qkv_t),
        in_hbm(proj),
        total,
        in_hbm(d_heads),
        d_far,
        in_hbm(attn_term),
        small,
    )


def pick_image(flag_ref, image, images, own_refs, far_refs):
    part = images // 2
    mine = (flag_ref[0] == 0) == (image < part)
    value = jnp.where(mine, own_refs[0][0], far_refs[0][0])
    for k in range(1, part):
        other = jnp.where(mine, own_refs[k][0], far_refs[k][0])
        value = jnp.where(lax.rem(image, part) == k, other, value)
    return value


def residual_kernel(images, flag_ref, *refs):
    own_refs, far_refs, refs = refs[: images // 2], refs[images // 2 : images], refs[images:]
    x_ref, w_out_ref, gain_ref, heads_out, resid_out, normed_out, moments_out = refs
    image = pl.program_id(0)
    heads = pick_image(flag_ref, image, images, own_refs, far_refs)
    attn = dot(heads, w_out_ref[...])
    resid = x_ref[0].astype(F32) + attn
    normed, unused = normalize(resid)
    heads_out[...] = heads
    resid_out[...] = resid
    normed_out[...] = (normed * gain_ref[...]).astype(BF16)
    moments = [jnp.sum(value * value, 0, keepdims=True) for value in (resid, attn)]
    moments_out[...] = jnp.where(image == 0, 0.0, moments_out[...]) + jnp.concatenate(moments, 0)


def residual_rows(flag, own, far, inputs, w_attn_out, gain):
    images, rows, width = inputs.shape
    tokens = images * rows
    block = pl.BlockSpec((rows, width), lambda i, flag_ref: (i, 0))
    return pl.pallas_call(
        functools.partial(residual_kernel, images),
        grid_spec=pltpu.PrefetchScalarGridSpec(
            num_scalar_prefetch=1,
            grid=(images,),
            in_specs=[whole((1, rows, width))] * images
            + [
                pl.BlockSpec((1, rows, width), lambda i, flag_ref: (i, 0, 0)),
                whole(w_attn_out.shape),
                whole(gain.shape),
            ],
            out_specs=[block, block, block, whole((2, width))],
        ),
        out_shape=[
            pltpu.HBM((tokens, width), BF16),
            pltpu.HBM((tokens, width), F32),
            jax.ShapeDtypeStruct((tokens, width), BF16),
            jax.ShapeDtypeStruct((2, width), F32),
        ],
        compiler_params=params(24),
        cost_estimate=cost(2 * width * tokens * width, 10 * MIB),
        name="residual_rows",
    )(flag, *own, *far, in_hbm(inputs), w_attn_out, gain)


def blocks_kernel(first, slots_ref, rows_ref, *out_refs):
    for k, out_ref in enumerate(out_refs):
        shape = (out_ref.shape[0], rows_ref.shape[0])
        places = lax.broadcasted_iota(jnp.int32, shape, 0) + (first + k) * out_ref.shape[0]
        hit = hits((slots_ref[0:1, :], slots_ref[1:2, :]), places)
        out_ref[...] = dot(hit, rows_ref[...]).astype(BF16)


def dispatch_blocks(slot_rows, rows, first, count, slots):
    tokens, width = rows.shape
    return pl.pallas_call(
        functools.partial(blocks_kernel, first),
        out_shape=[pltpu.HBM((slots, width), BF16)] * count,
        compiler_params=params(16),
        cost_estimate=cost(2 * count * slots * tokens * width, 4 * count * slots * width),
        name="dispatch_blocks",
    )(slot_rows, rows)


def expert_kernel(capacity, count, kept, me_ref, *refs):
    blocks, refs = refs[:count], refs[count:]
    up_ref, router_ref, w_in_ref, b_in_ref, w_out_ref, b_out_ref, *refs = refs
    y_out, rows_out, act_out, d_hidden_out, d_y_out, b_in_sum, b_out_sum, *refs = refs[kept:]
    backs, pair = refs[:count], refs[count]
    slots, width = blocks[0].shape
    step = 2 * slots
    hidden_width = w_in_ref.shape[1]
    chunk = 512
    index = pl.program_id(0)
    odd = me_ref[0] % 2 == 1
    for i in range(count // 2):

        @pl.when(index == i)
        def load():
            both = [blocks[2 * i][...].astype(F32), blocks[2 * i + 1][...].astype(F32)]
            pair[...] = jnp.concatenate(both, 0).astype(BF16)

    rows = pair[...]
    rows_out[...] = rows
    logits = dot(rows, router_ref[...], 1, 1)
    gate = jnp.exp(logits - jnp.max(logits, -1, keepdims=True))
    mine = lax.broadcasted_iota(jnp.int32, gate.shape, 1) == me_ref[0]
    total = jnp.sum(gate, -1, keepdims=True)
    gate = jnp.sum(jnp.where(mine, gate, 0.0), -1, keepdims=True) / total
    low, high = up_ref[0].astype(F32), up_ref[1].astype(F32)
    up_float = jnp.concatenate([jnp.where(odd, high, low), jnp.where(odd, low, high)], 0)
    d_y = (gate * up_float).astype(BF16)
    d_y_out[...] = d_y
    y = jnp.zeros((step, width), F32)
    back = jnp.zeros((step, width), F32)

    def accumulate(ref, at, value):
        ref[:, at] = jnp.where(index == 0, 0.0, ref[:, at]) + jnp.sum(
            value.astype(F32), 0, keepdims=True
        )

    for c in range(hidden_width // chunk):
        at = slice(c * chunk, (c + 1) * chunk)
        hidden = dot(rows, w_in_ref[:, at]) + b_in_ref[:, at].astype(F32)
        square = hidden * hidden
        root = math.sqrt(2.0 / math.pi)
        slope = jnp.tanh(hidden * (root + (root * 0.044715) * square))
        half = 0.5 * (1.0 + slope)
        act = (hidden * half).astype(BF16)
        d_gelu = half + (0.5 * hidden) * (1.0 - slope * slope) * (
            root + (3.0 * root * 0.044715) * square
        )
        d_hidden = (dot(d_y, w_out_ref[at, :], 1, 1) * d_gelu).astype(BF16)
        act_out[:, at] = act
        d_hidden_out[:, at] = d_hidden
        y += dot(act, w_out_ref[at, :])
        back += dot(d_hidden, w_in_ref[:, at], 1, 1)
        accumulate(b_in_sum, at, d_hidden)
    accumulate(b_out_sum, slice(0, width), d_y)
    y = (y + b_out_ref[...].astype(F32)).astype(BF16).astype(F32)
    d_weight = jnp.sum(y * up_float, -1, keepdims=True)
    y = y * gate
    y_out[0] = jnp.where(odd, y[slots:], y[:slots]).astype(BF16)
    y_out[1] = jnp.where(odd, y[:slots], y[slots:]).astype(BF16)
    row = lax.broadcasted_iota(jnp.int32, (step, width), 0)
    lane = lax.broadcasted_iota(jnp.int32, (step, width), 1)
    for s in range(2):
        line = jnp.sum(jnp.where(row - s * slots == lane, d_weight, 0.0), 0, keepdims=True)
        line = jnp.where(lane[:1] < capacity, line, 0.0)
        top = line.astype(BF16).astype(F32)
        back = jnp.where(row == s * slots + capacity, top, back)
        back = jnp.where(row == s * slots + capacity + 1, line - top, back)
    for i in range(count // 2):

        @pl.when(index == i)
        def store():
            backs[2 * i][...] = back[:slots].astype(BF16)
            backs[2 * i + 1][...] = back[slots:].astype(BF16)


def expert_group(me, blocks, first, up, w_router, w_in, b_in, w_out, b_out, capacity, kept):
    count = len(blocks)
    slots, width = blocks[0].shape
    sources = up.shape[0]
    total = sources * slots
    hidden_width = w_in.shape[1]
    step = 2 * slots
    begin = first // 2
    rows = lambda size: pl.BlockSpec((step, size), lambda i, me_ref: (i + begin, 0))
    sides = pl.BlockSpec((2, slots, width), lambda i, me_ref: ((me_ref[0] // 2) ^ (i + begin), 0, 0))
    anywhere = pl.BlockSpec(memory_space=pl.ANY)
    given = 1 + count + 6
    shapes = [
        pltpu.HBM((sources, slots, width), BF16),
        pltpu.HBM((total, width), BF16),
        pltpu.HBM((total, hidden_width), BF16),
        pltpu.HBM((total, hidden_width), BF16),
        pltpu.HBM((total, width), BF16),
    ]
    outs = pl.pallas_call(
        functools.partial(expert_kernel, capacity, count, len(kept)),
        grid_spec=pltpu.PrefetchScalarGridSpec(
            num_scalar_prefetch=1,
            grid=(count // 2,),
            in_specs=[whole((slots, width))] * count
            + [sides]
            + [whole(a.shape) for a in (w_router, w_in, b_in, w_out, b_out)]
            + [anywhere] * len(kept),
            out_specs=[sides, rows(width), rows(hidden_width), rows(hidden_width), rows(width)]
            + [whole((1, hidden_width)), whole((1, width))]
            + [whole((slots, width))] * count,
            scratch_shapes=[pltpu.VMEM((step, width), BF16)],
        ),
        out_shape=shapes
        + [jax.ShapeDtypeStruct((1, hidden_width), F32), jax.ShapeDtypeStruct((1, width), F32)]
        + [jax.ShapeDtypeStruct((slots, width), BF16)] * count,
        input_output_aliases={given + i: i for i in range(len(kept))},
        compiler_params=params(28),
        cost_estimate=cost(8 * count * slots * width * hidden_width, 8 * MIB),
        name="expert_group",
    )(me, *map(in_hbm, blocks), in_hbm(up), w_router, w_in, b_in, w_out, b_out, *kept)
    return outs[:5], outs[5:7], list(outs[7:])


def weight_kernel(left_ref, right_ref, out_ref, turned_ref):
    @pl.when(pl.program_id(0) == 0)
    def turn():
        turned_ref[...] = left_ref[...].T

    out_ref[...] = dot(turned_ref[...], right_ref[...]).astype(BF16)


def turned_weight_kernel(turned_ref, right_ref, out_ref):
    out_ref[...] = dot(turned_ref[...], right_ref[...]).astype(BF16)


def weight_grad(left, right, begin, end, turned=False, pinned=False, block=512):
    total = right.shape[0]
    width = left.shape[0] if turned else left.shape[1]
    blocks = end - begin
    out = pl.BlockSpec((width, block), lambda i: (0, i))
    kind = pltpu.HBM if pinned else jax.ShapeDtypeStruct
    shapes = [kind((width, blocks * block), BF16), pltpu.HBM((width, total), BF16)]
    outs = pl.pallas_call(
        turned_weight_kernel if turned else weight_kernel,
        grid=(blocks,),
        in_specs=[
            whole(left.shape),
            pl.BlockSpec((total, block), lambda i: (0, i + begin)),
        ],
        out_specs=[out] if turned else [out, whole((width, total))],
        out_shape=shapes[:1] if turned else shapes,
        compiler_params=params(24),
        cost_estimate=cost(2 * total * width * blocks * block, 7 * MIB),
        name="weight_grad",
    )(in_hbm(left), in_hbm(right))
    return outs[0] if turned else outs


def sides_kernel(turned, lows, low_ref, low_far_ref, high_ref, high_far_ref, out_ref):
    low = pl.program_id(0) < lows
    own = jnp.where(low, low_ref[...], high_ref[...]).astype(F32)
    far = jnp.where(low, low_far_ref[...], high_far_ref[...]).astype(F32)
    out_ref[...] = (own + far).T if turned else own + far


def sides_sum(low, low_far, high, high_far, turned, block=512):
    width, columns = low.shape[0], low.shape[1] + high.shape[1]
    blocks = low.shape[1] // block
    lows = pl.BlockSpec((width, block), lambda i: (0, jnp.minimum(i, blocks - 1)))
    highs = pl.BlockSpec((width, block), lambda i: (0, jnp.maximum(i - blocks, 0)))
    if turned:
        shape, out = (columns, width), pl.BlockSpec((block, width), lambda i: (i, 0))
    else:
        shape, out = (width, columns), pl.BlockSpec((width, block), lambda i: (0, i))
    return pl.pallas_call(
        functools.partial(sides_kernel, turned, blocks),
        grid=(columns // block,),
        in_specs=[lows, lows, highs, highs],
        out_specs=out,
        out_shape=jax.ShapeDtypeStruct(shape, F32),
        compiler_params=params(20),
        cost_estimate=cost(width * columns, 8 * width * columns),
        name="sides_sum",
    )(in_hbm(low), low_far, in_hbm(high), high_far)


def combine_kernel(slots_ref, y_ref, resid_ref, out_ref, moment_ref):
    step, total = out_ref.shape[0], y_ref.shape[0]
    places = lax.broadcasted_iota(jnp.int32, (step, total), 1)
    moe = dot(hits((slots_ref[:, 0:1], slots_ref[:, 1:2]), places), y_ref[...])
    out_ref[...] = (resid_ref[...] + moe).astype(BF16)
    moment = jnp.sum(moe * moe, 0, keepdims=True)
    moment_ref[...] = jnp.where(pl.program_id(0) == 0, 0.0, moment_ref[...]) + moment


def combine_rows(slot_columns, y, resid, step):
    tokens, width = resid.shape
    total = y.shape[0]
    block = lambda size: pl.BlockSpec((step, size), lambda i: (i, 0))
    return pl.pallas_call(
        combine_kernel,
        grid=(tokens // step,),
        in_specs=[block(TOP), whole(y.shape), block(width)],
        out_specs=[block(width), whole((1, width))],
        out_shape=[
            jax.ShapeDtypeStruct((tokens, width), BF16),
            jax.ShapeDtypeStruct((1, width), F32),
        ],
        compiler_params=params(24),
        cost_estimate=cost(2 * total * tokens * width, 8 * MIB),
        name="combine_rows",
    )(slot_columns, y, in_hbm(resid))


def token_back_kernel(
    capacity,
    slots,
    experts,
    later,
    flag_ref,
    *refs,
):
    me = flag_ref[2]
    backs, refs = refs[:experts], refs[experts:]
    if later:
        unused, attn_ref, router_ref_sum, gain_ref_sum, *refs = refs
    (
        columns_ref,
        lines_ref,
        resid_ref,
        normed_ref,
        heads_ref,
        up_ref,
        w_out_ref,
        router_ref,
        gain_ref,
        d_resid_out,
        d_heads_out,
        attn_sum,
        gain_sum,
        router_out,
        d_weights,
        back_ref,
        near_router,
        router_sum,
    ) = refs
    step, width = resid_ref.shape
    total = back_ref.shape[0]
    first = pl.program_id(0) == 0

    @pl.when(first)
    def columns():
        near_router[...] = jnp.concatenate(
            [router_ref[pl.ds(e ^ me, 1), :] for e in range(experts)], 0
        ).astype(BF16)
        row = lax.broadcasted_iota(jnp.int32, (slots, 256), 0)
        lane = lax.broadcasted_iota(jnp.int32, (slots, 256), 1)
        for e in range(0, experts, 2):
            pair = [backs[e][...].astype(F32), backs[e + 1][...].astype(F32)]
            back_ref[e * slots : (e + 2) * slots, :] = jnp.concatenate(pair, 0).astype(BF16)
        for e in range(experts):
            block = backs[e][:, 0:256].astype(F32)
            line = jnp.sum(jnp.where(row >= capacity, block, 0.0), 0, keepdims=True)
            column = jnp.sum(jnp.where(row == lane, line, 0.0), -1, keepdims=True)
            d_weights[e * slots : (e + 1) * slots, :] = jnp.broadcast_to(column, (slots, step))

    def accumulate(ref, value, given_ref=None):
        given = 0.0 if given_ref is None else given_ref[...]
        ref[...] = jnp.where(first, given, ref[...]) + value

    line_slots = (lines_ref[0:1, :], lines_ref[1:2, :])
    d_gates = []
    for e in range(experts):
        places = lax.broadcasted_iota(jnp.int32, (slots, step), 0) + e * slots
        hit = (places == line_slots[0]) | (places == line_slots[1])
        d_gates.append(
            jnp.sum(
                jnp.where(hit, d_weights[e * slots : (e + 1) * slots, :], 0.0), 0, keepdims=True
            )
        )
    d_gates = jnp.concatenate(d_gates, 0)
    logits = dot(near_router[...], normed_ref[...], 1, 1)
    gates = jnp.exp(logits - jnp.max(logits, 0, keepdims=True))
    gates = gates / jnp.sum(gates, 0, keepdims=True)
    d_logits = (gates * (d_gates - jnp.sum(gates * d_gates, 0, keepdims=True))).astype(BF16)
    places = lax.broadcasted_iota(jnp.int32, (step, total), 1)
    d_normed = dot(hits((columns_ref[:, 0:1], columns_ref[:, 1:2]), places), back_ref[...])
    d_normed += dot(d_logits, near_router[...], 0, 0)
    normed, inverse = normalize(resid_ref[...])
    d_resid = up_ref[...].astype(F32) + norm_back(d_normed * gain_ref[...], normed, inverse)
    d_attn = d_resid.astype(BF16)
    d_resid_out[...] = d_resid
    d_heads_out[...] = dot(d_attn, w_out_ref[...], 1, 1).astype(BF16)
    accumulate(attn_sum, dot(heads_ref[...], d_attn, 0, 0), attn_ref if later else None)
    accumulate(router_sum, dot(d_logits, normed_ref[...]))
    gain_term = jnp.sum(d_normed * normed, 0, keepdims=True)
    accumulate(gain_sum, gain_term, gain_ref_sum if later else None)

    @pl.when(pl.program_id(0) == pl.num_programs(0) - 1)
    def finish():
        for e in range(experts):
            at = pl.ds(e ^ me, 1)
            given = router_ref_sum[at, :] if later else 0.0
            router_out[at, :] = router_sum[e : e + 1, :] + given


def token_back(
    flag,
    mine,
    kept,
    slot_columns,
    slot_rows,
    backs,
    resid,
    normed,
    heads,
    up,
    w_attn_out,
    w_router_t,
    gain,
    capacity,
    slots,
    step,
):
    tokens, width = resid.shape
    experts = w_router_t.shape[0]
    total = experts * slots
    part = tokens // step // 2
    image = lambda i, flag_ref: i + (flag_ref[0] if mine else 1 - flag_ref[0]) * part
    block = lambda size: pl.BlockSpec((step, size), lambda i, flag_ref: (image(i, flag_ref), 0))
    sums = [(width, width), (1, width), (experts, width)]
    given = [kept[0], kept[2], kept[4], kept[3]] if kept else []
    return pl.pallas_call(
        functools.partial(token_back_kernel, capacity, slots, experts, bool(kept)),
        grid_spec=pltpu.PrefetchScalarGridSpec(
            num_scalar_prefetch=1,
            grid=(part,),
            in_specs=[whole((slots, width))] * experts
            + [pl.BlockSpec(memory_space=pl.ANY)] * (len(given) > 0)
            + [whole(value.shape) for value in given[1:]]
            + [
                block(TOP),
                pl.BlockSpec((TOP, step), lambda i, flag_ref: (0, image(i, flag_ref))),
                block(width),
                block(width),
                block(width),
                block(width),
                whole(w_attn_out.shape),
                whole(w_router_t.shape),
                whole(gain.shape),
            ],
            out_specs=[block(width), pl.BlockSpec((step, width), lambda i, flag_ref: (i, 0))]
            + [whole(shape) for shape in sums],
            scratch_shapes=[
                pltpu.VMEM((total, step), F32),
                pltpu.VMEM((total, width), BF16),
                pltpu.VMEM((experts, width), BF16),
                pltpu.VMEM((experts, width), F32),
            ],
        ),
        out_shape=[
            pltpu.HBM((tokens, width), F32),
            pltpu.HBM((part * step, width), BF16),
            pltpu.HBM((width, width), F32),
            jax.ShapeDtypeStruct((1, width), F32),
            jax.ShapeDtypeStruct((experts, width), F32),
        ],
        input_output_aliases={1 + experts: 0} if kept else {},
        compiler_params=params(30),
        cost_estimate=cost((total + 2 * width) * tokens * width, 7 * MIB),
        name="token_back",
    )(
        flag,
        *map(in_hbm, backs),
        *map(in_hbm, given),
        slot_columns,
        slot_rows,
        in_hbm(resid),
        in_hbm(normed),
        in_hbm(heads),
        in_hbm(up),
        w_attn_out,
        w_router_t,
        gain,
    )


def grad_sum_kernel(flag_ref, resid_ref, own_ref, far_ref, out_ref):
    mine = (flag_ref[0] == 0) == (pl.program_id(0) < pl.num_programs(0) // 2)
    out_ref[...] = resid_ref[...] + jnp.where(mine, own_ref[0], far_ref[0]).astype(F32)


def grad_sum(flag, d_resid, own, far):
    part, rows, width = own.shape
    tokens = d_resid.shape[0]
    pick = pl.BlockSpec((1, rows, width), lambda i, flag_ref: (lax.rem(i, part), 0, 0))
    return pl.pallas_call(
        grad_sum_kernel,
        grid_spec=pltpu.PrefetchScalarGridSpec(
            num_scalar_prefetch=1,
            grid=(tokens // rows,),
            in_specs=[pl.BlockSpec((rows, width), lambda i, flag_ref: (i, 0)), pick, pick],
            out_specs=pl.BlockSpec((rows, width), lambda i, flag_ref: (i, 0)),
        ),
        out_shape=jax.ShapeDtypeStruct((tokens, width), F32),
        compiler_params=params(16),
        cost_estimate=cost(tokens * width, 6 * MIB),
        name="grad_sum",
    )(flag, in_hbm(d_resid), own, far)


AXES = ("wide", "narrow")


def device_bits():
    n_narrow = lax.axis_size("narrow")
    masks = [1 << b for b in range((n_narrow * lax.axis_size("wide")).bit_length() - 1)]
    masks.remove(n_narrow)
    return [n_narrow] + masks


def sum_steps():
    first, *rest = device_bits()
    return [(first,)] + [tuple(rest[i : i + 2]) for i in range(0, len(rest), 2)]


def swap(value, mask, axes=AXES):
    size = math.prod(lax.axis_size(axis) for axis in axes)
    return lax.ppermute(value, axes, [(i, i ^ mask) for i in range(size)])


def partners(bits):
    me = lax.axis_index(AXES)
    place = sum(((me // bit) % 2) << b for b, bit in enumerate(bits))
    masks = [
        sum(bit for b, bit in enumerate(bits) if (j >> b) & 1) for j in range(1 << len(bits))
    ]
    return masks, place


def fold_kernel(given, members, place_ref, keep_ref, *refs):
    del place_ref
    step = pl.program_id(0)
    total = keep_ref[...]
    for far_ref in refs[:given]:
        total += far_ref[...].astype(F32)
    own_out, *send_outs = refs[given:]

    @pl.when(step == 0)
    def keep():
        own_out[...] = total

    for j, send_out in enumerate(send_outs):

        @pl.when(step == j + 1)
        def send():
            send_out[...] = total.astype(BF16)


def fold(keep, far, bits):
    masks, place = partners(bits)
    members = len(masks)
    rows, size = keep.shape
    part = rows // members
    pick = pl.BlockSpec((part, size), lambda j, place_ref: (place_ref[0] ^ j, 0))
    own, *send = pl.pallas_call(
        functools.partial(fold_kernel, len(far), members),
        grid_spec=pltpu.PrefetchScalarGridSpec(
            num_scalar_prefetch=1,
            grid=(members,),
            in_specs=[pick] * (1 + len(far)),
            out_specs=[whole((part, size))] * members,
        ),
        out_shape=[jax.ShapeDtypeStruct((part, size), F32)]
        + [jax.ShapeDtypeStruct((part, size), BF16)] * (members - 1),
        compiler_params=params(32),
        cost_estimate=cost(0, 8 * rows * size),
        name="fold",
    )(place.reshape(1).astype(jnp.int32), in_hbm(keep), *far)
    return own, [swap(value, mask) for value, mask in zip(send, masks[1:])]


def sum_parts(value, bits):
    masks, place = partners(bits)
    part = value.shape[0] // len(masks)
    pick = lambda j: lax.dynamic_slice_in_dim(value, (place ^ j) * part, part, 0)
    far = [swap(pick(j).astype(BF16), masks[j]) for j in range(1, len(masks))]
    total = pick(0)
    for term in far:
        total = total + term.astype(F32)
    return total


def spread_parts(value, bits):
    masks, place = partners(bits)
    parts = [value] + [swap(value, mask) for mask in masks[1:]]
    for b in range(len(bits)):
        side = (place >> b) % 2 == 0
        parts = [
            jnp.where(
                side,
                jnp.concatenate([parts[i], parts[i + 1]], 0),
                jnp.concatenate([parts[i + 1], parts[i]], 0),
            )
            for i in range(0, len(parts), 2)
        ]
    return parts[0]


def close_kernel(keep_ref, moment_ref, *refs):
    total = keep_ref[...]
    for far_ref in refs[:-1]:
        total += far_ref[...].astype(F32)
    row = lax.broadcasted_iota(jnp.int32, total.shape, 0)
    lane = lax.broadcasted_iota(jnp.int32, total.shape, 1) - (total.shape[1] - 2)
    moment = jnp.sum(moment_ref[...], 1, keepdims=True)
    high = moment.astype(BF16).astype(F32)
    extra = jnp.where(lane == 0, high, moment - high)
    refs[-1][...] = jnp.where((row == 0) & (lane >= 0), extra, total).astype(BF16)


def close(keep, far, moment):
    return pl.pallas_call(
        close_kernel,
        out_shape=jax.ShapeDtypeStruct(keep.shape, BF16),
        compiler_params=params(16),
        cost_estimate=cost(0, 8 * keep.size),
        name="close",
    )(keep, moment, *far)


def add_kernel(*refs):
    terms = [ref[...].astype(F32) for ref in refs[:-1]]
    while len(terms) > 1:
        terms = [terms[i] + terms[i + 1] for i in range(0, len(terms), 2)]
    refs[-1][...] = terms[0].astype(BF16)


def add(terms):
    return pl.pallas_call(
        add_kernel,
        out_shape=jax.ShapeDtypeStruct(terms[0].shape, BF16),
        compiler_params=params(16),
        cost_estimate=cost(0, 2 * len(terms) * terms[0].size),
        name="add",
    )(*terms)


def apart_kernel(experts, count, flag_ref, own_ref, far_ref, qkv_out, attn_out, router_out, *outs):
    gain_one_out, gain_two_out, stats_out, small = outs
    half, width = own_ref.shape[0], attn_out.shape[1]
    upper = flag_ref[1] == 1
    own, far = own_ref[...].astype(F32), far_ref[...].astype(F32)
    for rows, value in ((0, jnp.where(upper, far, own)), (half, jnp.where(upper, own, far))):
        rows = slice(rows, rows + half)
        qkv_out[rows, :] = value[:, : 3 * width]
        attn_out[rows, :] = value[:, 3 * width : 4 * width]
        small[rows, :] = value[:, 4 * width :]
    values = small[...]
    lines = values.T
    router_out[...] = lines[:experts]
    gain_two_out[...] = lines[experts : experts + 1, :]
    gain_one_out[...] = lines[experts + 3 : experts + 4, :]
    sums = jnp.sum(lines, 1, keepdims=True)
    moments = (
        sums[experts + 1 : experts + 2],
        sums[experts + 2 : experts + 3],
        sums[SMALL - 2 : SMALL - 1] + sums[SMALL - 1 :],
    )
    lane = lax.broadcasted_iota(jnp.int32, stats_out.shape, 1)
    stats = jnp.where(lane == 0, moments[0], jnp.where(lane == 1, moments[1], moments[2]))
    stats_out[...] = jnp.sqrt(stats / count + EPS)


def sums_apart(flag, own, far, experts, count):
    width = 2 * own.shape[0]
    shapes = [(width, 3 * width), (width, width), (experts, width), (1, width), (1, width), (1, 128)]
    return pl.pallas_call(
        functools.partial(apart_kernel, experts, count),
        grid_spec=pltpu.PrefetchScalarGridSpec(
            num_scalar_prefetch=1,
            grid=(1,),
            in_specs=[whole(own.shape), whole(far.shape)],
            out_specs=[whole(shape) for shape in shapes],
            scratch_shapes=[pltpu.VMEM((width, SMALL), F32)],
        ),
        out_shape=[jax.ShapeDtypeStruct(shape, F32) for shape in shapes],
        compiler_params=params(32),
        cost_estimate=cost(0, 8 * MIB),
        name="sums_apart",
    )(flag, own, far)


def gathered_attention(inputs, gain_one, w_qkv):
    images, rows_dev, width = inputs.shape
    tokens = images * rows_dev
    head_dim = width // HEADS
    scale = head_dim ** (-0.5)
    seq_len = rows_dev * lax.axis_size("narrow")
    group = math.gcd(images, max(1, 512 // rows_dev))
    blocks = images // group
    normed_one, inverse_one = normalize(inputs.astype(F32).reshape(tokens, width))
    input_one = (normed_one * gain_one).astype(BF16)
    projected = jnp.dot(input_one, w_qkv, preferred_element_type=F32).astype(BF16)
    queries = projected[:, :width].reshape(images, rows_dev, width)
    keys_own = projected[:, width : 2 * width].reshape(images, rows_dev, width)
    values_own = projected[:, 2 * width :].reshape(images, rows_dev, width)
    keys_all = lax.all_gather(keys_own, "narrow", axis=1, tiled=True)
    values_all = lax.all_gather(values_own, "narrow", axis=1, tiled=True)
    query_blocks = queries.reshape(blocks, group, rows_dev, HEADS, head_dim)
    key_blocks = keys_all.reshape(blocks, group, seq_len, HEADS, head_dim)
    value_blocks = values_all.reshape(blocks, group, seq_len, HEADS, head_dim)

    def attend_block(operands):
        query_b, key_b, value_b = operands
        scores = jnp.einsum("gqhd,gkhd->ghqk", query_b, key_b, preferred_element_type=F32) * scale
        top_score = jnp.max(scores, -1, keepdims=True)
        exponent = jnp.exp(scores - top_score)
        total = jnp.sum(exponent, -1, keepdims=True)
        weights = (exponent / total).astype(BF16)
        mixed = jnp.einsum("ghqk,gkhd->gqhd", weights, value_b, preferred_element_type=F32)
        return (mixed.astype(BF16), (top_score + jnp.log(total))[..., 0])

    heads_out, log_total = lax.map(attend_block, (query_blocks, key_blocks, value_blocks))

    def back_block(operands):
        query_b, key_b, value_b, total_b, d_head_b = operands
        scores = jnp.einsum("gqhd,gkhd->ghqk", query_b, key_b, preferred_element_type=F32) * scale
        weights = jnp.exp(scores - total_b[..., None])
        d_weights = jnp.einsum("gqhd,gkhd->ghqk", d_head_b, value_b, preferred_element_type=F32)
        spread = jnp.sum(weights * d_weights, -1, keepdims=True)
        d_scores = (weights * (d_weights - spread)).astype(BF16)
        d_query = jnp.einsum("ghqk,gkhd->gqhd", d_scores, key_b, preferred_element_type=F32) * scale
        d_key = jnp.einsum("ghqk,gqhd->gkhd", d_scores, query_b, preferred_element_type=F32) * scale
        d_value = jnp.einsum(
            "ghqk,gqhd->gkhd", weights.astype(BF16), d_head_b, preferred_element_type=F32
        )
        return (d_query.astype(BF16), d_key, d_value)

    def back(d_heads, d_resid):
        d_head_blocks = d_heads.reshape(blocks, group, rows_dev, HEADS, head_dim)
        d_queries, key_terms, value_terms = lax.map(
            back_block, (query_blocks, key_blocks, value_blocks, log_total, d_head_blocks)
        )
        d_keys, d_values = (
            lax.psum_scatter(
                terms.reshape(images, seq_len, width), "narrow", scatter_dimension=1, tiled=True
            )
            .astype(BF16)
            .reshape(tokens, width)
            for terms in (key_terms, value_terms)
        )
        d_projected = jnp.concatenate([d_queries.reshape(tokens, width), d_keys, d_values], 1)
        d_weight = jnp.dot(input_one.T, d_projected, preferred_element_type=F32)
        d_input = jnp.dot(d_projected, w_qkv.T, preferred_element_type=F32)
        d_gain = jnp.sum(d_input * normed_one, 0, keepdims=True)
        return (
            d_resid + norm_back(d_input * gain_one, normed_one, inverse_one),
            d_weight,
            d_gain,
        )

    return heads_out.reshape(images, rows_dev, width), back


def shards(
    inputs,
    cotangent,
    ln1_gain,
    w_qkv,
    w_attn_out,
    ln2_gain,
    w_router,
    expert_in,
    expert_in_bias,
    expert_out,
    expert_out_bias,
    route_ids,
    route_slots,
    route_dropped,
):
    images, rows_dev, width = inputs.shape
    tokens = images * rows_dev
    experts = w_router.shape[1]
    n_wide = lax.axis_size("wide")
    n_narrow = lax.axis_size("narrow")
    capacity = max(2, 42 * tokens // (20 * experts))
    slots = -(-(capacity + 2) // 8) * 8
    total = experts * slots
    gain_one = ln1_gain.astype(F32).reshape(1, width)
    gain_two = ln2_gain.astype(F32).reshape(1, width)
    paired = n_narrow == 2 and images % 2 == 0
    part = images // 2
    place = lax.axis_index("narrow") if paired else jnp.int32(0)
    me = lax.axis_index("wide")
    flag = jnp.stack([place, me % 2, me])

    slot_columns = jnp.where(
        route_dropped == 0, route_ids * slots + route_slots, -1
    ).reshape(tokens, TOP)
    slot_rows = slot_columns.T
    near_columns = jnp.where(
        route_dropped == 0, (route_ids ^ me) * slots + route_slots, -1
    ).reshape(tokens, TOP)
    near_rows = near_columns.T
    up = cotangent.reshape(tokens, width)

    def exchange(rows):
        return lax.all_to_all(
            rows.reshape(experts, slots, width), "wide", split_axis=0, concat_axis=0, tiled=True
        ).reshape(total, width)

    up_rows = dispatch_rows(slot_rows, up, total)
    if paired:
        pick = lambda k: lax.dynamic_slice_in_dim(inputs, (1 - place) * part + k, 1, 0)
        far_inputs = [swap(pick(0), 1)]
        far_inputs[0], up_rows = lax.optimization_barrier((far_inputs[0], up_rows))
        far_inputs += [swap(pick(k), 1) for k in range(1, part)]
    up_here = exchange(up_rows)

    if paired:
        w_qkv_t = w_qkv.T
        heads_own, heads_far, saved = [], [], []
        for k, far in enumerate(far_inputs):
            own_heads, far_heads, *saved = attend(
                flag, inputs, k, far, gain_one, w_qkv_t, saved
            )
            heads_own.append(own_heads)
            heads_far.append(swap(far_heads, 1))
        proj, log_total = saved
    else:
        heads_own, attention_back = gathered_attention(inputs, gain_one, w_qkv)
        heads_own = [heads_own[k : k + 1] for k in range(images)]
        heads_own, heads_far = heads_own[:part], heads_own[part:]

    heads, resid, normed_two, moments = residual_rows(
        flag, heads_own, heads_far, inputs, w_attn_out, gain_two
    )
    w_in, w_out = expert_in[0], expert_out[0]
    up_here = up_here.reshape(experts, slots, width)

    def expert(blocks, first, kept):
        return expert_group(
            me.reshape(1),
            blocks,
            first,
            up_here,
            w_router.T,
            w_in,
            expert_in_bias,
            w_out,
            expert_out_bias,
            capacity,
            kept,
        )

    def after(value, *others):
        return lax.optimization_barrier((value,) + others)[0]

    half = experts // 2
    quarter = half // 2
    send = lambda block, k: swap(block, k, ("wide",)) if k else block
    near_blocks = dispatch_blocks(near_rows, normed_two, 0, half, slots)
    blocks = dispatch_blocks(near_rows, after(normed_two, near_blocks[0]), half, half, slots)
    cross = [send(block, half + k) for k, block in enumerate(blocks[:2])]
    local = []
    for k, block in enumerate(near_blocks):
        local.append(send(after(block, local[k - 3]) if k > 3 else block, k))
    kept, sums_a, backs_a = expert(local, 0, [])
    for k in range(2, half):
        gate = local[k + half - EARLY] if k < EARLY else sums_a[1]
        cross.append(send(after(blocks[k], gate), half + k))
    backs_a = [send(block, k) for k, block in enumerate(backs_a)]
    kept, sums_b, backs_b = expert(cross[:quarter], half, kept)
    backs_b = [send(block, half + k) for k, block in enumerate(backs_b)]
    last = cross[quarter:]
    last[0] = after(last[0], *backs_a[1:6])
    kept, sums_c, backs_c = expert(last, half + quarter, kept)
    y, rows_here, act, d_hidden, d_y = kept
    y = y.reshape(total, width)
    last_block = w_in.shape[1] // 512
    low_out, d_y_t = weight_grad(after(d_y, *backs_b[:2]), act, 0, MIDDLE)
    grad_out = [low_out]
    backs_c = [
        send(after(block, grad_out[0]), half + quarter + k) for k, block in enumerate(backs_c)
    ]
    d_y_t = after(d_y_t, grad_out[0], *backs_b[2:], *backs_a[6:])
    grad_out.append(weight_grad(d_y_t, act, MIDDLE, last_block, True))
    rows_here = after(rows_here, grad_out[1], *backs_c[:2])
    low_in, rows_t = weight_grad(rows_here, d_hidden, 0, LATE, pinned=True)
    grad_in = [low_in]
    b_in_sum, b_out_sum = (sum(terms) for terms in zip(sums_a, sums_b, sums_c))
    backs = backs_a + backs_b + backs_c
    far_out = [swap(part_grad, 1) for part_grad in grad_out] if n_narrow == 2 else []
    backs[-1] = after(backs[-1], *grad_in)

    def back_to_tokens(mine, kept):
        return token_back(
            flag,
            mine,
            kept,
            near_columns,
            near_rows,
            backs,
            resid,
            normed_two,
            heads,
            up,
            w_attn_out,
            w_router.T.astype(F32),
            gain_two,
            capacity,
            slots,
            rows_dev,
        )

    first = back_to_tokens(False, [])
    sent = first[1]
    d_resid, d_heads, attn_term, gain_two_term, router_term = back_to_tokens(True, first)
    sent, grad_in[0] = lax.optimization_barrier((sent, grad_in[0]))
    biases = jnp.concatenate([b_in_sum, b_out_sum], 1)
    small = jnp.concatenate([router_term, gain_two_term, moments], 0)
    count = tokens * width * n_wide * n_narrow
    steps = sum_steps()
    if paired:
        d_far = swap(sent.reshape(part, rows_dev, width), 1)
        far_in = [swap(grad_in[0], 1)]
        far_biases = swap(biases, 1)
        y = exchange(after(y, sent))
        d_far, *far_out = lax.optimization_barrier((d_far, *far_out))
        d_own, d_far, keep, send = attend_back(
            flag,
            inputs,
            far_inputs,
            gain_one,
            w_qkv_t,
            proj,
            log_total,
            d_heads.reshape(part, rows_dev, width),
            d_far,
            attn_term,
            small,
        )
        sums, far = fold(keep, [swap(send, steps[0][0])], steps[1])
        block_out, moe_moment = combine_rows(slot_columns, after(y, sums), resid, rows_dev)
        grad_in.append(weight_grad(after(rows_t, sums), d_hidden, LATE, last_block, True))
        far_in.append(swap(grad_in[1], 1))
        far[0], moe_moment, far_biases, far_in[0], *unused = lax.optimization_barrier(
            (far[0], moe_moment, far_biases, far_in[0], grad_in[1])
        )
        biases = biases + far_biases
        bias_outs = (biases[:, : w_in.shape[1]], biases[:, w_in.shape[1] :])
        sums = close(sums, far, moe_moment)
        d_far = swap(after(d_far, sums), 1)
        for bits in steps[2:]:
            masks, unused = partners(bits)
            terms = [sums] + [swap(sums, mask) for mask in masks[1:]]
            grad_expert_out = sides_sum(
                grad_out[0], far_out[0], grad_out[1], after(far_out[1], sums), True
            )
            terms[1], grad_expert_out, *bias_outs = lax.optimization_barrier(
                (terms[1], grad_expert_out, *bias_outs)
            )
            sums = add(terms)
        sums, d_far, far_in[1] = lax.optimization_barrier((sums, d_far, far_in[1]))
        input_grad = grad_sum(flag, d_resid, d_own, d_far)
        grad_expert_in = sides_sum(grad_in[0], far_in[0], grad_in[1], far_in[1], False)
        sums = spread_parts(sums, steps[1])
        sums, input_grad, grad_expert_in = lax.optimization_barrier(
            (sums, input_grad, grad_expert_in)
        )
    else:
        y = exchange(y)
        grad_in.append(weight_grad(rows_t, d_hidden, LATE, last_block, True))
        grad_out, grad_in = lax.psum((grad_out, grad_in), "narrow")
        grad_expert_out = jnp.concatenate(grad_out, 1).astype(F32).T
        grad_expert_in = jnp.concatenate(grad_in, 1).astype(F32)
        biases = lax.psum(biases, "narrow")
        bias_outs = (biases[:, : w_in.shape[1]], biases[:, w_in.shape[1] :])
        d_heads = jnp.concatenate([d_heads, sent], 0)
        input_grad, qkv_term, gain_one_term = attention_back(d_heads, d_resid)
        small = small_columns(small, gain_one_term)
        sums = jnp.concatenate([qkv_term, attn_term, small], 1)
        for bits in steps:
            sums = sum_parts(sums, bits)
        block_out, moe_moment = combine_rows(slot_columns, y, resid, rows_dev)
        sums = close(sums, [], moe_moment)
        for bits in reversed(steps[1:]):
            sums = spread_parts(sums, bits)
    grad_qkv, grad_attn_out, grad_router, grad_gain_one, grad_gain_two, stats = sums_apart(
        flag, sums, swap(sums, steps[0][0]), experts, count
    )
    return (
        block_out.reshape(images, rows_dev, width),
        input_grad.reshape(images, rows_dev, width),
        grad_gain_one.reshape(width),
        grad_qkv,
        grad_attn_out,
        grad_gain_two.reshape(width),
        grad_router.T,
        grad_expert_in[None],
        bias_outs[0],
        grad_expert_out[None],
        bias_outs[1],
        stats[0, :3],
    )


def solution(mesh):
    return jax.shard_map(
        shards,
        mesh=mesh,
        in_specs=(
            P("wide", "narrow", None),
            P("wide", "narrow", None),
            P(),
            P(),
            P(),
            P(),
            P(),
            P("wide", None, None),
            P("wide", None),
            P("wide", None, None),
            P("wide", None),
            P("wide", "narrow", None),
            P("wide", "narrow", None),
            P("wide", "narrow", None),
        ),
        out_specs=(
            P("wide", "narrow", None),
            P("wide", "narrow", None),
            P(),
            P(),
            P(),
            P(),
            P(),
            P("wide", None, None),
            P("wide", None),
            P("wide", None, None),
            P("wide", None),
            P(),
        ),
        check_vma=False,
    )
```

```python
import functools
import math

import jax
import jax.numpy as jnp
from jax import lax
from jax.experimental import pallas as pl
from jax.experimental.pallas import tpu as pltpu
from jax.sharding import PartitionSpec as P

HEADS = 8
TOP = 2


EPS = 1e-06
BF16 = jnp.bfloat16
F32 = jnp.float32
MIB = 1 << 20
SMALL = 128
EARLY = 5
MIDDLE = 2
LATE = 3


def normalize(values):
    centre = jnp.mean(values, -1, keepdims=True)
    shifted = values - centre
    inverse = lax.rsqrt(jnp.mean(shifted * shifted, -1, keepdims=True) + EPS)
    return (shifted * inverse, inverse)


def norm_back(d_normed, normed, inverse):
    return inverse * (
        d_normed
        - jnp.mean(d_normed, -1, keepdims=True)
        - normed * jnp.mean(d_normed * normed, -1, keepdims=True)
    )


def dot(left, right, left_dim=1, right_dim=0):
    return lax.dot_general(
        left, right, (((left_dim,), (right_dim,)), ((), ())), preferred_element_type=F32
    )


def params(mib):
    return pltpu.CompilerParams(vmem_limit_bytes=mib * MIB)


def in_hbm(value):
    return pltpu.with_memory_space_constraint(value, pltpu.HBM)


def in_vmem(value):
    return pltpu.with_memory_space_constraint(value, pltpu.VMEM)


def cost(flops, bytes_accessed, transcendentals=0):
    return pl.CostEstimate(
        flops=int(flops), bytes_accessed=int(bytes_accessed), transcendentals=int(transcendentals)
    )


def whole(shape):
    return pl.BlockSpec(shape, lambda *unused: (0,) * len(shape))


def hits(slots, places):
    first, second = slots
    return jnp.where((places == first) | (places == second), 1.0, 0.0).astype(BF16)


def put_rows(slots_ref, rows_ref, out_ref):
    step = out_ref.shape[0]
    places = lax.broadcasted_iota(jnp.int32, (step, rows_ref.shape[0]), 0) + pl.program_id(0) * step
    out_ref[...] = dot(hits((slots_ref[0:1, :], slots_ref[1:2, :]), places), rows_ref[...]).astype(
        BF16
    )


def dispatch_rows(slot_rows, rows, total, steps=8):
    tokens, width = rows.shape
    step = total // steps
    return pl.pallas_call(
        put_rows,
        grid=(steps,),
        in_specs=[whole(slot_rows.shape), whole(rows.shape)],
        out_specs=pl.BlockSpec((step, width), lambda i: (i, 0)),
        out_shape=jax.ShapeDtypeStruct((total, width), BF16),
        compiler_params=params(20),
        cost_estimate=cost(2 * total * tokens * width, 4 * total * width),
        name="dispatch_rows",
    )(slot_rows, rows)


def attend_kernel(flag_ref, own_ref, far_ref, gain_ref, wt_ref, *refs):
    del flag_ref
    own_out, far_out, proj_ref, total_ref, mixed = refs[-5:]
    rows, width = own_ref.shape[1], own_ref.shape[2]
    head_dim = width // HEADS
    scale = head_dim ** (-0.5)
    x_float = jnp.concatenate([own_ref[0], far_ref[0]], 0).astype(F32)
    normed, unused = normalize(x_float)
    normed = (normed * gain_ref[...]).astype(BF16)
    proj_ref[0] = dot(wt_ref[...], normed, 1, 1).astype(BF16)

    def head(h, carry):
        at = pl.multiple_of(h * head_dim, head_dim)
        query = proj_ref[0, pl.ds(at, head_dim), :]
        key = proj_ref[0, pl.ds(at + width, head_dim), :]
        value = proj_ref[0, pl.ds(at + 2 * width, head_dim), :]
        scores = dot(key, query * scale, 0, 0)
        top = jnp.max(scores, 0, keepdims=True)
        exponent = jnp.exp(scores - top)
        total = jnp.sum(exponent, 0, keepdims=True)
        out = dot(value, exponent.astype(BF16)) * (1.0 / total)
        mixed[pl.ds(at, head_dim), :] = out
        total_ref[0, pl.ds(h, 1), :] = top + jnp.log(total)
        return carry

    lax.fori_loop(0, HEADS, head, 0, unroll=4)
    heads_out = mixed[...].T.astype(BF16)
    own_out[0] = heads_out[:rows]
    far_out[0] = heads_out[rows:]


def attend(flag, inputs, image, far, gain, w_qkv_t, kept):
    unused, rows, width = far.shape
    seq_len = 2 * rows
    part = inputs.shape[0] // 2
    block = lambda k, *shape: pl.BlockSpec((1,) + shape, lambda i, flag_ref: (k,) + (0,) * len(shape))
    return pl.pallas_call(
        attend_kernel,
        grid_spec=pltpu.PrefetchScalarGridSpec(
            num_scalar_prefetch=1,
            grid=(1,),
            in_specs=[
                pl.BlockSpec(
                    (1, rows, width), lambda i, flag_ref: (image + flag_ref[0] * part, 0, 0)
                ),
                block(0, rows, width),
                whole(gain.shape),
                whole(w_qkv_t.shape),
            ]
            + [pl.BlockSpec(memory_space=pl.ANY)] * len(kept),
            out_specs=[
                block(0, rows, width),
                block(0, rows, width),
                block(image, 3 * width, seq_len),
                block(image, HEADS, seq_len),
            ],
            scratch_shapes=[pltpu.VMEM((width, seq_len), F32)],
        ),
        out_shape=[
            jax.ShapeDtypeStruct((1, rows, width), BF16),
            jax.ShapeDtypeStruct((1, rows, width), BF16),
            pltpu.HBM((part, 3 * width, seq_len), BF16),
            pltpu.HBM((part, HEADS, seq_len), F32),
        ],
        input_output_aliases={5 + i: 2 + i for i in range(len(kept))},
        compiler_params=params(28),
        cost_estimate=cost(8e9, 8 * MIB, HEADS * seq_len**2),
        name="attend",
    )(flag, in_hbm(inputs), far, gain, w_qkv_t, *kept)


def small_columns(small, gain):
    rest = jnp.zeros((SMALL - small.shape[0] - 1, small.shape[1]), F32)
    return jnp.concatenate([small, gain, rest], 0).T


def attend_back_kernel(
    part,
    flag_ref,
    own_ref,
    *refs,
):
    far_refs, refs = refs[:part], refs[part:]
    attend_back_body(flag_ref, own_ref, far_refs, *refs)


def attend_back_body(
    flag_ref,
    own_ref,
    far_refs,
    gain_ref,
    wt_ref,
    proj_ref,
    total_ref,
    d_own_ref,
    d_far_ref,
    attn_ref,
    small_ref,
    own_out,
    far_out,
    keep_out,
    send_out,
    d_proj,
    d_mixed,
    weight_sum,
    gain_out,
    small_sum,
):
    image, last = pl.program_id(0), pl.num_programs(0) - 1
    rows, width = own_ref.shape[1], own_ref.shape[2]
    head_dim = width // HEADS
    scale = head_dim ** (-0.5)
    d_mixed[...] = jnp.concatenate([d_own_ref[0], d_far_ref[0]], 0).astype(F32).T.astype(BF16)

    def head(h, carry):
        at = pl.multiple_of(h * head_dim, head_dim)
        query = proj_ref[0, pl.ds(at, head_dim), :]
        key = proj_ref[0, pl.ds(at + width, head_dim), :]
        value = proj_ref[0, pl.ds(at + 2 * width, head_dim), :]
        d_out = d_mixed[pl.ds(at, head_dim), :]
        weights = jnp.exp(dot(key, query * scale, 0, 0) - total_ref[0, pl.ds(h, 1), :])
        product = weights * dot(value, d_out, 0, 0)
        spread = jnp.sum(product, 0, keepdims=True)
        d_scores = (product - weights * spread).astype(BF16)
        d_proj[pl.ds(at, head_dim), :] = (dot(key, d_scores) * scale).astype(BF16)
        d_proj[pl.ds(at + width, head_dim), :] = (dot(query, d_scores, 1, 1) * scale).astype(BF16)
        d_proj[pl.ds(at + 2 * width, head_dim), :] = dot(d_out, weights.astype(BF16), 1, 1).astype(
            BF16
        )
        return carry

    lax.fori_loop(0, HEADS, head, 0, unroll=1)
    far = far_refs[0][0]
    for k, far_ref in enumerate(far_refs[1:]):
        far = jnp.where(image == k + 1, far_ref[0], far)
    x_float = jnp.concatenate([own_ref[0], far], 0).astype(F32)
    normed, inverse = normalize(x_float)
    d_input = dot(d_proj[...], wt_ref[...], 0, 0)
    weight_term = dot((normed * gain_ref[...]).T.astype(BF16), d_proj[...], 1, 1)
    gain_term = jnp.sum(d_input * normed, 0, keepdims=True)
    d_x = norm_back(d_input * gain_ref[...], normed, inverse).astype(BF16)
    own_out[0] = d_x[:rows]
    far_out[0] = d_x[rows:]

    @pl.when(image == 0)
    def start():
        weight_sum[...] = weight_term
        gain_out[...] = gain_term

    @pl.when(image != 0)
    def add():
        weight_sum[...] += weight_term
        gain_out[...] += gain_term

    @pl.when(image == last)
    def finish():
        half = width // 2
        small_sum[...] = small_columns(small_ref[...], gain_out[...])
        near = pl.ds(pl.multiple_of(flag_ref[1] * half, half), half)
        away = pl.ds(pl.multiple_of((1 - flag_ref[1]) * half, half), half)
        for ref, at in ((weight_sum, 0), (attn_ref, 3 * width), (small_sum, 4 * width)):
            at = slice(at, at + ref.shape[1])
            keep_out[:, at] = ref[near, :]
            send_out[:, at] = ref[away, :].astype(BF16)


def attend_back(flag, inputs, far, gain, w_qkv_t, proj, total, d_heads, d_far, attn_term, small):
    part = len(far)
    unused, rows, width = far[0].shape
    seq_len = 2 * rows
    block = lambda *shape: pl.BlockSpec((1,) + shape, lambda i, flag_ref: (i,) + (0,) * len(shape))
    return pl.pallas_call(
        functools.partial(attend_back_kernel, part),
        grid_spec=pltpu.PrefetchScalarGridSpec(
            num_scalar_prefetch=1,
            grid=(part,),
            in_specs=[
                pl.BlockSpec((1, rows, width), lambda i, flag_ref: (i + flag_ref[0] * part, 0, 0)),
            ]
            + [whole((1, rows, width))] * part
            + [
                whole(gain.shape),
                whole(w_qkv_t.shape),
                block(3 * width, seq_len),
                block(HEADS, seq_len),
                block(rows, width),
                block(rows, width),
                whole(attn_term.shape),
                whole(small.shape),
            ],
            out_specs=[
                block(rows, width),
                block(rows, width),
                whole((width // 2, 4 * width + SMALL)),
                whole((width // 2, 4 * width + SMALL)),
            ],
            scratch_shapes=[
                pltpu.VMEM((3 * width, seq_len), BF16),
                pltpu.VMEM((width, seq_len), BF16),
                pltpu.VMEM((width, 3 * width), F32),
                pltpu.VMEM((1, width), F32),
                pltpu.VMEM((width, SMALL), F32),
            ],
        ),
        out_shape=[
            pltpu.HBM((part, rows, width), BF16),
            pltpu.HBM((part, rows, width), BF16),
            pltpu.HBM((width // 2, 4 * width + SMALL), F32),
            jax.ShapeDtypeStruct((width // 2, 4 * width + SMALL), BF16),
        ],
        compiler_params=params(36),
        cost_estimate=cost(part * 16e9, 12 * MIB, part * HEADS * seq_len**2),
        name="attend_back",
    )(
        flag,
        in_hbm(inputs),
        *map(in_hbm, far),
        gain,
        in_hbm(w_qkv_t),
        in_hbm(proj),
        total,
        in_hbm(d_heads),
        d_far,
        in_hbm(attn_term),
        small,
    )


def pick_image(flag_ref, image, images, own_refs, far_refs):
    part = images // 2
    mine = (flag_ref[0] == 0) == (image < part)
    value = jnp.where(mine, own_refs[0][0], far_refs[0][0])
    for k in range(1, part):
        other = jnp.where(mine, own_refs[k][0], far_refs[k][0])
        value = jnp.where(lax.rem(image, part) == k, other, value)
    return value


def residual_kernel(images, flag_ref, *refs):
    own_refs, far_refs, refs = refs[: images // 2], refs[images // 2 : images], refs[images:]
    x_ref, w_out_ref, gain_ref, heads_out, resid_out, normed_out, moments_out = refs
    image = pl.program_id(0)
    heads = pick_image(flag_ref, image, images, own_refs, far_refs)
    attn = dot(heads, w_out_ref[...])
    resid = x_ref[0].astype(F32) + attn
    normed, unused = normalize(resid)
    heads_out[...] = heads
    resid_out[...] = resid
    normed_out[...] = (normed * gain_ref[...]).astype(BF16)
    moments = [jnp.sum(value * value, 0, keepdims=True) for value in (resid, attn)]
    moments_out[...] = jnp.where(image == 0, 0.0, moments_out[...]) + jnp.concatenate(moments, 0)


def residual_rows(flag, own, far, inputs, w_attn_out, gain):
    images, rows, width = inputs.shape
    tokens = images * rows
    block = pl.BlockSpec((rows, width), lambda i, flag_ref: (i, 0))
    return pl.pallas_call(
        functools.partial(residual_kernel, images),
        grid_spec=pltpu.PrefetchScalarGridSpec(
            num_scalar_prefetch=1,
            grid=(images,),
            in_specs=[whole((1, rows, width))] * images
            + [
                pl.BlockSpec((1, rows, width), lambda i, flag_ref: (i, 0, 0)),
                whole(w_attn_out.shape),
                whole(gain.shape),
            ],
            out_specs=[block, block, block, whole((2, width))],
        ),
        out_shape=[
            pltpu.HBM((tokens, width), BF16),
            pltpu.HBM((tokens, width), F32),
            jax.ShapeDtypeStruct((tokens, width), BF16),
            jax.ShapeDtypeStruct((2, width), F32),
        ],
        compiler_params=params(24),
        cost_estimate=cost(2 * width * tokens * width, 10 * MIB),
        name="residual_rows",
    )(flag, *own, *far, in_hbm(inputs), w_attn_out, gain)


def blocks_kernel(first, slots_ref, rows_ref, *out_refs):
    for k, out_ref in enumerate(out_refs):
        shape = (out_ref.shape[0], rows_ref.shape[0])
        places = lax.broadcasted_iota(jnp.int32, shape, 0) + (first + k) * out_ref.shape[0]
        hit = hits((slots_ref[0:1, :], slots_ref[1:2, :]), places)
        out_ref[...] = dot(hit, rows_ref[...]).astype(BF16)


def dispatch_blocks(slot_rows, rows, first, count, slots):
    tokens, width = rows.shape
    return pl.pallas_call(
        functools.partial(blocks_kernel, first),
        out_shape=[pltpu.HBM((slots, width), BF16)] * count,
        compiler_params=params(16),
        cost_estimate=cost(2 * count * slots * tokens * width, 4 * count * slots * width),
        name="dispatch_blocks",
    )(slot_rows, rows)


def expert_kernel(capacity, count, kept, me_ref, *refs):
    blocks, refs = refs[:count], refs[count:]
    up_ref, router_ref, w_in_ref, b_in_ref, w_out_ref, b_out_ref, *refs = refs
    y_out, rows_out, act_out, d_hidden_out, d_y_out, b_in_sum, b_out_sum, *refs = refs[kept:]
    backs, pair = refs[:count], refs[count]
    slots, width = blocks[0].shape
    step = 2 * slots
    hidden_width = w_in_ref.shape[1]
    chunk = 512
    index = pl.program_id(0)
    odd = me_ref[0] % 2 == 1
    for i in range(count // 2):

        @pl.when(index == i)
        def load():
            both = [blocks[2 * i][...].astype(F32), blocks[2 * i + 1][...].astype(F32)]
            pair[...] = jnp.concatenate(both, 0).astype(BF16)

    rows = pair[...]
    rows_out[...] = rows
    logits = dot(rows, router_ref[...], 1, 1)
    gate = jnp.exp(logits - jnp.max(logits, -1, keepdims=True))
    mine = lax.broadcasted_iota(jnp.int32, gate.shape, 1) == me_ref[0]
    total = jnp.sum(gate, -1, keepdims=True)
    gate = jnp.sum(jnp.where(mine, gate, 0.0), -1, keepdims=True) / total
    low, high = up_ref[0].astype(F32), up_ref[1].astype(F32)
    up_float = jnp.concatenate([jnp.where(odd, high, low), jnp.where(odd, low, high)], 0)
    d_y = (gate * up_float).astype(BF16)
    d_y_out[...] = d_y
    y = jnp.zeros((step, width), F32)
    back = jnp.zeros((step, width), F32)

    def accumulate(ref, at, value):
        ref[:, at] = jnp.where(index == 0, 0.0, ref[:, at]) + jnp.sum(
            value.astype(F32), 0, keepdims=True
        )

    for c in range(hidden_width // chunk):
        at = slice(c * chunk, (c + 1) * chunk)
        hidden = dot(rows, w_in_ref[:, at]) + b_in_ref[:, at].astype(F32)
        square = hidden * hidden
        root = math.sqrt(2.0 / math.pi)
        slope = jnp.tanh(hidden * (root + (root * 0.044715) * square))
        half = 0.5 * (1.0 + slope)
        act = (hidden * half).astype(BF16)
        d_gelu = half + (0.5 * hidden) * (1.0 - slope * slope) * (
            root + (3.0 * root * 0.044715) * square
        )
        d_hidden = (dot(d_y, w_out_ref[at, :], 1, 1) * d_gelu).astype(BF16)
        act_out[:, at] = act
        d_hidden_out[:, at] = d_hidden
        y += dot(act, w_out_ref[at, :])
        back += dot(d_hidden, w_in_ref[:, at], 1, 1)
        accumulate(b_in_sum, at, d_hidden)
    accumulate(b_out_sum, slice(0, width), d_y)
    y = (y + b_out_ref[...].astype(F32)).astype(BF16).astype(F32)
    d_weight = jnp.sum(y * up_float, -1, keepdims=True)
    y = y * gate
    y_out[0] = jnp.where(odd, y[slots:], y[:slots]).astype(BF16)
    y_out[1] = jnp.where(odd, y[:slots], y[slots:]).astype(BF16)
    row = lax.broadcasted_iota(jnp.int32, (step, width), 0)
    lane = lax.broadcasted_iota(jnp.int32, (step, width), 1)
    for s in range(2):
        line = jnp.sum(jnp.where(row - s * slots == lane, d_weight, 0.0), 0, keepdims=True)
        line = jnp.where(lane[:1] < capacity, line, 0.0)
        top = line.astype(BF16).astype(F32)
        back = jnp.where(row == s * slots + capacity, top, back)
        back = jnp.where(row == s * slots + capacity + 1, line - top, back)
    for i in range(count // 2):

        @pl.when(index == i)
        def store():
            backs[2 * i][...] = back[:slots].astype(BF16)
            backs[2 * i + 1][...] = back[slots:].astype(BF16)


def expert_group(me, blocks, first, up, w_router, w_in, b_in, w_out, b_out, capacity, kept):
    count = len(blocks)
    slots, width = blocks[0].shape
    sources = up.shape[0]
    total = sources * slots
    hidden_width = w_in.shape[1]
    step = 2 * slots
    begin = first // 2
    rows = lambda size: pl.BlockSpec((step, size), lambda i, me_ref: (i + begin, 0))
    sides = pl.BlockSpec((2, slots, width), lambda i, me_ref: ((me_ref[0] // 2) ^ (i + begin), 0, 0))
    anywhere = pl.BlockSpec(memory_space=pl.ANY)
    given = 1 + count + 6
    shapes = [
        pltpu.HBM((sources, slots, width), BF16),
        pltpu.HBM((total, width), BF16),
        pltpu.HBM((total, hidden_width), BF16),
        pltpu.HBM((total, hidden_width), BF16),
        pltpu.HBM((total, width), BF16),
    ]
    outs = pl.pallas_call(
        functools.partial(expert_kernel, capacity, count, len(kept)),
        grid_spec=pltpu.PrefetchScalarGridSpec(
            num_scalar_prefetch=1,
            grid=(count // 2,),
            in_specs=[whole((slots, width))] * count
            + [sides]
            + [whole(a.shape) for a in (w_router, w_in, b_in, w_out, b_out)]
            + [anywhere] * len(kept),
            out_specs=[sides, rows(width), rows(hidden_width), rows(hidden_width), rows(width)]
            + [whole((1, hidden_width)), whole((1, width))]
            + [whole((slots, width))] * count,
            scratch_shapes=[pltpu.VMEM((step, width), BF16)],
        ),
        out_shape=shapes
        + [jax.ShapeDtypeStruct((1, hidden_width), F32), jax.ShapeDtypeStruct((1, width), F32)]
        + [jax.ShapeDtypeStruct((slots, width), BF16)] * count,
        input_output_aliases={given + i: i for i in range(len(kept))},
        compiler_params=params(28),
        cost_estimate=cost(8 * count * slots * width * hidden_width, 8 * MIB),
        name="expert_group",
    )(me, *map(in_hbm, blocks), in_hbm(up), w_router, w_in, b_in, w_out, b_out, *kept)
    return outs[:5], outs[5:7], list(outs[7:])


def weight_kernel(left_ref, right_ref, out_ref, turned_ref):
    @pl.when(pl.program_id(0) == 0)
    def turn():
        turned_ref[...] = left_ref[...].T

    out_ref[...] = dot(turned_ref[...], right_ref[...]).astype(BF16)


def turned_weight_kernel(turned_ref, right_ref, out_ref):
    out_ref[...] = dot(turned_ref[...], right_ref[...]).astype(BF16)


def weight_grad(left, right, begin, end, turned=False, pinned=False, block=512):
    total = right.shape[0]
    width = left.shape[0] if turned else left.shape[1]
    blocks = end - begin
    out = pl.BlockSpec((width, block), lambda i: (0, i))
    kind = pltpu.HBM if pinned else jax.ShapeDtypeStruct
    shapes = [kind((width, blocks * block), BF16), pltpu.HBM((width, total), BF16)]
    outs = pl.pallas_call(
        turned_weight_kernel if turned else weight_kernel,
        grid=(blocks,),
        in_specs=[
            whole(left.shape),
            pl.BlockSpec((total, block), lambda i: (0, i + begin)),
        ],
        out_specs=[out] if turned else [out, whole((width, total))],
        out_shape=shapes[:1] if turned else shapes,
        compiler_params=params(24),
        cost_estimate=cost(2 * total * width * blocks * block, 7 * MIB),
        name="weight_grad",
    )(in_hbm(left), in_hbm(right))
    return outs[0] if turned else outs


def sides_kernel(turned, lows, low_ref, low_far_ref, high_ref, high_far_ref, out_ref):
    low = pl.program_id(0) < lows
    own = jnp.where(low, low_ref[...], high_ref[...]).astype(F32)
    far = jnp.where(low, low_far_ref[...], high_far_ref[...]).astype(F32)
    out_ref[...] = (own + far).T if turned else own + far


def sides_sum(low, low_far, high, high_far, turned, block=512):
    width, columns = low.shape[0], low.shape[1] + high.shape[1]
    blocks = low.shape[1] // block
    lows = pl.BlockSpec((width, block), lambda i: (0, jnp.minimum(i, blocks - 1)))
    highs = pl.BlockSpec((width, block), lambda i: (0, jnp.maximum(i - blocks, 0)))
    if turned:
        shape, out = (columns, width), pl.BlockSpec((block, width), lambda i: (i, 0))
    else:
        shape, out = (width, columns), pl.BlockSpec((width, block), lambda i: (0, i))
    return pl.pallas_call(
        functools.partial(sides_kernel, turned, blocks),
        grid=(columns // block,),
        in_specs=[lows, lows, highs, highs],
        out_specs=out,
        out_shape=jax.ShapeDtypeStruct(shape, F32),
        compiler_params=params(20),
        cost_estimate=cost(width * columns, 8 * width * columns),
        name="sides_sum",
    )(in_hbm(low), low_far, in_hbm(high), high_far)


def combine_kernel(slots_ref, y_ref, resid_ref, out_ref, moment_ref):
    step, total = out_ref.shape[0], y_ref.shape[0]
    places = lax.broadcasted_iota(jnp.int32, (step, total), 1)
    moe = dot(hits((slots_ref[:, 0:1], slots_ref[:, 1:2]), places), y_ref[...])
    out_ref[...] = (resid_ref[...] + moe).astype(BF16)
    moment = jnp.sum(moe * moe, 0, keepdims=True)
    moment_ref[...] = jnp.where(pl.program_id(0) == 0, 0.0, moment_ref[...]) + moment


def combine_rows(slot_columns, y, resid, step):
    tokens, width = resid.shape
    total = y.shape[0]
    block = lambda size: pl.BlockSpec((step, size), lambda i: (i, 0))
    return pl.pallas_call(
        combine_kernel,
        grid=(tokens // step,),
        in_specs=[block(TOP), whole(y.shape), block(width)],
        out_specs=[block(width), whole((1, width))],
        out_shape=[
            jax.ShapeDtypeStruct((tokens, width), BF16),
            jax.ShapeDtypeStruct((1, width), F32),
        ],
        compiler_params=params(24),
        cost_estimate=cost(2 * total * tokens * width, 8 * MIB),
        name="combine_rows",
    )(slot_columns, y, in_hbm(resid))


def token_back_kernel(
    capacity,
    slots,
    experts,
    later,
    flag_ref,
    *refs,
):
    me = flag_ref[2]
    backs, refs = refs[:experts], refs[experts:]
    if later:
        unused, attn_ref, router_ref_sum, gain_ref_sum, *refs = refs
    (
        columns_ref,
        lines_ref,
        resid_ref,
        normed_ref,
        heads_ref,
        up_ref,
        w_out_ref,
        router_ref,
        gain_ref,
        d_resid_out,
        d_heads_out,
        attn_sum,
        gain_sum,
        router_out,
        d_weights,
        back_ref,
        near_router,
        router_sum,
    ) = refs
    step, width = resid_ref.shape
    total = back_ref.shape[0]
    first = pl.program_id(0) == 0

    @pl.when(first)
    def columns():
        near_router[...] = jnp.concatenate(
            [router_ref[pl.ds(e ^ me, 1), :] for e in range(experts)], 0
        ).astype(BF16)
        row = lax.broadcasted_iota(jnp.int32, (slots, 256), 0)
        lane = lax.broadcasted_iota(jnp.int32, (slots, 256), 1)
        for e in range(0, experts, 2):
            pair = [backs[e][...].astype(F32), backs[e + 1][...].astype(F32)]
            back_ref[e * slots : (e + 2) * slots, :] = jnp.concatenate(pair, 0).astype(BF16)
        for e in range(experts):
            block = backs[e][:, 0:256].astype(F32)
            line = jnp.sum(jnp.where(row >= capacity, block, 0.0), 0, keepdims=True)
            column = jnp.sum(jnp.where(row == lane, line, 0.0), -1, keepdims=True)
            d_weights[e * slots : (e + 1) * slots, :] = jnp.broadcast_to(column, (slots, step))

    def accumulate(ref, value, given_ref=None):
        given = 0.0 if given_ref is None else given_ref[...]
        ref[...] = jnp.where(first, given, ref[...]) + value

    line_slots = (lines_ref[0:1, :], lines_ref[1:2, :])
    d_gates = []
    for e in range(experts):
        places = lax.broadcasted_iota(jnp.int32, (slots, step), 0) + e * slots
        hit = (places == line_slots[0]) | (places == line_slots[1])
        d_gates.append(
            jnp.sum(
                jnp.where(hit, d_weights[e * slots : (e + 1) * slots, :], 0.0), 0, keepdims=True
            )
        )
    d_gates = jnp.concatenate(d_gates, 0)
    logits = dot(near_router[...], normed_ref[...], 1, 1)
    gates = jnp.exp(logits - jnp.max(logits, 0, keepdims=True))
    gates = gates / jnp.sum(gates, 0, keepdims=True)
    d_logits = (gates * (d_gates - jnp.sum(gates * d_gates, 0, keepdims=True))).astype(BF16)
    places = lax.broadcasted_iota(jnp.int32, (step, total), 1)
    d_normed = dot(hits((columns_ref[:, 0:1], columns_ref[:, 1:2]), places), back_ref[...])
    d_normed += dot(d_logits, near_router[...], 0, 0)
    normed, inverse = normalize(resid_ref[...])
    d_resid = up_ref[...].astype(F32) + norm_back(d_normed * gain_ref[...], normed, inverse)
    d_attn = d_resid.astype(BF16)
    d_resid_out[...] = d_resid
    d_heads_out[...] = dot(d_attn, w_out_ref[...], 1, 1).astype(BF16)
    accumulate(attn_sum, dot(heads_ref[...], d_attn, 0, 0), attn_ref if later else None)
    accumulate(router_sum, dot(d_logits, normed_ref[...]))
    gain_term = jnp.sum(d_normed * normed, 0, keepdims=True)
    accumulate(gain_sum, gain_term, gain_ref_sum if later else None)

    @pl.when(pl.program_id(0) == pl.num_programs(0) - 1)
    def finish():
        for e in range(experts):
            at = pl.ds(e ^ me, 1)
            given = router_ref_sum[at, :] if later else 0.0
            router_out[at, :] = router_sum[e : e + 1, :] + given


def token_back(
    flag,
    mine,
    kept,
    slot_columns,
    slot_rows,
    backs,
    resid,
    normed,
    heads,
    up,
    w_attn_out,
    w_router_t,
    gain,
    capacity,
    slots,
    step,
):
    tokens, width = resid.shape
    experts = w_router_t.shape[0]
    total = experts * slots
    part = tokens // step // 2
    image = lambda i, flag_ref: i + (flag_ref[0] if mine else 1 - flag_ref[0]) * part
    block = lambda size: pl.BlockSpec((step, size), lambda i, flag_ref: (image(i, flag_ref), 0))
    sums = [(width, width), (1, width), (experts, width)]
    given = [kept[0], kept[2], kept[4], kept[3]] if kept else []
    return pl.pallas_call(
        functools.partial(token_back_kernel, capacity, slots, experts, bool(kept)),
        grid_spec=pltpu.PrefetchScalarGridSpec(
            num_scalar_prefetch=1,
            grid=(part,),
            in_specs=[whole((slots, width))] * experts
            + [pl.BlockSpec(memory_space=pl.ANY)] * (len(given) > 0)
            + [whole(value.shape) for value in given[1:]]
            + [
                block(TOP),
                pl.BlockSpec((TOP, step), lambda i, flag_ref: (0, image(i, flag_ref))),
                block(width),
                block(width),
                block(width),
                block(width),
                whole(w_attn_out.shape),
                whole(w_router_t.shape),
                whole(gain.shape),
            ],
            out_specs=[block(width), pl.BlockSpec((step, width), lambda i, flag_ref: (i, 0))]
            + [whole(shape) for shape in sums],
            scratch_shapes=[
                pltpu.VMEM((total, step), F32),
                pltpu.VMEM((total, width), BF16),
                pltpu.VMEM((experts, width), BF16),
                pltpu.VMEM((experts, width), F32),
            ],
        ),
        out_shape=[
            pltpu.HBM((tokens, width), F32),
            pltpu.HBM((part * step, width), BF16),
            pltpu.HBM((width, width), F32),
            jax.ShapeDtypeStruct((1, width), F32),
            jax.ShapeDtypeStruct((experts, width), F32),
        ],
        input_output_aliases={1 + experts: 0} if kept else {},
        compiler_params=params(30),
        cost_estimate=cost((total + 2 * width) * tokens * width, 7 * MIB),
        name="token_back",
    )(
        flag,
        *map(in_hbm, backs),
        *map(in_hbm, given),
        slot_columns,
        slot_rows,
        in_hbm(resid),
        in_hbm(normed),
        in_hbm(heads),
        in_hbm(up),
        w_attn_out,
        w_router_t,
        gain,
    )


def grad_sum_kernel(flag_ref, resid_ref, own_ref, far_ref, out_ref):
    mine = (flag_ref[0] == 0) == (pl.program_id(0) < pl.num_programs(0) // 2)
    out_ref[...] = resid_ref[...] + jnp.where(mine, own_ref[0], far_ref[0]).astype(F32)


def grad_sum(flag, d_resid, own, far):
    part, rows, width = own.shape
    tokens = d_resid.shape[0]
    pick = pl.BlockSpec((1, rows, width), lambda i, flag_ref: (lax.rem(i, part), 0, 0))
    return pl.pallas_call(
        grad_sum_kernel,
        grid_spec=pltpu.PrefetchScalarGridSpec(
            num_scalar_prefetch=1,
            grid=(tokens // rows,),
            in_specs=[pl.BlockSpec((rows, width), lambda i, flag_ref: (i, 0)), pick, pick],
            out_specs=pl.BlockSpec((rows, width), lambda i, flag_ref: (i, 0)),
        ),
        out_shape=jax.ShapeDtypeStruct((tokens, width), F32),
        compiler_params=params(16),
        cost_estimate=cost(tokens * width, 6 * MIB),
        name="grad_sum",
    )(flag, in_hbm(d_resid), own, far)


AXES = ("wide", "narrow")


def device_bits():
    n_narrow = lax.axis_size("narrow")
    masks = [1 << b for b in range((n_narrow * lax.axis_size("wide")).bit_length() - 1)]
    masks.remove(n_narrow)
    return [n_narrow] + masks


def sum_steps():
    first, *rest = device_bits()
    return [(first,)] + [tuple(rest[i : i + 2]) for i in range(0, len(rest), 2)]


def swap(value, mask, axes=AXES):
    size = math.prod(lax.axis_size(axis) for axis in axes)
    return lax.ppermute(value, axes, [(i, i ^ mask) for i in range(size)])


def partners(bits):
    me = lax.axis_index(AXES)
    place = sum(((me // bit) % 2) << b for b, bit in enumerate(bits))
    masks = [
        sum(bit for b, bit in enumerate(bits) if (j >> b) & 1) for j in range(1 << len(bits))
    ]
    return masks, place


def fold_kernel(given, members, place_ref, keep_ref, *refs):
    del place_ref
    step = pl.program_id(0)
    total = keep_ref[...]
    for far_ref in refs[:given]:
        total += far_ref[...].astype(F32)
    own_out, *send_outs = refs[given:]

    @pl.when(step == 0)
    def keep():
        own_out[...] = total

    for j, send_out in enumerate(send_outs):

        @pl.when(step == j + 1)
        def send():
            send_out[...] = total.astype(BF16)


def fold(keep, far, bits):
    masks, place = partners(bits)
    members = len(masks)
    rows, size = keep.shape
    part = rows // members
    pick = pl.BlockSpec((part, size), lambda j, place_ref: (place_ref[0] ^ j, 0))
    own, *send = pl.pallas_call(
        functools.partial(fold_kernel, len(far), members),
        grid_spec=pltpu.PrefetchScalarGridSpec(
            num_scalar_prefetch=1,
            grid=(members,),
            in_specs=[pick] * (1 + len(far)),
            out_specs=[whole((part, size))] * members,
        ),
        out_shape=[jax.ShapeDtypeStruct((part, size), F32)]
        + [jax.ShapeDtypeStruct((part, size), BF16)] * (members - 1),
        compiler_params=params(32),
        cost_estimate=cost(0, 8 * rows * size),
        name="fold",
    )(place.reshape(1).astype(jnp.int32), in_hbm(keep), *far)
    return own, [swap(value, mask) for value, mask in zip(send, masks[1:])]


def sum_parts(value, bits):
    masks, place = partners(bits)
    part = value.shape[0] // len(masks)
    pick = lambda j: lax.dynamic_slice_in_dim(value, (place ^ j) * part, part, 0)
    far = [swap(pick(j).astype(BF16), masks[j]) for j in range(1, len(masks))]
    total = pick(0)
    for term in far:
        total = total + term.astype(F32)
    return total


def spread_parts(value, bits):
    masks, place = partners(bits)
    parts = [value] + [swap(value, mask) for mask in masks[1:]]
    for b in range(len(bits)):
        side = (place >> b) % 2 == 0
        parts = [
            jnp.where(
                side,
                jnp.concatenate([parts[i], parts[i + 1]], 0),
                jnp.concatenate([parts[i + 1], parts[i]], 0),
            )
            for i in range(0, len(parts), 2)
        ]
    return parts[0]


def close_kernel(keep_ref, moment_ref, *refs):
    total = keep_ref[...]
    for far_ref in refs[:-1]:
        total += far_ref[...].astype(F32)
    row = lax.broadcasted_iota(jnp.int32, total.shape, 0)
    lane = lax.broadcasted_iota(jnp.int32, total.shape, 1) - (total.shape[1] - 2)
    moment = jnp.sum(moment_ref[...], 1, keepdims=True)
    high = moment.astype(BF16).astype(F32)
    extra = jnp.where(lane == 0, high, moment - high)
    refs[-1][...] = jnp.where((row == 0) & (lane >= 0), extra, total).astype(BF16)


def close(keep, far, moment):
    return pl.pallas_call(
        close_kernel,
        out_shape=jax.ShapeDtypeStruct(keep.shape, BF16),
        compiler_params=params(16),
        cost_estimate=cost(0, 8 * keep.size),
        name="close",
    )(keep, moment, *far)


def add_kernel(*refs):
    terms = [ref[...].astype(F32) for ref in refs[:-1]]
    while len(terms) > 1:
        terms = [terms[i] + terms[i + 1] for i in range(0, len(terms), 2)]
    refs[-1][...] = terms[0].astype(BF16)


def add(terms):
    return pl.pallas_call(
        add_kernel,
        out_shape=jax.ShapeDtypeStruct(terms[0].shape, BF16),
        compiler_params=params(16),
        cost_estimate=cost(0, 2 * len(terms) * terms[0].size),
        name="add",
    )(*terms)


def apart_kernel(experts, count, flag_ref, own_ref, far_ref, qkv_out, attn_out, router_out, *outs):
    gain_one_out, gain_two_out, stats_out, small = outs
    half, width = own_ref.shape[0], attn_out.shape[1]
    upper = flag_ref[1] == 1
    own, far = own_ref[...].astype(F32), far_ref[...].astype(F32)
    for rows, value in ((0, jnp.where(upper, far, own)), (half, jnp.where(upper, own, far))):
        rows = slice(rows, rows + half)
        qkv_out[rows, :] = value[:, : 3 * width]
        attn_out[rows, :] = value[:, 3 * width : 4 * width]
        small[rows, :] = value[:, 4 * width :]
    values = small[...]
    lines = values.T
    router_out[...] = lines[:experts]
    gain_two_out[...] = lines[experts : experts + 1, :]
    gain_one_out[...] = lines[experts + 3 : experts + 4, :]
    sums = jnp.sum(lines, 1, keepdims=True)
    moments = (
        sums[experts + 1 : experts + 2],
        sums[experts + 2 : experts + 3],
        sums[SMALL - 2 : SMALL - 1] + sums[SMALL - 1 :],
    )
    lane = lax.broadcasted_iota(jnp.int32, stats_out.shape, 1)
    stats = jnp.where(lane == 0, moments[0], jnp.where(lane == 1, moments[1], moments[2]))
    stats_out[...] = jnp.sqrt(stats / count + EPS)


def sums_apart(flag, own, far, experts, count):
    width = 2 * own.shape[0]
    shapes = [(width, 3 * width), (width, width), (experts, width), (1, width), (1, width), (1, 3)]
    return pl.pallas_call(
        functools.partial(apart_kernel, experts, count),
        grid_spec=pltpu.PrefetchScalarGridSpec(
            num_scalar_prefetch=1,
            grid=(1,),
            in_specs=[whole(own.shape), whole(far.shape)],
            out_specs=[whole(shape) for shape in shapes],
            scratch_shapes=[pltpu.VMEM((width, SMALL), F32)],
        ),
        out_shape=[jax.ShapeDtypeStruct(shape, F32) for shape in shapes],
        compiler_params=params(32),
        cost_estimate=cost(0, 8 * MIB),
        name="sums_apart",
    )(flag, own, far)


def gathered_attention(inputs, gain_one, w_qkv):
    images, rows_dev, width = inputs.shape
    tokens = images * rows_dev
    head_dim = width // HEADS
    scale = head_dim ** (-0.5)
    seq_len = rows_dev * lax.axis_size("narrow")
    group = math.gcd(images, max(1, 512 // rows_dev))
    blocks = images // group
    normed_one, inverse_one = normalize(inputs.astype(F32).reshape(tokens, width))
    input_one = (normed_one * gain_one).astype(BF16)
    projected = jnp.dot(input_one, w_qkv, preferred_element_type=F32).astype(BF16)
    queries = projected[:, :width].reshape(images, rows_dev, width)
    keys_own = projected[:, width : 2 * width].reshape(images, rows_dev, width)
    values_own = projected[:, 2 * width :].reshape(images, rows_dev, width)
    keys_all = lax.all_gather(keys_own, "narrow", axis=1, tiled=True)
    values_all = lax.all_gather(values_own, "narrow", axis=1, tiled=True)
    query_blocks = queries.reshape(blocks, group, rows_dev, HEADS, head_dim)
    key_blocks = keys_all.reshape(blocks, group, seq_len, HEADS, head_dim)
    value_blocks = values_all.reshape(blocks, group, seq_len, HEADS, head_dim)

    def attend_block(operands):
        query_b, key_b, value_b = operands
        scores = jnp.einsum("gqhd,gkhd->ghqk", query_b, key_b, preferred_element_type=F32) * scale
        top_score = jnp.max(scores, -1, keepdims=True)
        exponent = jnp.exp(scores - top_score)
        total = jnp.sum(exponent, -1, keepdims=True)
        weights = (exponent / total).astype(BF16)
        mixed = jnp.einsum("ghqk,gkhd->gqhd", weights, value_b, preferred_element_type=F32)
        return (mixed.astype(BF16), (top_score + jnp.log(total))[..., 0])

    heads_out, log_total = lax.map(attend_block, (query_blocks, key_blocks, value_blocks))

    def back_block(operands):
        query_b, key_b, value_b, total_b, d_head_b = operands
        scores = jnp.einsum("gqhd,gkhd->ghqk", query_b, key_b, preferred_element_type=F32) * scale
        weights = jnp.exp(scores - total_b[..., None])
        d_weights = jnp.einsum("gqhd,gkhd->ghqk", d_head_b, value_b, preferred_element_type=F32)
        spread = jnp.sum(weights * d_weights, -1, keepdims=True)
        d_scores = (weights * (d_weights - spread)).astype(BF16)
        d_query = jnp.einsum("ghqk,gkhd->gqhd", d_scores, key_b, preferred_element_type=F32) * scale
        d_key = jnp.einsum("ghqk,gqhd->gkhd", d_scores, query_b, preferred_element_type=F32) * scale
        d_value = jnp.einsum(
            "ghqk,gqhd->gkhd", weights.astype(BF16), d_head_b, preferred_element_type=F32
        )
        return (d_query.astype(BF16), d_key, d_value)

    def back(d_heads, d_resid):
        d_head_blocks = d_heads.reshape(blocks, group, rows_dev, HEADS, head_dim)
        d_queries, key_terms, value_terms = lax.map(
            back_block, (query_blocks, key_blocks, value_blocks, log_total, d_head_blocks)
        )
        d_keys, d_values = (
            lax.psum_scatter(
                terms.reshape(images, seq_len, width), "narrow", scatter_dimension=1, tiled=True
            )
            .astype(BF16)
            .reshape(tokens, width)
            for terms in (key_terms, value_terms)
        )
        d_projected = jnp.concatenate([d_queries.reshape(tokens, width), d_keys, d_values], 1)
        d_weight = jnp.dot(input_one.T, d_projected, preferred_element_type=F32)
        d_input = jnp.dot(d_projected, w_qkv.T, preferred_element_type=F32)
        d_gain = jnp.sum(d_input * normed_one, 0, keepdims=True)
        return (
            d_resid + norm_back(d_input * gain_one, normed_one, inverse_one),
            d_weight,
            d_gain,
        )

    return heads_out.reshape(images, rows_dev, width), back


def shards(
    inputs,
    cotangent,
    ln1_gain,
    w_qkv,
    w_attn_out,
    ln2_gain,
    w_router,
    expert_in,
    expert_in_bias,
    expert_out,
    expert_out_bias,
    route_ids,
    route_slots,
    route_dropped,
):
    images, rows_dev, width = inputs.shape
    tokens = images * rows_dev
    experts = w_router.shape[1]
    n_wide = lax.axis_size("wide")
    n_narrow = lax.axis_size("narrow")
    capacity = max(2, 42 * tokens // (20 * experts))
    slots = -(-(capacity + 2) // 8) * 8
    total = experts * slots
    gain_one = ln1_gain.astype(F32).reshape(1, width)
    gain_two = ln2_gain.astype(F32).reshape(1, width)
    paired = n_narrow == 2 and images % 2 == 0
    part = images // 2
    place = lax.axis_index("narrow") if paired else jnp.int32(0)
    me = lax.axis_index("wide")
    flag = jnp.stack([place, me % 2, me])

    slot_columns = jnp.where(
        route_dropped == 0, route_ids * slots + route_slots, -1
    ).reshape(tokens, TOP)
    slot_rows = slot_columns.T
    near_columns = jnp.where(
        route_dropped == 0, (route_ids ^ me) * slots + route_slots, -1
    ).reshape(tokens, TOP)
    near_rows = near_columns.T
    up = cotangent.reshape(tokens, width)

    def exchange(rows):
        return lax.all_to_all(
            rows.reshape(experts, slots, width), "wide", split_axis=0, concat_axis=0, tiled=True
        ).reshape(total, width)

    up_rows = dispatch_rows(slot_rows, up, total)
    if paired:
        pick = lambda k: lax.dynamic_slice_in_dim(inputs, (1 - place) * part + k, 1, 0)
        far_inputs = [swap(pick(0), 1)]
        far_inputs[0], up_rows = lax.optimization_barrier((far_inputs[0], up_rows))
        far_inputs += [swap(pick(k), 1) for k in range(1, part)]
    up_here = exchange(up_rows)

    if paired:
        w_qkv_t = w_qkv.T
        heads_own, heads_far, saved = [], [], []
        for k, far in enumerate(far_inputs):
            own_heads, far_heads, *saved = attend(
                flag, inputs, k, far, gain_one, w_qkv_t, saved
            )
            heads_own.append(own_heads)
            heads_far.append(swap(far_heads, 1))
        proj, log_total = saved
    else:
        heads_own, attention_back = gathered_attention(inputs, gain_one, w_qkv)
        heads_own = [heads_own[k : k + 1] for k in range(images)]
        heads_own, heads_far = heads_own[:part], heads_own[part:]

    heads, resid, normed_two, moments = residual_rows(
        flag, heads_own, heads_far, inputs, w_attn_out, gain_two
    )
    w_in, w_out = expert_in[0], expert_out[0]
    up_here = up_here.reshape(experts, slots, width)

    def expert(blocks, first, kept):
        return expert_group(
            me.reshape(1),
            blocks,
            first,
            up_here,
            w_router.T,
            w_in,
            expert_in_bias,
            w_out,
            expert_out_bias,
            capacity,
            kept,
        )

    def after(value, *others):
        return lax.optimization_barrier((value,) + others)[0]

    half = experts // 2
    quarter = half // 2
    send = lambda block, k: swap(block, k, ("wide",)) if k else block
    near_blocks = dispatch_blocks(near_rows, normed_two, 0, half, slots)
    blocks = dispatch_blocks(near_rows, after(normed_two, near_blocks[0]), half, half, slots)
    cross = [send(block, half + k) for k, block in enumerate(blocks[:2])]
    local = []
    for k, block in enumerate(near_blocks):
        local.append(send(after(block, local[k - 3]) if k > 3 else block, k))
    kept, sums_a, backs_a = expert(local, 0, [])
    for k in range(2, half):
        gate = local[k + half - EARLY] if k < EARLY else sums_a[1]
        cross.append(send(after(blocks[k], gate), half + k))
    backs_a = [send(block, k) for k, block in enumerate(backs_a)]
    kept, sums_b, backs_b = expert(cross[:quarter], half, kept)
    backs_b = [send(block, half + k) for k, block in enumerate(backs_b)]
    last = cross[quarter:]
    last[0] = after(last[0], *backs_a[1:6])
    kept, sums_c, backs_c = expert(last, half + quarter, kept)
    y, rows_here, act, d_hidden, d_y = kept
    y = y.reshape(total, width)
    last_block = w_in.shape[1] // 512
    low_out, d_y_t = weight_grad(after(d_y, *backs_b[:2]), act, 0, MIDDLE)
    grad_out = [low_out]
    backs_c = [
        send(after(block, grad_out[0]), half + quarter + k) for k, block in enumerate(backs_c)
    ]
    d_y_t = after(d_y_t, grad_out[0], *backs_b[2:], *backs_a[6:])
    grad_out.append(weight_grad(d_y_t, act, MIDDLE, last_block, True))
    rows_here = after(rows_here, grad_out[1], *backs_c[:2])
    low_in, rows_t = weight_grad(rows_here, d_hidden, 0, LATE, pinned=True)
    grad_in = [low_in]
    b_in_sum, b_out_sum = (sum(terms) for terms in zip(sums_a, sums_b, sums_c))
    backs = backs_a + backs_b + backs_c
    far_out = [swap(part_grad, 1) for part_grad in grad_out] if n_narrow == 2 else []
    backs[-1] = after(backs[-1], *grad_in)

    def back_to_tokens(mine, kept):
        return token_back(
            flag,
            mine,
            kept,
            near_columns,
            near_rows,
            backs,
            resid,
            normed_two,
            heads,
            up,
            w_attn_out,
            w_router.T.astype(F32),
            gain_two,
            capacity,
            slots,
            rows_dev,
        )

    first = back_to_tokens(False, [])
    sent = first[1]
    d_resid, d_heads, attn_term, gain_two_term, router_term = back_to_tokens(True, first)
    sent, grad_in[0] = lax.optimization_barrier((sent, grad_in[0]))
    biases = jnp.concatenate([b_in_sum, b_out_sum], 1)
    small = jnp.concatenate([router_term, gain_two_term, moments], 0)
    count = tokens * width * n_wide * n_narrow
    steps = sum_steps()
    if paired:
        d_far = swap(sent.reshape(part, rows_dev, width), 1)
        far_in = [swap(grad_in[0], 1)]
        far_biases = swap(biases, 1)
        y = exchange(after(y, sent))
        d_far, *far_out = lax.optimization_barrier((d_far, *far_out))
        d_own, d_far, keep, send = attend_back(
            flag,
            inputs,
            far_inputs,
            gain_one,
            w_qkv_t,
            proj,
            log_total,
            d_heads.reshape(part, rows_dev, width),
            d_far,
            attn_term,
            small,
        )
        sums, far = fold(keep, [swap(send, steps[0][0])], steps[1])
        block_out, moe_moment = combine_rows(slot_columns, after(y, sums), resid, rows_dev)
        grad_in.append(weight_grad(after(rows_t, sums), d_hidden, LATE, last_block, True))
        far_in.append(swap(grad_in[1], 1))
        far[0], moe_moment, far_biases, far_in[0], *unused = lax.optimization_barrier(
            (far[0], moe_moment, far_biases, far_in[0], grad_in[1])
        )
        biases = biases + far_biases
        bias_outs = (biases[:, : w_in.shape[1]], biases[:, w_in.shape[1] :])
        sums = close(sums, far, moe_moment)
        d_far = swap(after(d_far, sums), 1)
        for bits in steps[2:]:
            masks, unused = partners(bits)
            terms = [sums] + [swap(sums, mask) for mask in masks[1:]]
            grad_expert_out = sides_sum(
                grad_out[0], far_out[0], grad_out[1], after(far_out[1], sums), True
            )
            terms[1], grad_expert_out, *bias_outs = lax.optimization_barrier(
                (terms[1], grad_expert_out, *bias_outs)
            )
            sums = add(terms)
        sums, d_far, far_in[1] = lax.optimization_barrier((sums, d_far, far_in[1]))
        input_grad = grad_sum(flag, d_resid, d_own, d_far)
        grad_expert_in = sides_sum(grad_in[0], far_in[0], grad_in[1], far_in[1], False)
        sums = spread_parts(sums, steps[1])
        sums, input_grad, grad_expert_in = lax.optimization_barrier(
            (sums, input_grad, grad_expert_in)
        )
    else:
        y = exchange(y)
        grad_in.append(weight_grad(rows_t, d_hidden, LATE, last_block, True))
        grad_out, grad_in = lax.psum((grad_out, grad_in), "narrow")
        grad_expert_out = jnp.concatenate(grad_out, 1).astype(F32).T
        grad_expert_in = jnp.concatenate(grad_in, 1).astype(F32)
        biases = lax.psum(biases, "narrow")
        bias_outs = (biases[:, : w_in.shape[1]], biases[:, w_in.shape[1] :])
        d_heads = jnp.concatenate([d_heads, sent], 0)
        input_grad, qkv_term, gain_one_term = attention_back(d_heads, d_resid)
        small = small_columns(small, gain_one_term)
        sums = jnp.concatenate([qkv_term, attn_term, small], 1)
        for bits in steps:
            sums = sum_parts(sums, bits)
        block_out, moe_moment = combine_rows(slot_columns, y, resid, rows_dev)
        sums = close(sums, [], moe_moment)
        for bits in reversed(steps[1:]):
            sums = spread_parts(sums, bits)
    grad_qkv, grad_attn_out, grad_router, grad_gain_one, grad_gain_two, stats = sums_apart(
        flag, sums, swap(sums, steps[0][0]), experts, count
    )
    return (
        block_out.reshape(images, rows_dev, width),
        input_grad.reshape(images, rows_dev, width),
        grad_gain_one.reshape(width),
        grad_qkv,
        grad_attn_out,
        grad_gain_two.reshape(width),
        grad_router.T,
        grad_expert_in[None],
        bias_outs[0],
        grad_expert_out[None],
        bias_outs[1],
        stats.reshape(3),
    )


def solution(mesh):
    return jax.shard_map(
        shards,
        mesh=mesh,
        in_specs=(
            P("wide", "narrow", None),
            P("wide", "narrow", None),
            P(),
            P(),
            P(),
            P(),
            P(),
            P("wide", None, None),
            P("wide", None),
            P("wide", None, None),
            P("wide", None),
            P("wide", "narrow", None),
            P("wide", "narrow", None),
            P("wide", "narrow", None),
        ),
        out_specs=(
            P("wide", "narrow", None),
            P("wide", "narrow", None),
            P(),
            P(),
            P(),
            P(),
            P(),
            P("wide", None, None),
            P("wide", None),
            P("wide", None, None),
            P("wide", None),
            P(),
        ),
        check_vma=False,
    )
```
